128 devices in a mesh: lat: 8 (over z, x_hi), lon: 16 (over x_lo, y, core).
Axes of the slice: x: 4 (x_hi: 2, x_lo: 2; x = x_hi * 2 + x_lo), y: 4, z: 4, core: 2. Of those that a mesh axis runs over, the one named last changes fastest.
Arguments:
- obs_values: bfloat16 [128, 128, 8, 128], P(('lat', 'lon')), may hold values from -6 to 6
- obs_cells: int32 [128, 128, 8], P(('lat', 'lon')), may hold values from 0 to 767
- obs_counts: int32 [128, 128], P(('lat', 'lon')), may hold values from 1 to 8, as said below
- embed_weight: bfloat16 [128, 256], replicated, may hold values from -0.5 to 0.5
- density_row: float32 [256], replicated, may hold values from -6 to 6
- conv_weight: bfloat16 [2, 3, 3, 256, 256], replicated, may hold values from -0.125 to 0.125
- grid_cotangent: bfloat16 [128, 768, 256], P('lat', 'lon'), may hold values from -6 to 6
Outputs:
- grid_out: bfloat16 [128, 768, 256], P('lat', 'lon')
- grad_conv: float32 [2, 3, 3, 256, 256], replicated
- grad_embed: float32 [128, 256], replicated
- grad_obs: bfloat16 [128, 128, 8, 128], P(('lat', 'lon'))
The draws below stay inside these ranges and needn't reach their ends.
Inputs may be any that keep to these rules, and one draw needn't show every extreme that they name: `obs_counts`: in every draw one destination tile receives all 8 slots used from every sender; the loads of the other tiles differ from tile to tile.
All inputs are finite; a program needn't handle non-finite values.
Results may differ from the reference program's by a relative error of at most 0.0085.
Values may be sent and summed in bfloat16 or wider, within the bound.
A program may use at most 64 MiB of HBM per device.

```python
import jax
import jax.numpy as jnp
from jax import lax

C = 256
F = 128
LAYERS = 2
TLAT = 16
TLON = 48
CAP = 8
TILES = 128
NLAT = 128
NLON = 768
N_LAT = 8
N_LON = 16


def draw_obs_counts(key, part):
    key = jax.random.fold_in(key, 7)
    key_level = jax.random.fold_in(key, 1)
    key_drop = jax.random.fold_in(key, 2)
    key_full = jax.random.fold_in(key, 3)
    level = jax.random.randint(key_level, (TILES,), 1, CAP + 1)
    raw_drop = jax.random.randint(key_drop, (TILES, TILES), 0, CAP + 1)
    drop = raw_drop % (level // 2 + 1)[None, :]
    counts = level[None, :] - drop
    full_tile = jax.random.randint(key_full, (), 0, TILES)
    counts = jnp.where(jnp.arange(TILES)[None, :] == full_tile, CAP, counts)
    return counts.astype(jnp.int32)


def set_ends(values, own_key, low, top_value):
    index_at = [jax.random.randint(jax.random.fold_in(own_key, axis), (), 0, length) for axis, length in enumerate(values.shape)]
    longest = values.shape.index(max(values.shape))
    next_to = index_at[:longest] + [(index_at[longest] + 1) % values.shape[longest]] + index_at[longest + 1:]
    return values.at[tuple(index_at)].set(low).at[tuple(next_to)].set(top_value)


def levels(rng, dims, shards, smallest, high):
    gain = 1.0
    for position, shards_of in shards:
        draws = jax.random.uniform(jax.random.fold_in(jax.random.fold_in(rng, 6), position), (shards_of,), jnp.float32, smallest / len(shards), high / len(shards))
        gain = gain * jnp.repeat(jnp.exp(draws), dims[position] // shards_of).reshape((-1,) + (1,) * (len(dims) - 1 - position))
    return gain


def noise(rng, extent, width, bound, shards=(), kind=jnp.bfloat16):
    loudness = levels(rng, extent, shards, -0.22, 0.18) if shards else 1.0
    drawn = jax.random.normal(rng, extent, jnp.float32) * width * loudness
    return jnp.minimum(jnp.maximum(drawn, -bound), bound).astype(kind)


def setup_inputs(seed: int = 0) -> dict:
    seeds = jax.random.split(jax.random.key(seed), 8)
    obs_values = noise(seeds[0], (TILES, TILES, CAP, F), 1.0, 6.0, ((0, 128),))
    obs_cells = set_ends(jax.random.randint(seeds[1], (TILES, TILES, CAP), 0, TLAT * TLON), jax.random.fold_in(seeds[1], 1), 0, (TLAT * TLON) - 1).astype(jnp.int32)
    obs_counts = draw_obs_counts(jax.random.fold_in(seeds[7], 71), 0)
    embed_weight = noise(seeds[3], (F, C), F ** -0.5, 0.5)
    density_row = noise(seeds[4], (C,), 1.0, 6.0, (), jnp.float32)
    conv_weight = noise(seeds[5], (LAYERS, 3, 3, C, C), (9 * C) ** -0.5, 0.125)
    grid_cotangent = noise(seeds[6], (NLAT, NLON, C), 1.0, 6.0, ((0, 8), (1, 16)))
    return dict(obs_values=obs_values, obs_cells=obs_cells, obs_counts=obs_counts, embed_weight=embed_weight, density_row=density_row, conv_weight=conv_weight, grid_cotangent=grid_cotangent)


def gelu_grad(pre_act, upstream):
    return jax.vjp(jax.nn.gelu, pre_act)[1](upstream)[0]

def wrap_pad(field):
    with_poles = jnp.pad(field, ((1, 1), (0, 0), (0, 0)))
    return jnp.concatenate([with_poles[:, -1:], with_poles, with_poles[:, :1]], axis=1)

def conv_forward(padded, weight, row_count, col_count):
    summed = jnp.zeros((row_count * col_count, weight.shape[-1]), jnp.float32)
    for tap_row in range(3):
        for tap_col in range(3):
            window = padded[tap_row:tap_row + row_count, tap_col:tap_col + col_count].reshape(row_count * col_count, -1)
            summed = summed + jnp.dot(window, weight[tap_row, tap_col], preferred_element_type=jnp.float32)
    return summed

def conv_backward(padded_grad, weight, row_count, col_count):
    summed = jnp.zeros((row_count * col_count, weight.shape[-2]), jnp.float32)
    for tap_row in range(3):
        for tap_col in range(3):
            window = padded_grad[2 - tap_row:2 - tap_row + row_count, 2 - tap_col:2 - tap_col + col_count].reshape(row_count * col_count, -1)
            summed = summed + lax.dot_general(window, weight[tap_row, tap_col], (((1,), (1,)), ((), ())), preferred_element_type=jnp.float32)
    return summed

def kernel_grad(padded, pre_grad, row_count, col_count):
    taps = []
    for tap_row in range(3):
        for tap_col in range(3):
            window = padded[tap_row:tap_row + row_count, tap_col:tap_col + col_count].reshape(row_count * col_count, -1)
            taps.append(lax.dot_general(window, pre_grad, (((0,), (0,)), ((), ())), preferred_element_type=jnp.float32))
    return jnp.stack(taps).reshape(3, 3, pre_grad.shape[1], pre_grad.shape[1])

def reference(obs_values, obs_cells, obs_counts, embed_weight, density_row, conv_weight, grid_cotangent):
    row_count = TLAT * N_LAT
    col_count = TLON * N_LON
    slot_ids = jnp.arange(CAP, dtype=jnp.int32)
    is_valid = slot_ids[None, None, :] < obs_counts[:, :, None]
    tile_ids = jnp.arange(TILES, dtype=jnp.int32)[None, :, None]
    grid_row = tile_ids // N_LON * TLAT + obs_cells // TLON
    grid_col = tile_ids % N_LON * TLON + obs_cells % TLON
    flat_ids = (grid_row * col_count + grid_col).reshape(-1).astype(jnp.int32)
    used_mask = is_valid.reshape(-1).astype(jnp.float32)
    values = obs_values.reshape(-1, F).astype(jnp.float32) * used_mask[:, None]
    sums = jax.ops.segment_sum(values, flat_ids, num_segments=row_count * col_count)
    numbers = jax.ops.segment_sum(used_mask, flat_ids, num_segments=row_count * col_count)
    divisor = jnp.maximum(numbers, 1.0)
    cell_means = (sums / divisor[:, None]).astype(jnp.bfloat16)
    embedded = jnp.dot(cell_means, embed_weight, preferred_element_type=jnp.float32) + jnp.log1p(numbers)[:, None] * density_row[None, :]
    field = embedded.astype(jnp.bfloat16).reshape(row_count, col_count, C)
    stored_pads = []
    stored_pre = []
    for layer_idx in range(LAYERS):
        padded = wrap_pad(field)
        pre_act = conv_forward(padded, conv_weight[layer_idx], row_count, col_count)
        stored_pads.append(padded)
        stored_pre.append(pre_act)
        field = (field.reshape(-1, C).astype(jnp.float32) + jax.nn.gelu(pre_act)).astype(jnp.bfloat16).reshape(row_count, col_count, C)
    grid_out = field
    upstream = grid_cotangent.reshape(-1, C).astype(jnp.float32)
    kernel_grads = [None] * LAYERS
    for layer_idx in reversed(range(LAYERS)):
        pre_grad = gelu_grad(stored_pre[layer_idx], upstream).astype(jnp.bfloat16)
        kernel_grads[layer_idx] = kernel_grad(stored_pads[layer_idx], pre_grad, row_count, col_count)
        padded_grad = wrap_pad(pre_grad.reshape(row_count, col_count, C))
        upstream = upstream + conv_backward(padded_grad, conv_weight[layer_idx], row_count, col_count)
    top_grad = upstream.astype(jnp.bfloat16)
    grad_embed = lax.dot_general(cell_means, top_grad, (((0,), (0,)), ((), ())), preferred_element_type=jnp.float32)
    mean_grad = lax.dot_general(top_grad, embed_weight, (((1,), (1,)), ((), ())), preferred_element_type=jnp.float32)
    scaled = (mean_grad / divisor[:, None]).astype(jnp.bfloat16)
    picked = scaled[flat_ids].reshape(TILES, TILES, CAP, F)
    grad_obs = jnp.where(is_valid[..., None], picked, jnp.zeros_like(picked)).astype(jnp.bfloat16)
    return (grid_out, jnp.stack(kernel_grads), grad_embed, grad_obs)
```

```python
import functools

import jax
import jax.numpy as jnp
from jax import lax
from jax.experimental import pallas as pl
from jax.experimental.pallas import tpu as pltpu
from jax.sharding import PartitionSpec as P

MESH = pl.DeviceIdType.MESH
NA, NB = 8, 16
NT = NA * NB
TR, TC = 16, 48
CELLS = TR * TC
CH, F, CAP = 256, 128, 8
SLOTS = NT * CAP
HR = 4
HC = 2
SIDE = 8
W = TC + 2 * SIDE
STRIP = 16
UNITS = 592
F32, BF16 = jnp.float32, jnp.bfloat16
GC, GA = 0.7978845608028654, 0.044715


def coords():
    return lax.axis_index("lat"), lax.axis_index("lon")


def tile_dev(t):
    return (t // NB, lax.rem(t, NB))


def barrier_all():
    a, b = coords()
    me = a * NB + b
    sem = pltpu.get_barrier_semaphore()

    def signal(k, carry):
        t = lax.rem(me + k, NT)
        pl.semaphore_signal(sem, inc=1, device_id=tile_dev(t), device_id_type=MESH)
        return carry

    lax.fori_loop(1, NT, signal, 0)
    pl.semaphore_wait(sem, NT - 1)


def exchange_start(src, dst, send, recv):
    a, b = coords()
    me = a * NB + b

    def go(k, carry):
        t = lax.rem(me + k, NT)
        pltpu.make_async_remote_copy(
            src_ref=src.at[t],
            dst_ref=dst.at[me],
            send_sem=send,
            recv_sem=recv,
            device_id=tile_dev(t),
            device_id_type=MESH,
        ).start()
        return carry

    lax.fori_loop(1, NT, go, 0)
    pltpu.make_async_copy(src.at[me], dst.at[me], recv).start()


def exchange_wait_recv(dst, recv):
    pltpu.make_async_copy(dst, dst, recv).wait()


def exchange_wait_send(src, send):
    part = src.at[pl.ds(0, NT - 1)]
    pltpu.make_async_copy(part, part, send).wait()


DIRS = [(-1, 0), (1, 0), (0, -1), (0, 1), (-1, -1), (-1, 1), (1, -1), (1, 1)]


def halo_copies(src, bufs, rows, send, recv):
    a, b = coords()
    copies = []
    for i, (da, db) in enumerate(DIRS):
        back = DIRS.index((-da, -db))
        row = {-1: pl.ds(0, rows), 0: pl.ds(0, TR), 1: pl.ds(TR - rows, rows)}[da]
        col = {-1: pl.ds(0, STRIP), 0: pl.ds(0, TC), 1: pl.ds(TC - STRIP, STRIP)}[db]
        copies.append(
            pltpu.make_async_remote_copy(
                src_ref=src.at[row, col],
                dst_ref=bufs[back],
                send_sem=send.at[i],
                recv_sem=recv.at[back],
                device_id=(
                    jnp.clip(a + da, 0, NA - 1),
                    lax.rem(b + db + NB, NB),
                ),
                device_id_type=MESH,
            )
        )
    return copies


def when_exists(da, fn):
    a, _ = coords()
    if da == 0:
        fn()
    elif da < 0:
        pl.when(a > 0)(fn)
    else:
        pl.when(a < NA - 1)(fn)


def halo_start(copies):
    for (da, _), copy in zip(DIRS, copies):
        when_exists(da, copy.start)


def halo_wait(src, bufs, rows, send, recv):
    copies = halo_copies(src, bufs, rows, send, recv)
    for i, (da, db) in enumerate(DIRS):
        when_exists(da, copies[i].wait_send)
        back = DIRS.index((-da, -db))
        when_exists(da, copies[back].wait_recv)


def halo_zero(bufs):
    for i, (da, _) in enumerate(DIRS):
        if da:

            def clear(buf=bufs[i]):
                buf[...] = jnp.zeros(buf.shape, buf.dtype)

            a, _ = coords()
            pl.when(a == (0 if da < 0 else NA - 1))(clear)


def ext_row(core, bufs, rows, r):
    if r < rows:
        left, mid, right, k = bufs[4], bufs[0], bufs[5], r
    elif r < rows + TR:
        left, mid, right, k = bufs[2], core, bufs[3], r - rows
    else:
        left, mid, right, k = bufs[6], bufs[1], bufs[7], r - rows - TR
    return jnp.concatenate(
        [
            left[k].astype(F32)[STRIP - SIDE :],
            mid[k].astype(F32),
            right[k].astype(F32)[:SIDE],
        ],
        axis=0,
    )


def put3(dst, rows, value):
    n = value.shape[0] // W
    for q, shift in ((0, 1), (1, 0), (2, value.shape[0] - 1)):
        moved = value if shift == 0 else pltpu.roll(value, shift, 0)
        dst[rows, :, q * CH : (q + 1) * CH] = moved.astype(BF16).reshape(n, W, CH)


def row_mask(first, n):
    rows = lax.broadcasted_iota(jnp.int32, (n * W, CH), 0) // W + first
    return (rows >= 0) & (rows < NA * TR)


def gelu_parts(x):
    x2 = x * x
    t = jnp.tanh(GC * x * (1.0 + GA * x2))
    half = 0.5 * (1.0 + t)
    value = x * half
    slope = half + 0.5 * x * (1.0 - t * t) * (GC * (1.0 + 3.0 * GA * x2))
    return value, slope


def conv_fwd(src, weight, layer, start, n):
    acc = None
    for p in range(3):
        window = src[pl.ds(start + p, n)].reshape(n * W, 3 * CH)
        part = jnp.dot(window, weight[layer, p], preferred_element_type=F32)
        acc = part if acc is None else acc + part
    return acc


def conv_bwd(src, weight, layer, start, n):
    acc = None
    for p in range(3):
        for q in range(3):
            lanes = slice((2 - q) * CH, (3 - q) * CH)
            window = src[pl.ds(start + 2 - p, n), :, lanes].reshape(n * W, CH)
            part = lax.dot_general(
                window,
                weight[layer, p, q * CH : (q + 1) * CH],
                (((1,), (1,)), ((), ())),
                preferred_element_type=F32,
            )
            acc = part if acc is None else acc + part
    return acc


def store_units(dst, first, value):
    n = value.shape[0] // 8
    for h in range(2):
        dst[first : first + n, h] = value[:, h * 128 : (h + 1) * 128].astype(BF16).reshape(n, 8, 128)


def kernel_grad(src, first, grad, dst, unit):
    col = lax.broadcasted_iota(jnp.int32, (TR * W, CH), 0) & (W - 1)
    masked = jnp.where((col >= SIDE) & (col < SIDE + TC), grad.astype(F32), 0.0).astype(BF16)
    for p in range(3):
        window = src[first + p : first + p + TR].reshape(TR * W, 3 * CH)
        taps = lax.dot_general(
            window, masked, (((0,), (0,)), ((), ())), preferred_element_type=F32
        )
        store_units(dst, unit + p * 96, taps)


def main_kernel(
    payload, embed, density, weight, cot,
    out_ref, grads_ref, picked_ref,
    recv, onehot, means, inv, field,
    fN, fS, fW, fE, fNW, fNE, fSW, fSE,
    cN, cS, cW, cE, cNW, cNE, cSW, cSE,
    x0, x1, g1, g0, slope0, cot_ext, up1, grid2, top,
    a2a_sem, halo_send, halo_recv, cot_send, cot_recv,
):
    a, _ = coords()
    fbufs = (fN, fS, fW, fE, fNW, fNE, fSW, fSE)
    cbufs = (cN, cS, cW, cE, cNW, cNE, cSW, cSE)
    barrier_all()
    exchange_start(payload, recv, a2a_sem.at[0], a2a_sem.at[1])
    halo_start(halo_copies(cot, cbufs, HC, cot_send, cot_recv))
    halo_zero(fbufs)
    halo_zero(cbufs)
    halo_wait(cot, cbufs, HC, cot_send, cot_recv)
    for r in range(TR + 2 * HC):
        cot_ext[r] = ext_row(cot, cbufs, HC, r)
    exchange_wait_recv(recv, a2a_sem.at[1])

    group = 16

    def build(i, carry):
        codes = recv[pl.ds(i * group, group), 8:16, :].astype(F32).reshape(group * CAP, F)
        cell = (codes[:, 0:1] * TC + codes[:, 64:65]).astype(jnp.int32)
        lane = lax.broadcasted_iota(jnp.int32, (group * CAP, CELLS), 1)
        onehot[pl.ds(i * group * CAP, group * CAP), :] = jnp.where(cell == lane, 1.0, 0.0).astype(BF16)
        return carry

    lax.fori_loop(0, NT // group, build, 0)
    values = recv[:, 0:8, :].reshape(SLOTS, F)
    both = jnp.concatenate([values, jnp.ones((SLOTS, F), BF16)], axis=1)
    sums = lax.dot_general(
        onehot[...], both, (((0,), (0,)), ((), ())), preferred_element_type=F32
    )
    numbers = sums[:, F:]
    divisor = jnp.maximum(numbers, 1.0)
    inv[...] = divisor
    cell_means = (sums[:, :F] / divisor).astype(BF16)
    means[...] = cell_means
    logs = jnp.log(1.0 + numbers)
    embedded = jnp.dot(cell_means, embed[...], preferred_element_type=F32) + jnp.concatenate(
        [logs, logs], axis=1
    ) * density[...]
    field[...] = embedded.astype(BF16).reshape(TR, TC, CH)

    halo_start(halo_copies(field, fbufs, HR, halo_send, halo_recv))
    halo_wait(field, fbufs, HR, halo_send, halo_recv)
    for r in range(TR + 2 * HR):
        put3(x0, slice(r, r + 1), ext_row(field, fbufs, HR, r))

    n = 11

    def fwd0(c, carry):
        pre = conv_fwd(x0, weight, 0, c * n, n)
        value, slope = gelu_parts(pre)
        old = x0[pl.ds(c * n + 1, n), :, CH : 2 * CH].reshape(n * W, CH).astype(F32)
        new = jnp.where(row_mask(a * TR - 3 + c * n, n), old + value, 0.0)
        new = new.astype(BF16).astype(F32)
        put3(x1, pl.ds(c * n, n), new)
        slope0[pl.ds(c * n, n)] = slope.reshape(n, W, CH)
        return carry

    lax.fori_loop(0, 2, fwd0, 0)
    m = 10

    def fwd1(c, carry):
        pre = conv_fwd(x1, weight, 1, c * m, m)
        value, slope = gelu_parts(pre)
        old = x1[pl.ds(c * m + 1, m), :, CH : 2 * CH].reshape(m * W, CH).astype(F32)
        grid2[pl.ds(c * m, m)] = (old + value).astype(BF16).reshape(m, W, CH)
        grad = cot_ext[pl.ds(c * m, m)].reshape(m * W, CH) * slope
        put3(g1, pl.ds(c * m, m), grad.astype(BF16).astype(F32))
        return carry

    lax.fori_loop(0, 2, fwd1, 0)
    out_ref[...] = grid2[2 : 2 + TR, SIDE : SIDE + TC, :]

    kernel_grad(x1, 2, g1[2 : 2 + TR, :, CH : 2 * CH].reshape(TR * W, CH), grads_ref, 288)
    k = 9

    def bwd1(c, carry):
        up = conv_bwd(g1, weight, 1, c * k, k) + cot_ext[pl.ds(c * k + 1, k)].reshape(k * W, CH)
        up1[pl.ds(c * k, k)] = up.reshape(k, W, CH)
        grad = up * slope0[pl.ds(c * k + 2, k)].reshape(k * W, CH)
        grad = jnp.where(row_mask(a * TR - 1 + c * k, k), grad, 0.0)
        put3(g0, pl.ds(c * k, k), grad.astype(BF16).astype(F32))
        return carry

    lax.fori_loop(0, 2, bwd1, 0)
    kernel_grad(x0, 3, g0[1 : 1 + TR, :, CH : 2 * CH].reshape(TR * W, CH), grads_ref, 0)
    j = 8

    def bwd0(c, carry):
        up = conv_bwd(g0, weight, 0, c * j, j) + up1[pl.ds(c * j + 1, j)].reshape(j * W, CH)
        top[pl.ds(c * j, j)] = up.reshape(j, W, CH)[:, SIDE : SIDE + TC].astype(BF16)
        return carry

    lax.fori_loop(0, 2, bwd0, 0)
    top_grad = top[...].reshape(CELLS, CH)
    store_units(
        grads_ref,
        576,
        lax.dot_general(
            means[...], top_grad, (((0,), (0,)), ((), ())), preferred_element_type=F32
        ),
    )
    mean_grad = lax.dot_general(
        top_grad, embed[...], (((1,), (1,)), ((), ())), preferred_element_type=F32
    )
    scaled = (mean_grad / inv[...]).astype(BF16)
    picked = jnp.dot(onehot[...], scaled, preferred_element_type=F32)
    picked_ref[...] = picked.astype(BF16).reshape(NT, CAP, F)
    exchange_wait_send(payload, a2a_sem.at[0])


ORDERS = (("x", "y", "z"), ("y", "z", "x"), ("z", "x", "y"))


def place():
    a, b = coords()
    return {"z": a // 2, "x": lax.rem(a, 2) * 2 + b // 8, "y": lax.rem(b // 2, 4), "c": lax.rem(b, 2)}


def device_at(pos):
    x = pos["x"]
    return (pos["z"] * 2 + x // 2, lax.rem(x, 2) * 8 + pos["y"] * 2 + pos["c"])


def along(pos, axis, step):
    moved = dict(pos)
    moved[axis] = lax.rem(pos[axis] + step, 4)
    return moved


def remote(src, dst, send, recv, pos):
    copy = pltpu.make_async_remote_copy(
        src_ref=src, dst_ref=dst, send_sem=send, recv_sem=recv,
        device_id=device_at(pos), device_id_type=MESH,
    )
    copy.start()


def wait_bytes(ref, sem):
    pltpu.make_async_copy(ref, ref, sem).wait()


def add_parts(own, got):
    total = own.astype(F32)
    for i in range(3):
        total = total + got[i].astype(F32)
    return total.astype(BF16)


def reduce_kernel(
    grads, picked, total, back,
    pair, own, r1, r2, r3, t1, t2, e1, e2, e3, f1, f2,
    a2a_sem, pair_sem, ssem, rsem, gssem, grsem,
):
    pos = place()
    c = pos["c"]
    sibling = dict(pos)
    sibling["c"] = 1 - c
    barrier_all()
    remote(grads.at[:, 1 - c], pair, pair_sem.at[0], pair_sem.at[1], sibling)
    wait_bytes(pair, pair_sem.at[1])
    own[...] = (grads[:, c].astype(F32) + pair[...].astype(F32)).astype(BF16)

    sizes = (48, 12, 3)
    for s, order in enumerate(ORDERS):
        for step in range(1, 4):
            peer = along(pos, order[0], step)
            first = s * 192 + peer[order[0]] * 48
            remote(own.at[pl.ds(first, 48)], r1.at[s, step - 1], ssem.at[0, s], rsem.at[0, s], peer)
    for step in range(1, 4):
        peer = along(pos, "x", step)
        remote(own.at[pl.ds(576 + peer["x"] * 4, 4)], e1.at[step - 1], ssem.at[0, 3], rsem.at[0, 3], peer)
    exchange_start(picked, back, a2a_sem.at[0], a2a_sem.at[1])
    for s, order in enumerate(ORDERS):
        wait_bytes(r1.at[s], rsem.at[0, s])
        t1[s] = add_parts(own[pl.ds(s * 192 + pos[order[0]] * 48, 48)], r1.at[s])
        for step in range(1, 4):
            peer = along(pos, order[1], step)
            first = peer[order[1]] * 12
            remote(t1.at[s, pl.ds(first, 12)], r2.at[s, step - 1], ssem.at[1, s], rsem.at[1, s], peer)
    wait_bytes(e1, rsem.at[0, 3])
    f1[...] = add_parts(own[pl.ds(576 + pos["x"] * 4, 4)], e1)
    for step in range(1, 4):
        peer = along(pos, "y", step)
        remote(f1.at[pl.ds(peer["y"], 1)], e2.at[step - 1], ssem.at[1, 3], rsem.at[1, 3], peer)
    for s, order in enumerate(ORDERS):
        wait_bytes(r2.at[s], rsem.at[1, s])
        t2[s] = add_parts(t1[s, pl.ds(pos[order[1]] * 12, 12)], r2.at[s])
        for step in range(1, 4):
            peer = along(pos, order[2], step)
            first = peer[order[2]] * 3
            remote(t2.at[s, pl.ds(first, 3)], r3.at[s, step - 1], ssem.at[2, s], rsem.at[2, s], peer)
    wait_bytes(e2, rsem.at[1, 3])
    f2[...] = add_parts(f1[pl.ds(pos["y"], 1)], e2)
    for step in range(1, 4):
        peer = along(pos, "z", step)
        remote(f2, e3.at[step - 1], ssem.at[2, 3], rsem.at[2, 3], peer)

    base = [s * 192 + pos[o[0]] * 48 + pos[o[1]] * 12 + pos[o[2]] * 3 for s, o in enumerate(ORDERS)]
    for s, order in enumerate(ORDERS):
        wait_bytes(r3.at[s], rsem.at[2, s])
        total[pl.ds(base[s], 3), c] = add_parts(t2[s, pl.ds(pos[order[2]] * 3, 3)], r3.at[s])
        block = total.at[pl.ds(base[s], 3), c]
        for step in range(1, 4):
            remote(block, block, gssem.at[0, s], grsem.at[0, s], along(pos, order[2], step))
    wait_bytes(e3, rsem.at[2, 3])
    ebase = 576 + pos["x"] * 4 + pos["y"]
    total[pl.ds(ebase, 1), c] = add_parts(f2[...], e3)
    block = total.at[pl.ds(ebase, 1), c]
    for step in range(1, 4):
        remote(block, block, gssem.at[0, 3], grsem.at[0, 3], along(pos, "y", step))
    for s, order in enumerate(ORDERS):
        wait_bytes(total.at[pl.ds(0, 9), c], grsem.at[0, s])
        block = total.at[pl.ds(s * 192 + pos[order[0]] * 48 + pos[order[1]] * 12, 12), c]
        for step in range(1, 4):
            remote(block, block, gssem.at[1, s], grsem.at[1, s], along(pos, order[1], step))
    wait_bytes(total.at[pl.ds(0, 3), c], grsem.at[0, 3])
    block = total.at[pl.ds(576 + pos["x"] * 4, 4), c]
    for step in range(1, 4):
        remote(block, block, gssem.at[1, 3], grsem.at[1, 3], along(pos, "x", step))
    for s, order in enumerate(ORDERS):
        wait_bytes(total.at[pl.ds(0, 36), c], grsem.at[1, s])
        block = total.at[pl.ds(s * 192 + pos[order[0]] * 48, 48), c]
        for step in range(1, 4):
            remote(block, block, gssem.at[2, s], grsem.at[2, s], along(pos, order[0], step))
    wait_bytes(total.at[pl.ds(0, 12), c], grsem.at[1, 3])
    for s in range(3):
        wait_bytes(total.at[pl.ds(0, 144), c], grsem.at[2, s])
    half = total.at[:, c]
    remote(half, half, pair_sem.at[2], pair_sem.at[3], sibling)

    exchange_wait_recv(back, a2a_sem.at[1])
    exchange_wait_send(picked, a2a_sem.at[0])
    wait_bytes(pair, pair_sem.at[0])
    for phase in range(3):
        for s in range(3):
            wait_bytes(own.at[pl.ds(0, 3 * sizes[phase])], ssem.at[phase, s])
            wait_bytes(own.at[pl.ds(0, 3 * sizes[2 - phase])], gssem.at[phase, s])
    for phase, units in enumerate((12, 3, 3)):
        wait_bytes(own.at[pl.ds(0, units)], ssem.at[phase, 3])
    for phase, units in enumerate((3, 12)):
        wait_bytes(own.at[pl.ds(0, units)], gssem.at[phase, 3])
    wait_bytes(pair, pair_sem.at[2])
    wait_bytes(pair, pair_sem.at[3])


VM = pl.BlockSpec(memory_space=pltpu.VMEM)
DMA = pltpu.SemaphoreType.DMA


def vmem(shape, dtype=BF16):
    return pltpu.VMEM(shape, dtype)


def halo_shapes(rows):
    wide, side, corner = (rows, TC, CH), (TR, STRIP, CH), (rows, STRIP, CH)
    return [vmem(s) for s in (wide, wide, side, side, corner, corner, corner, corner)]


def body(obs_values, obs_cells, obs_counts, embed_weight, density_row, conv_weight, grid_cotangent):
    cells, counts = obs_cells[0], obs_counts[0]
    used = jnp.arange(CAP, dtype=jnp.int32)[None, :] < counts[:, None]
    row = jnp.where(used, cells // TC, -100)[:, :, None]
    col = (cells % TC)[:, :, None]
    lane = jnp.arange(F, dtype=jnp.int32)[None, None, :]
    codes = jnp.where(lane < 64, row, col).astype(BF16)
    payload = jnp.concatenate([obs_values[0], codes], axis=1)
    weight = conv_weight.reshape(2, 3, 3 * CH, CH)
    field, grads, picked = pl.pallas_call(
        main_kernel,
        out_shape=[
            jax.ShapeDtypeStruct((TR, TC, CH), BF16),
            jax.ShapeDtypeStruct((UNITS, 2, 8, 128), BF16),
            jax.ShapeDtypeStruct((NT, CAP, F), BF16),
        ],
        in_specs=[VM] * 5,
        out_specs=[VM] * 3,
        scratch_shapes=[
            vmem((NT, 16, F)), vmem((SLOTS, CELLS)), vmem((CELLS, F)), vmem((CELLS, F), F32),
            vmem((TR, TC, CH)), *halo_shapes(HR), *halo_shapes(HC),
            vmem((24, W, 3 * CH)), vmem((22, W, 3 * CH)), vmem((20, W, 3 * CH)), vmem((18, W, 3 * CH)),
            vmem((22, W, CH), F32), vmem((20, W, CH), F32), vmem((18, W, CH), F32),
            vmem((20, W, CH)), vmem((TR, TC, CH)),
            DMA((2,)), DMA((8,)), DMA((8,)), DMA((8,)), DMA((8,)),
        ],
        compiler_params=pltpu.CompilerParams(
            collective_id=0, has_side_effects=True, vmem_limit_bytes=56 * 2**20
        ),
    )(payload, embed_weight, density_row.reshape(1, CH), weight, grid_cotangent)
    total, back = pl.pallas_call(
        reduce_kernel,
        out_shape=[
            jax.ShapeDtypeStruct((UNITS, 2, 8, 128), BF16),
            jax.ShapeDtypeStruct((NT, CAP, F), BF16),
        ],
        in_specs=[VM] * 2,
        out_specs=[VM] * 2,
        scratch_shapes=[
            vmem((UNITS, 8, 128)), vmem((UNITS, 8, 128)),
            vmem((3, 3, 48, 8, 128)), vmem((3, 3, 12, 8, 128)), vmem((3, 3, 3, 8, 128)),
            vmem((3, 48, 8, 128)), vmem((3, 12, 8, 128)),
            vmem((3, 4, 8, 128)), vmem((3, 1, 8, 128)), vmem((3, 1, 8, 128)),
            vmem((4, 8, 128)), vmem((1, 8, 128)),
            DMA((2,)), DMA((4,)), DMA((3, 4)), DMA((3, 4)), DMA((3, 4)), DMA((3, 4)),
        ],
        compiler_params=pltpu.CompilerParams(
            collective_id=1, has_side_effects=True, vmem_limit_bytes=40 * 2**20
        ),
    )(grads, picked)
    whole = total.transpose(0, 2, 1, 3).reshape(UNITS * 8, CH).astype(F32)
    grad_conv = whole[:4608].reshape(2, 3, 3, CH, CH)
    return field, grad_conv, whole[4608:], back[None]


def solution(mesh):
    return jax.shard_map(
        body,
        mesh=mesh,
        in_specs=(
            P(("lat", "lon"), None, None, None),
            P(("lat", "lon"), None, None),
            P(("lat", "lon"), None),
            P(),
            P(),
            P(),
            P("lat", "lon", None),
        ),
        out_specs=(P("lat", "lon", None), P(), P(), P(("lat", "lon"), None, None, None)),
        check_vma=False,
    )
```

```python
import functools

import jax
import jax.numpy as jnp
from jax import lax
from jax.experimental import pallas as pl
from jax.experimental.pallas import tpu as pltpu
from jax.sharding import PartitionSpec as P

MESH = pl.DeviceIdType.MESH
NA, NB = 8, 16
NT = NA * NB
TR, TC = 16, 48
CELLS = TR * TC
CH, F, CAP = 256, 128, 8
SLOTS = NT * CAP
HR = 4
HC = 2
SIDE = 8
W = TC + 2 * SIDE
STRIP = 16
UNITS = 592
F32, BF16 = jnp.float32, jnp.bfloat16
GC, GA = 0.7978845608028654, 0.044715


def coords():
    return lax.axis_index("lat"), lax.axis_index("lon")


def tile_dev(t):
    return (t // NB, lax.rem(t, NB))


def barrier_signal():
    a, b = coords()
    me = a * NB + b
    sem = pltpu.get_barrier_semaphore()

    def signal(k, carry):
        t = lax.rem(me + k, NT)
        pl.semaphore_signal(sem, inc=1, device_id=tile_dev(t), device_id_type=MESH)
        return carry

    lax.fori_loop(1, NT, signal, 0)


def barrier_wait():
    pl.semaphore_wait(pltpu.get_barrier_semaphore(), NT - 1)


def exchange_start(src, dst, send, recv):
    a, b = coords()
    me = a * NB + b

    def go(k, carry):
        ta = lax.rem(a + k // NB, NA)
        tb = lax.rem(b + lax.rem(k, NB), NB)
        pltpu.make_async_remote_copy(
            src_ref=src.at[ta * NB + tb],
            dst_ref=dst.at[me],
            send_sem=send,
            recv_sem=recv.at[a],
            device_id=(ta, tb),
            device_id_type=MESH,
        ).start()
        return carry

    pltpu.make_async_copy(src.at[me], dst.at[me], recv.at[a]).start()
    lax.fori_loop(1, NT, go, 0)


def exchange_wait_recv(dst, recv, lat):
    part = dst.at[pl.ds(lat * NB, NB)]
    pltpu.make_async_copy(part, part, recv.at[lat]).wait()


def exchange_wait_send(src, send):
    part = src.at[pl.ds(0, NT - 1)]
    pltpu.make_async_copy(part, part, send).wait()


DIRS = [(-1, 0), (1, 0), (0, -1), (0, 1), (-1, -1), (-1, 1), (1, -1), (1, 1)]


def halo_copies(src, bufs, rows, send, recv):
    a, b = coords()
    copies = []
    for i, (da, db) in enumerate(DIRS):
        back = DIRS.index((-da, -db))
        row = {-1: pl.ds(0, rows), 0: pl.ds(0, TR), 1: pl.ds(TR - rows, rows)}[da]
        col = {-1: pl.ds(0, STRIP), 0: pl.ds(0, TC), 1: pl.ds(TC - STRIP, STRIP)}[db]
        copies.append(
            pltpu.make_async_remote_copy(
                src_ref=src.at[row, col],
                dst_ref=bufs[back],
                send_sem=send.at[i],
                recv_sem=recv.at[back],
                device_id=(
                    jnp.clip(a + da, 0, NA - 1),
                    lax.rem(b + db + NB, NB),
                ),
                device_id_type=MESH,
            )
        )
    return copies


def when_exists(da, fn):
    a, _ = coords()
    if da == 0:
        fn()
    elif da < 0:
        pl.when(a > 0)(fn)
    else:
        pl.when(a < NA - 1)(fn)


def halo_start(copies):
    for (da, _), copy in zip(DIRS, copies):
        when_exists(da, copy.start)


def halo_wait(src, bufs, rows, send, recv):
    copies = halo_copies(src, bufs, rows, send, recv)
    for i, (da, db) in enumerate(DIRS):
        when_exists(da, copies[i].wait_send)
        back = DIRS.index((-da, -db))
        when_exists(da, copies[back].wait_recv)


def halo_zero(bufs):
    for i, (da, _) in enumerate(DIRS):
        if da:

            def clear(buf=bufs[i]):
                buf[...] = jnp.zeros(buf.shape, buf.dtype)

            a, _ = coords()
            pl.when(a == (0 if da < 0 else NA - 1))(clear)


def ext_row(core, bufs, rows, r):
    if r < rows:
        left, mid, right, k = bufs[4], bufs[0], bufs[5], r
    elif r < rows + TR:
        left, mid, right, k = bufs[2], core, bufs[3], r - rows
    else:
        left, mid, right, k = bufs[6], bufs[1], bufs[7], r - rows - TR
    return jnp.concatenate(
        [
            left[k].astype(F32)[STRIP - SIDE :],
            mid[k].astype(F32),
            right[k].astype(F32)[:SIDE],
        ],
        axis=0,
    )


def put3(dst, rows, value):
    n = value.shape[0] // W
    for q, shift in ((0, 1), (1, 0), (2, value.shape[0] - 1)):
        moved = value if shift == 0 else pltpu.roll(value, shift, 0)
        dst[rows, :, q * CH : (q + 1) * CH] = moved.astype(BF16).reshape(n, W, CH)


def row_mask(first, n):
    rows = lax.broadcasted_iota(jnp.int32, (n * W, CH), 0) // W + first
    return (rows >= 0) & (rows < NA * TR)


def gelu_parts(x):
    x2 = x * x
    t = jnp.tanh(GC * x * (1.0 + GA * x2))
    half = 0.5 * (1.0 + t)
    value = x * half
    slope = half + 0.5 * x * (1.0 - t * t) * (GC * (1.0 + 3.0 * GA * x2))
    return value, slope


def conv_fwd(src, weight, layer, start, n):
    acc = None
    for p in range(3):
        window = src[pl.ds(start + p, n)].reshape(n * W, 3 * CH)
        part = jnp.dot(window, weight[layer, p], preferred_element_type=F32)
        acc = part if acc is None else acc + part
    return acc


def conv_bwd(src, weight, layer, start, n):
    acc = None
    for p in range(3):
        for q in range(3):
            lanes = slice((2 - q) * CH, (3 - q) * CH)
            window = src[pl.ds(start + 2 - p, n), :, lanes].reshape(n * W, CH)
            part = lax.dot_general(
                window,
                weight[layer, p, q * CH : (q + 1) * CH],
                (((1,), (1,)), ((), ())),
                preferred_element_type=F32,
            )
            acc = part if acc is None else acc + part
    return acc


def store_units(dst, first, value):
    n = value.shape[0] // 8
    for h in range(2):
        dst[first : first + n, h] = value[:, h * 128 : (h + 1) * 128].astype(BF16).reshape(n, 8, 128)


def kernel_grad(src, first, grad, dst, unit, taps_of):
    col = lax.broadcasted_iota(jnp.int32, (TR * W, CH), 0) & (W - 1)
    masked = jnp.where((col >= SIDE) & (col < SIDE + TC), grad.astype(F32), 0.0).astype(BF16)
    for p in taps_of:
        window = src[first + p : first + p + TR].reshape(TR * W, 3 * CH)
        taps = lax.dot_general(
            window, masked, (((0,), (0,)), ((), ())), preferred_element_type=F32
        )
        store_units(dst, unit + p * 96, taps)


ORDERS = (("x", "y", "z"), ("y", "z", "x"), ("z", "x", "y"))
WAVES = ((384, 1), (0, 2))
EMBED0, EMBED_UNITS = 576, 16


def place():
    a, b = coords()
    return {"z": a // 2, "x": lax.rem(a, 2) * 2 + b // 8, "y": lax.rem(b // 2, 4), "c": lax.rem(b, 2)}


def device_at(pos):
    x = pos["x"]
    return (pos["z"] * 2 + x // 2, lax.rem(x, 2) * 8 + pos["y"] * 2 + pos["c"])


def along(pos, axis, step):
    moved = dict(pos)
    moved[axis] = lax.rem(pos[axis] + step, 4)
    return moved


def other_core(pos):
    moved = dict(pos)
    moved["c"] = 1 - pos["c"]
    return moved


def remote(src, dst, send, recv, pos):
    pltpu.make_async_remote_copy(
        src_ref=src, dst_ref=dst, send_sem=send, recv_sem=recv,
        device_id=device_at(pos), device_id_type=MESH,
    ).start()


def wait_bytes(ref, sem):
    pltpu.make_async_copy(ref, ref, sem).wait()


def add_parts(own, got, count):
    total = own.astype(F32)
    for i in range(count):
        total = total + got[i].astype(F32)
    return total.astype(BF16)


def on_plane(pos, axes, fn):
    def step(k, carry):
        peer = along(along(pos, axes[0], k // 4), axes[1], lax.rem(k, 4))
        fn(peer, k - 1)
        return carry

    lax.fori_loop(1, 16, step, 0)


class Wave:
    def __init__(self, w, pos, grads, total, bufs, sems):
        self.first, self.per = WAVES[w]
        self.pos, self.grads, self.total = pos, grads, total
        self.pair, self.own, self.r1, self.t1, self.r2 = bufs
        self.pair_sem, self.sem = sems
        self.stream = 64 * self.per

    def send(self, s, phase):
        return self.sem.at[s, phase, 0]

    def recv(self, s, phase):
        return self.sem.at[s, phase, 1]

    def mine(self):
        return self.grads.at[pl.ds(self.first, 3 * self.stream), 1 - self.pos["c"]]

    def pair_start(self):
        remote(self.mine(), self.pair, self.pair_sem.at[0], self.pair_sem.at[1], other_core(self.pos))

    def rs1_start(self):
        pos, part = self.pos, 16 * self.per
        wait_bytes(self.pair, self.pair_sem.at[1])
        kept = self.grads[pl.ds(self.first, 3 * self.stream), pos["c"]]
        self.own[...] = (kept.astype(F32) + self.pair[...].astype(F32)).astype(BF16)
        for step in (2, 1, 3):
            for s, order in enumerate(ORDERS):
                peer = along(pos, order[0], step)
                src = self.own.at[pl.ds(s * self.stream + peer[order[0]] * part, part)]
                remote(src, self.r1.at[s, step - 1], self.send(s, 0), self.recv(s, 0), peer)

    def rs2_start(self):
        pos, part, per = self.pos, 16 * self.per, self.per
        for s, order in enumerate(ORDERS):
            wait_bytes(self.r1.at[s], self.recv(s, 0))
            kept = self.own[pl.ds(s * self.stream + pos[order[0]] * part, part)]
            self.t1[s] = add_parts(kept, self.r1.at[s], 3)

            def go(peer, k, s=s, order=order):
                src = self.t1.at[s, pl.ds((peer[order[1]] * 4 + peer[order[2]]) * per, per)]
                remote(src, self.r2.at[s, k], self.send(s, 1), self.recv(s, 1), peer)

            on_plane(pos, order[1:], go)

    def block(self, s, order):
        pos, per = self.pos, self.per
        start = self.first + s * self.stream + pos[order[0]] * 16 * per
        return start, (pos[order[1]] * 4 + pos[order[2]]) * per

    def ag2_start(self):
        pos, per, c = self.pos, self.per, self.pos["c"]
        for s, order in enumerate(ORDERS):
            wait_bytes(self.r2.at[s], self.recv(s, 1))
            start, inner = self.block(s, order)
            self.total[pl.ds(start + inner, per), c] = add_parts(
                self.t1[s, pl.ds(inner, per)], self.r2.at[s], 15
            )
            block = self.total.at[pl.ds(start + inner, per), c]

            def go(peer, k, s=s, block=block):
                remote(block, block, self.send(s, 2), self.recv(s, 2), peer)

            on_plane(pos, order[1:], go)

    def ag1_start(self):
        pos, per, c = self.pos, self.per, self.pos["c"]
        for s, order in enumerate(ORDERS):
            wait_bytes(self.total.at[pl.ds(0, 15 * per), c], self.recv(s, 2))
            start, _ = self.block(s, order)
            block = self.total.at[pl.ds(start, 16 * per), c]
            for step in (2, 1, 3):
                remote(block, block, self.send(s, 3), self.recv(s, 3), along(pos, order[0], step))

    def pair2_start(self):
        c = self.pos["c"]
        for s in range(3):
            wait_bytes(self.total.at[pl.ds(0, 48 * self.per), c], self.recv(s, 3))
            block = self.total.at[pl.ds(self.first + s * self.stream, self.stream), c]
            remote(block, block, self.send(s, 4), self.recv(s, 4), other_core(self.pos))

    def finish(self):
        c, per = self.pos["c"], self.per
        wait_bytes(self.pair, self.pair_sem.at[0])
        for s in range(3):
            for phase, units in enumerate((48, 15, 15, 48, 64)):
                wait_bytes(self.total.at[pl.ds(0, units * per), c], self.send(s, phase))
            wait_bytes(self.total.at[pl.ds(0, self.stream), c], self.recv(s, 4))


class EmbedSum:
    def __init__(self, pos, grads, total, bufs, sem):
        self.pos, self.grads, self.total, self.sem = pos, grads, total, sem
        self.pair, self.own, self.r1, self.t1, self.r2 = bufs

    def pair_start(self):
        src = self.grads.at[pl.ds(EMBED0, EMBED_UNITS), 1 - self.pos["c"]]
        remote(src, self.pair, self.sem.at[0, 0], self.sem.at[0, 1], other_core(self.pos))

    def rs_start(self):
        pos = self.pos
        wait_bytes(self.pair, self.sem.at[0, 1])
        kept = self.grads[pl.ds(EMBED0, EMBED_UNITS), pos["c"]]
        self.own[...] = (kept.astype(F32) + self.pair[...].astype(F32)).astype(BF16)

        def go(peer, k):
            src = self.own.at[pl.ds(peer["y"] * 4 + peer["z"], 1)]
            remote(src, self.r1.at[k], self.sem.at[1, 0], self.sem.at[1, 1], peer)

        on_plane(pos, ("y", "z"), go)

    def sum_start(self):
        pos = self.pos
        wait_bytes(self.r1, self.sem.at[1, 1])
        self.t1[...] = add_parts(self.own[pl.ds(pos["y"] * 4 + pos["z"], 1)], self.r1, 15)
        for step in range(1, 4):
            remote(self.t1, self.r2.at[step - 1], self.sem.at[2, 0], self.sem.at[2, 1], along(pos, "x", step))

    def ag_start(self):
        pos, c = self.pos, self.pos["c"]
        wait_bytes(self.r2, self.sem.at[2, 1])
        at = EMBED0 + pos["y"] * 4 + pos["z"]
        parts = []
        for i in range(4):
            got = self.t1[...].astype(F32)
            for step in range(1, 4):
                got = jnp.where(lax.rem(pos["x"] - step + 4, 4) == i, self.r2[step - 1].astype(F32), got)
            parts.append(got)
        self.total[pl.ds(at, 1), c] = (((parts[0] + parts[1]) + parts[2]) + parts[3]).astype(BF16)
        block = self.total.at[pl.ds(at, 1), c]
        on_plane(
            pos, ("y", "z"),
            lambda peer, k: remote(block, block, self.sem.at[3, 0], self.sem.at[3, 1], peer),
        )

    def pair2_start(self):
        c = self.pos["c"]
        wait_bytes(self.total.at[pl.ds(0, 15), c], self.sem.at[3, 1])
        block = self.total.at[pl.ds(EMBED0, EMBED_UNITS), c]
        remote(block, block, self.sem.at[4, 0], self.sem.at[4, 1], other_core(self.pos))

    def finish(self):
        c = self.pos["c"]
        for phase, units in enumerate((16, 15, 3, 15, 16)):
            wait_bytes(self.total.at[pl.ds(0, units), c], self.sem.at[phase, 0])
        wait_bytes(self.total.at[pl.ds(0, 16), c], self.sem.at[4, 1])


def make_payload(payload, values, cells, counts, table):
    eye = lax.broadcasted_iota(jnp.int32, (NT, NT), 0) == lax.broadcasted_iota(jnp.int32, (NT, NT), 1)
    used = jnp.where(eye, counts[...].astype(F32), 0.0).sum(axis=1, keepdims=True)
    slot = lax.broadcasted_iota(jnp.int32, (NT, CAP), 1).astype(F32)
    cell = cells[...]
    row = (cell * 1366) >> 16
    table[...] = jnp.zeros_like(table)
    table[:, 0:CAP] = jnp.where(slot < used, row.astype(F32), -100.0)
    table[:, CAP : 2 * CAP] = (cell - row * TC).astype(F32)
    spread = jnp.broadcast_to(table[...][:, None, :], (NT, CAP, F)).reshape(SLOTS, F)
    sub = lax.broadcasted_iota(jnp.int32, (SLOTS, F), 0) & (CAP - 1)
    lane = lax.broadcasted_iota(jnp.int32, (SLOTS, F), 1)
    spread = jnp.where((lane & (CAP - 1)) == sub, spread, 0.0).astype(BF16)
    l0 = lax.broadcasted_iota(jnp.int32, (F, F), 0)
    l1 = lax.broadcasted_iota(jnp.int32, (F, F), 1)
    pick = ((l0 < CAP) & (l1 < 64)) | ((l0 >= CAP) & (l0 < 2 * CAP) & (l1 >= 64))
    codes = jnp.dot(spread, jnp.where(pick, 1.0, 0.0).astype(BF16), preferred_element_type=F32)
    payload[:, 0:CAP, :] = values[...]
    payload[:, CAP : 2 * CAP, :] = codes.astype(BF16).reshape(NT, CAP, F)


def kernel(
    values_hbm, cells_hbm, counts_hbm, embed_hbm, density_hbm, weight_hbm, cot_hbm,
    out_ref, total, back,
    values, cells, counts, embed, density, weight, cot, table,
    payload, recv, onehot, means, inv, field,
    fN, fS, fW, fE, fNW, fNE, fSW, fSE,
    cN, cS, cW, cE, cNW, cNE, cSW, cSE,
    x0, x1, g1, g0, slope0, cot_ext, up1, grid2, top, grads, picked,
    *rest,
):
    w1_bufs, w2_bufs, e_bufs = rest[0:5], rest[5:10], rest[10:15]
    (load_sem, a2a_send, a2a_recv, halo_send, halo_recv, cot_send, cot_recv,
     w1_pair, w1_sem, w2_pair, w2_sem, e_sem) = rest[15:]
    a, _ = coords()
    pos = place()
    fbufs = (fN, fS, fW, fE, fNW, fNE, fSW, fSE)
    cbufs = (cN, cS, cW, cE, cNW, cNE, cSW, cSE)
    w1 = Wave(0, pos, grads, total, w1_bufs, (w1_pair, w1_sem))
    w2 = Wave(1, pos, grads, total, w2_bufs, (w2_pair, w2_sem))
    es = EmbedSum(pos, grads, total, e_bufs, e_sem)
    loads = [
        pltpu.make_async_copy(src, dst, load_sem.at[i])
        for i, (src, dst) in enumerate(
            (
                (cells_hbm, cells), (counts_hbm, counts), (values_hbm, values), (cot_hbm, cot),
                (embed_hbm, embed), (density_hbm, density), (weight_hbm, weight),
            )
        )
    ]
    for load in loads:
        load.start()
    barrier_signal()
    for load in loads[:3]:
        load.wait()
    make_payload(payload, values, cells, counts, table)
    halo_zero(fbufs)
    halo_zero(cbufs)
    loads[3].wait()
    barrier_wait()
    exchange_start(payload, recv, a2a_send, a2a_recv)
    halo_start(halo_copies(cot, cbufs, HC, cot_send, cot_recv))
    for load in loads[4:]:
        load.wait()

    def build(i, carry):
        lat = lax.rem(a - i + NA, NA)
        exchange_wait_recv(recv, a2a_recv, lat)
        rows = pl.ds(lat * NB * CAP, NB * CAP)
        codes = recv[pl.ds(lat * NB, NB), CAP : 2 * CAP, :].astype(F32).reshape(NB * CAP, F)
        cell = (codes[:, 0:1] * TC + codes[:, 64:65]).astype(jnp.int32)
        lane = lax.broadcasted_iota(jnp.int32, (NB * CAP, CELLS), 1)
        onehot[rows, :] = jnp.where(cell == lane, 1.0, 0.0).astype(BF16)
        return carry

    lax.fori_loop(0, NA, build, 0)
    both = jnp.concatenate([recv[:, 0:CAP, :].reshape(SLOTS, F), jnp.ones((SLOTS, F), BF16)], axis=1)
    sums = lax.dot_general(
        onehot[...], both, (((0,), (0,)), ((), ())), preferred_element_type=F32
    )
    numbers = sums[:, F:]
    divisor = jnp.maximum(numbers, 1.0)
    inv[...] = divisor
    cell_means = (sums[:, :F] / divisor).astype(BF16)
    means[...] = cell_means
    logs = jnp.log(1.0 + numbers)
    embedded = jnp.dot(cell_means, embed[...], preferred_element_type=F32) + jnp.concatenate(
        [logs, logs], axis=1
    ) * density[...]
    field[...] = embedded.astype(BF16).reshape(TR, TC, CH)
    halo_start(halo_copies(field, fbufs, HR, halo_send, halo_recv))
    halo_wait(cot, cbufs, HC, cot_send, cot_recv)
    for r in range(TR + 2 * HC):
        cot_ext[r] = ext_row(cot, cbufs, HC, r)
    halo_wait(field, fbufs, HR, halo_send, halo_recv)
    for r in range(TR + 2 * HR):
        put3(x0, slice(r, r + 1), ext_row(field, fbufs, HR, r))

    n = 11

    def fwd0(c, carry):
        pre = conv_fwd(x0, weight, 0, c * n, n)
        value, slope = gelu_parts(pre)
        old = x0[pl.ds(c * n + 1, n), :, CH : 2 * CH].reshape(n * W, CH).astype(F32)
        new = jnp.where(row_mask(a * TR - 3 + c * n, n), old + value, 0.0)
        new = new.astype(BF16).astype(F32)
        put3(x1, pl.ds(c * n, n), new)
        slope0[pl.ds(c * n, n)] = slope.reshape(n, W, CH)
        return carry

    lax.fori_loop(0, 2, fwd0, 0)
    m = 10

    def fwd1(c, carry):
        pre = conv_fwd(x1, weight, 1, c * m, m)
        value, slope = gelu_parts(pre)
        old = x1[pl.ds(c * m + 1, m), :, CH : 2 * CH].reshape(m * W, CH).astype(F32)
        grid2[pl.ds(c * m, m)] = (old + value).astype(BF16).reshape(m, W, CH)
        grad = cot_ext[pl.ds(c * m, m)].reshape(m * W, CH) * slope
        put3(g1, pl.ds(c * m, m), grad.astype(BF16).astype(F32))
        return carry

    lax.fori_loop(0, 2, fwd1, 0)

    grad1 = g1[2 : 2 + TR, :, CH : 2 * CH].reshape(TR * W, CH)
    kernel_grad(x1, 2, grad1, grads, 288, (1, 2))
    w1.pair_start()
    k = 9

    def bwd1(c, carry):
        up = conv_bwd(g1, weight, 1, c * k, k) + cot_ext[pl.ds(c * k + 1, k)].reshape(k * W, CH)
        up1[pl.ds(c * k, k)] = up.reshape(k, W, CH)
        grad = up * slope0[pl.ds(c * k + 2, k)].reshape(k * W, CH)
        grad = jnp.where(row_mask(a * TR - 1 + c * k, k), grad, 0.0)
        put3(g0, pl.ds(c * k, k), grad.astype(BF16).astype(F32))
        return carry

    lax.fori_loop(0, 2, bwd1, 0)
    w1.rs1_start()
    kernel_grad(x1, 2, grad1, grads, 288, (0,))
    kernel_grad(x0, 3, g0[1 : 1 + TR, :, CH : 2 * CH].reshape(TR * W, CH), grads, 0, (0, 1, 2))
    w2.pair_start()
    j = 8

    def bwd0(c, carry):
        up = conv_bwd(g0, weight, 0, c * j, j) + up1[pl.ds(c * j + 1, j)].reshape(j * W, CH)
        top[pl.ds(c * j, j)] = up.reshape(j, W, CH)[:, SIDE : SIDE + TC].astype(BF16)
        return carry

    lax.fori_loop(0, 2, bwd0, 0)
    w2.rs1_start()
    w1.rs2_start()
    top_grad = top[...].reshape(CELLS, CH)
    store_units(
        grads,
        EMBED0,
        lax.dot_general(
            means[...], top_grad, (((0,), (0,)), ((), ())), preferred_element_type=F32
        ),
    )
    es.pair_start()
    mean_grad = lax.dot_general(
        top_grad, embed[...], (((1,), (1,)), ((), ())), preferred_element_type=F32
    )
    scaled = (mean_grad / inv[...]).astype(BF16)
    picked[...] = jnp.dot(onehot[...], scaled, preferred_element_type=F32).astype(BF16).reshape(NT, CAP, F)
    out_ref[...] = grid2[2 : 2 + TR, SIDE : SIDE + TC, :]
    exchange_wait_send(payload, a2a_send)
    es.rs_start()
    w1.ag2_start()
    w2.rs2_start()
    exchange_start(picked, back, a2a_send, a2a_recv)
    es.sum_start()
    w1.ag1_start()
    w2.ag2_start()
    es.ag_start()
    w1.pair2_start()
    w2.ag1_start()
    es.pair2_start()
    w2.pair2_start()
    for lat in range(NA):
        exchange_wait_recv(back, a2a_recv, lat)
    exchange_wait_send(picked, a2a_send)
    w1.finish()
    w2.finish()
    es.finish()


VM = pl.BlockSpec(memory_space=pltpu.VMEM)
ANY = pl.BlockSpec(memory_space=pl.ANY)
DMA = pltpu.SemaphoreType.DMA


def vmem(shape, dtype=BF16):
    return pltpu.VMEM(shape, dtype)


def halo_shapes(rows):
    wide, side, corner = (rows, TC, CH), (TR, STRIP, CH), (rows, STRIP, CH)
    return [vmem(s) for s in (wide, wide, side, side, corner, corner, corner, corner)]


def wave_shapes(w):
    per = WAVES[w][1]
    units = 192 * per
    return [
        vmem((units, 8, 128)), vmem((units, 8, 128)), vmem((3, 3, 16 * per, 8, 128)),
        vmem((3, 16 * per, 8, 128)), vmem((3, 15, per, 8, 128)),
    ]


def body(obs_values, obs_cells, obs_counts, embed_weight, density_row, conv_weight, grid_cotangent):
    weight = conv_weight.reshape(2, 3, 3 * CH, CH)
    field, total, back = pl.pallas_call(
        kernel,
        out_shape=[
            jax.ShapeDtypeStruct((TR, TC, CH), BF16),
            jax.ShapeDtypeStruct((UNITS, 2, 8, 128), BF16),
            jax.ShapeDtypeStruct((NT, CAP, F), BF16),
        ],
        in_specs=[ANY] * 7,
        out_specs=[VM] * 3,
        scratch_shapes=[
            vmem((NT, CAP, F)), vmem((NT, CAP), jnp.int32), vmem((1, NT), jnp.int32), vmem((F, CH)),
            vmem((1, CH), F32), vmem((2, 3, 3 * CH, CH)), vmem((TR, TC, CH)), vmem((NT, F), F32),
            vmem((NT, 16, F)), vmem((NT, 16, F)), vmem((SLOTS, CELLS)), vmem((CELLS, F)), vmem((CELLS, F), F32),
            vmem((TR, TC, CH)), *halo_shapes(HR), *halo_shapes(HC),
            vmem((24, W, 3 * CH)), vmem((22, W, 3 * CH)), vmem((20, W, 3 * CH)), vmem((18, W, 3 * CH)),
            vmem((22, W, CH), F32), vmem((20, W, CH), F32), vmem((18, W, CH), F32),
            vmem((20, W, CH)), vmem((TR, TC, CH)), vmem((UNITS, 2, 8, 128)), vmem((NT, CAP, F)),
            *wave_shapes(0), *wave_shapes(1),
            vmem((16, 8, 128)), vmem((16, 8, 128)), vmem((15, 1, 8, 128)), vmem((1, 8, 128)), vmem((3, 1, 8, 128)),
            DMA((7,)), DMA, DMA((NA,)), DMA((8,)), DMA((8,)), DMA((8,)), DMA((8,)),
            DMA((2,)), DMA((3, 5, 2)), DMA((2,)), DMA((3, 5, 2)), DMA((5, 2)),
        ],
        compiler_params=pltpu.CompilerParams(
            collective_id=0, has_side_effects=True, vmem_limit_bytes=56 * 2**20
        ),
    )(
        obs_values[0], obs_cells[0], obs_counts, embed_weight, density_row.reshape(1, CH), weight, grid_cotangent
    )
    whole = total.transpose(0, 2, 1, 3).reshape(UNITS * 8, CH).astype(F32)
    grad_conv = whole[:4608].reshape(2, 3, 3, CH, CH)
    return field, grad_conv, whole[4608:], back[None]


def solution(mesh):
    return jax.shard_map(
        body,
        mesh=mesh,
        in_specs=(
            P(("lat", "lon"), None, None, None),
            P(("lat", "lon"), None, None),
            P(("lat", "lon"), None),
            P(),
            P(),
            P(),
            P("lat", "lon", None),
        ),
        out_specs=(P("lat", "lon", None), P(), P(), P(("lat", "lon"), None, None, None)),
        check_vma=False,
    )
```

```python
import functools

import jax
import jax.numpy as jnp
from jax import lax
from jax.experimental import pallas as pl
from jax.experimental.pallas import tpu as pltpu
from jax.sharding import PartitionSpec as P

MESH = pl.DeviceIdType.MESH
NA, NB = 8, 16
NT = NA * NB
TR, TC = 16, 48
CELLS = TR * TC
CH, F, CAP = 256, 128, 8
SLOTS = NT * CAP
HR = 4
HC = 2
SIDE = 8
W = TC + 2 * SIDE
STRIP = 16
UNITS = 592
F32, BF16 = jnp.float32, jnp.bfloat16
GC, GA = 0.7978845608028654, 0.044715


def coords():
    return lax.axis_index("lat"), lax.axis_index("lon")


def tile_dev(t):
    return (t // NB, lax.rem(t, NB))


def barrier_signal():
    a, b = coords()
    me = a * NB + b
    sem = pltpu.get_barrier_semaphore()

    def signal(k, carry):
        t = lax.rem(me + k, NT)
        pl.semaphore_signal(sem, inc=1, device_id=tile_dev(t), device_id_type=MESH)
        return carry

    lax.fori_loop(1, NT, signal, 0)


def barrier_wait():
    pl.semaphore_wait(pltpu.get_barrier_semaphore(), NT - 1)


def exchange_start(src, dst, send, recv):
    a, b = coords()
    me = a * NB + b

    def go(k, carry):
        ta = lax.rem(a + k // NB, NA)
        tb = lax.rem(b + lax.rem(k, NB), NB)
        pltpu.make_async_remote_copy(
            src_ref=src.at[ta * NB + tb],
            dst_ref=dst.at[me],
            send_sem=send,
            recv_sem=recv.at[a],
            device_id=(ta, tb),
            device_id_type=MESH,
        ).start()
        return carry

    pltpu.make_async_copy(src.at[me], dst.at[me], recv.at[a]).start()
    lax.fori_loop(1, NT, go, 0)


def exchange_wait_recv(dst, recv, lat):
    part = dst.at[pl.ds(lat * NB, NB)]
    pltpu.make_async_copy(part, part, recv.at[lat]).wait()


def exchange_wait_send(src, send):
    part = src.at[pl.ds(0, NT - 1)]
    pltpu.make_async_copy(part, part, send).wait()


DIRS = [(-1, 0), (1, 0), (0, -1), (0, 1), (-1, -1), (-1, 1), (1, -1), (1, 1)]


def halo_copies(src, bufs, rows, send, recv):
    a, b = coords()
    copies = []
    for i, (da, db) in enumerate(DIRS):
        back = DIRS.index((-da, -db))
        row = {-1: pl.ds(0, rows), 0: pl.ds(0, TR), 1: pl.ds(TR - rows, rows)}[da]
        col = {-1: pl.ds(0, STRIP), 0: pl.ds(0, TC), 1: pl.ds(TC - STRIP, STRIP)}[db]
        copies.append(
            pltpu.make_async_remote_copy(
                src_ref=src.at[row, col],
                dst_ref=bufs[back],
                send_sem=send.at[i],
                recv_sem=recv.at[back],
                device_id=(
                    jnp.clip(a + da, 0, NA - 1),
                    lax.rem(b + db + NB, NB),
                ),
                device_id_type=MESH,
            )
        )
    return copies


def when_exists(da, fn):
    a, _ = coords()
    if da == 0:
        fn()
    elif da < 0:
        pl.when(a > 0)(fn)
    else:
        pl.when(a < NA - 1)(fn)


def halo_start(copies):
    for (da, _), copy in zip(DIRS, copies):
        when_exists(da, copy.start)


def halo_wait(src, bufs, rows, send, recv):
    copies = halo_copies(src, bufs, rows, send, recv)
    for i, (da, db) in enumerate(DIRS):
        when_exists(da, copies[i].wait_send)
        back = DIRS.index((-da, -db))
        when_exists(da, copies[back].wait_recv)


def halo_zero(bufs):
    for i, (da, _) in enumerate(DIRS):
        if da:

            def clear(buf=bufs[i]):
                buf[...] = jnp.zeros(buf.shape, buf.dtype)

            a, _ = coords()
            pl.when(a == (0 if da < 0 else NA - 1))(clear)


def ext_row(core, bufs, rows, r):
    if r < rows:
        left, mid, right, k = bufs[4], bufs[0], bufs[5], r
    elif r < rows + TR:
        left, mid, right, k = bufs[2], core, bufs[3], r - rows
    else:
        left, mid, right, k = bufs[6], bufs[1], bufs[7], r - rows - TR
    return jnp.concatenate(
        [
            left[k].astype(F32)[STRIP - SIDE :],
            mid[k].astype(F32),
            right[k].astype(F32)[:SIDE],
        ],
        axis=0,
    )


def put3(dst, rows, value):
    n = value.shape[0] // W
    for q, shift in ((0, 1), (1, 0), (2, value.shape[0] - 1)):
        moved = value if shift == 0 else pltpu.roll(value, shift, 0)
        dst[rows, :, q * CH : (q + 1) * CH] = moved.astype(BF16).reshape(n, W, CH)


def row_mask(first, n):
    rows = lax.broadcasted_iota(jnp.int32, (n * W, CH), 0) // W + first
    return (rows >= 0) & (rows < NA * TR)


def gelu_parts(x):
    x2 = x * x
    t = jnp.tanh(GC * x * (1.0 + GA * x2))
    half = 0.5 * (1.0 + t)
    value = x * half
    slope = half + 0.5 * x * (1.0 - t * t) * (GC * (1.0 + 3.0 * GA * x2))
    return value, slope


def conv_fwd(src, weight, layer, start, n):
    acc = None
    for p in range(3):
        window = src[pl.ds(start + p, n)].reshape(n * W, 3 * CH)
        part = jnp.dot(window, weight[layer, p], preferred_element_type=F32)
        acc = part if acc is None else acc + part
    return acc


def conv_bwd(src, weight, layer, start, n):
    acc = None
    for p in range(3):
        for q in range(3):
            lanes = slice((2 - q) * CH, (3 - q) * CH)
            window = src[pl.ds(start + 2 - p, n), :, lanes].reshape(n * W, CH)
            part = lax.dot_general(
                window,
                weight[layer, p, q * CH : (q + 1) * CH],
                (((1,), (1,)), ((), ())),
                preferred_element_type=F32,
            )
            acc = part if acc is None else acc + part
    return acc


def store_units(dst, first, value):
    n = value.shape[0] // 8
    for h in range(2):
        dst[first : first + n, h] = value[:, h * 128 : (h + 1) * 128].astype(BF16).reshape(n, 8, 128)


def kernel_grad(src, first, grad, dst, unit, taps_of):
    for p in taps_of:
        window = src[first + p : first + p + TR, SIDE : SIDE + TC, :].reshape(CELLS, 3 * CH)
        taps = lax.dot_general(
            window, grad, (((0,), (0,)), ((), ())), preferred_element_type=F32
        )
        store_units(dst, unit + p * 96, taps)


ORDERS = (("x", "y", "z"), ("y", "z", "x"), ("z", "x", "y"))
WAVES = ((384, 1), (0, 2))
EMBED0, EMBED_UNITS = 576, 16


def place():
    a, b = coords()
    return {"z": a // 2, "x": lax.rem(a, 2) * 2 + b // 8, "y": lax.rem(b // 2, 4), "c": lax.rem(b, 2)}


def device_at(pos):
    x = pos["x"]
    return (pos["z"] * 2 + x // 2, lax.rem(x, 2) * 8 + pos["y"] * 2 + pos["c"])


def along(pos, axis, step):
    moved = dict(pos)
    moved[axis] = lax.rem(pos[axis] + step, 4)
    return moved


def other_core(pos):
    moved = dict(pos)
    moved["c"] = 1 - pos["c"]
    return moved


def remote(src, dst, send, recv, pos):
    pltpu.make_async_remote_copy(
        src_ref=src, dst_ref=dst, send_sem=send, recv_sem=recv,
        device_id=device_at(pos), device_id_type=MESH,
    ).start()


def wait_bytes(ref, sem):
    pltpu.make_async_copy(ref, ref, sem).wait()


def add_parts(own, got, count):
    total = own.astype(F32)
    for i in range(count):
        total = total + got[i].astype(F32)
    return total.astype(BF16)


def on_plane(pos, axes, fn):
    def step(k, carry):
        peer = along(along(pos, axes[0], k // 4), axes[1], lax.rem(k, 4))
        fn(peer, k - 1)
        return carry

    lax.fori_loop(1, 16, step, 0)


class Wave:
    def __init__(self, w, pos, grads, total, bufs, sems):
        self.first, self.per = WAVES[w]
        self.pos, self.grads, self.total = pos, grads, total
        self.pair, self.own, self.r1, self.t1, self.r2 = bufs
        self.pair_sem, self.sem = sems
        self.stream = 64 * self.per

    def send(self, s, phase):
        return self.sem.at[s, phase, 0]

    def recv(self, s, phase):
        return self.sem.at[s, phase, 1]

    def mine(self):
        return self.grads.at[pl.ds(self.first, 3 * self.stream), 1 - self.pos["c"]]

    def pair_start(self):
        remote(self.mine(), self.pair, self.pair_sem.at[0], self.pair_sem.at[1], other_core(self.pos))

    def rs1_start(self):
        pos, part = self.pos, 16 * self.per
        wait_bytes(self.pair, self.pair_sem.at[1])
        kept = self.grads[pl.ds(self.first, 3 * self.stream), pos["c"]]
        self.own[...] = (kept.astype(F32) + self.pair[...].astype(F32)).astype(BF16)
        for step in (2, 1, 3):
            for s, order in enumerate(ORDERS):
                peer = along(pos, order[0], step)
                src = self.own.at[pl.ds(s * self.stream + peer[order[0]] * part, part)]
                remote(src, self.r1.at[s, step - 1], self.send(s, 0), self.recv(s, 0), peer)

    def rs2_start(self):
        pos, part, per = self.pos, 16 * self.per, self.per
        for s, order in enumerate(ORDERS):
            wait_bytes(self.r1.at[s], self.recv(s, 0))
            kept = self.own[pl.ds(s * self.stream + pos[order[0]] * part, part)]
            self.t1[s] = add_parts(kept, self.r1.at[s], 3)

            def go(peer, k, s=s, order=order):
                src = self.t1.at[s, pl.ds((peer[order[1]] * 4 + peer[order[2]]) * per, per)]
                remote(src, self.r2.at[s, k], self.send(s, 1), self.recv(s, 1), peer)

            on_plane(pos, order[1:], go)

    def block(self, s, order):
        pos, per = self.pos, self.per
        start = self.first + s * self.stream + pos[order[0]] * 16 * per
        return start, (pos[order[1]] * 4 + pos[order[2]]) * per

    def ag2_start(self):
        pos, per, c = self.pos, self.per, self.pos["c"]
        for s, order in enumerate(ORDERS):
            wait_bytes(self.r2.at[s], self.recv(s, 1))
            start, inner = self.block(s, order)
            self.total[pl.ds(start + inner, per), c] = add_parts(
                self.t1[s, pl.ds(inner, per)], self.r2.at[s], 15
            )
            block = self.total.at[pl.ds(start + inner, per), c]

            def go(peer, k, s=s, block=block):
                remote(block, block, self.send(s, 2), self.recv(s, 2), peer)

            on_plane(pos, order[1:], go)

    def ag1_start(self):
        pos, per, c = self.pos, self.per, self.pos["c"]
        for s, order in enumerate(ORDERS):
            wait_bytes(self.total.at[pl.ds(0, 15 * per), c], self.recv(s, 2))
            start, _ = self.block(s, order)
            block = self.total.at[pl.ds(start, 16 * per), c]
            for step in (2, 1, 3):
                remote(block, block, self.send(s, 3), self.recv(s, 3), along(pos, order[0], step))

    def pair2_start(self):
        c = self.pos["c"]
        for s in range(3):
            wait_bytes(self.total.at[pl.ds(0, 48 * self.per), c], self.recv(s, 3))
            block = self.total.at[pl.ds(self.first + s * self.stream, self.stream), c]
            remote(block, block, self.send(s, 4), self.recv(s, 4), other_core(self.pos))

    def finish(self):
        c, per = self.pos["c"], self.per
        wait_bytes(self.pair, self.pair_sem.at[0])
        for s in range(3):
            for phase, units in enumerate((48, 15, 15, 48, 64)):
                wait_bytes(self.total.at[pl.ds(0, units * per), c], self.send(s, phase))
            wait_bytes(self.total.at[pl.ds(0, self.stream), c], self.recv(s, 4))


class EmbedSum:
    def __init__(self, pos, grads, total, bufs, sem):
        self.pos, self.grads, self.total, self.sem = pos, grads, total, sem
        self.pair, self.own, self.r1, self.t1, self.r2 = bufs

    def pair_start(self):
        src = self.grads.at[pl.ds(EMBED0, EMBED_UNITS), 1 - self.pos["c"]]
        remote(src, self.pair, self.sem.at[0, 0], self.sem.at[0, 1], other_core(self.pos))

    def rs_start(self):
        pos = self.pos
        wait_bytes(self.pair, self.sem.at[0, 1])
        kept = self.grads[pl.ds(EMBED0, EMBED_UNITS), pos["c"]]
        self.own[...] = (kept.astype(F32) + self.pair[...].astype(F32)).astype(BF16)

        def go(peer, k):
            src = self.own.at[pl.ds(peer["y"] * 4 + peer["z"], 1)]
            remote(src, self.r1.at[k], self.sem.at[1, 0], self.sem.at[1, 1], peer)

        on_plane(pos, ("y", "z"), go)

    def sum_start(self):
        pos = self.pos
        wait_bytes(self.r1, self.sem.at[1, 1])
        self.t1[...] = add_parts(self.own[pl.ds(pos["y"] * 4 + pos["z"], 1)], self.r1, 15)
        for step in range(1, 4):
            remote(self.t1, self.r2.at[step - 1], self.sem.at[2, 0], self.sem.at[2, 1], along(pos, "x", step))

    def ag_start(self):
        pos, c = self.pos, self.pos["c"]
        wait_bytes(self.r2, self.sem.at[2, 1])
        at = EMBED0 + pos["y"] * 4 + pos["z"]
        parts = []
        for i in range(4):
            got = self.t1[...].astype(F32)
            for step in range(1, 4):
                got = jnp.where(lax.rem(pos["x"] - step + 4, 4) == i, self.r2[step - 1].astype(F32), got)
            parts.append(got)
        self.total[pl.ds(at, 1), c] = (((parts[0] + parts[1]) + parts[2]) + parts[3]).astype(BF16)
        block = self.total.at[pl.ds(at, 1), c]
        on_plane(
            pos, ("y", "z"),
            lambda peer, k: remote(block, block, self.sem.at[3, 0], self.sem.at[3, 1], peer),
        )

    def pair2_start(self):
        c = self.pos["c"]
        wait_bytes(self.total.at[pl.ds(0, 15), c], self.sem.at[3, 1])
        block = self.total.at[pl.ds(EMBED0, EMBED_UNITS), c]
        remote(block, block, self.sem.at[4, 0], self.sem.at[4, 1], other_core(self.pos))

    def finish(self):
        c = self.pos["c"]
        for phase, units in enumerate((16, 15, 3, 15, 16)):
            wait_bytes(self.total.at[pl.ds(0, units), c], self.sem.at[phase, 0])
        wait_bytes(self.total.at[pl.ds(0, 16), c], self.sem.at[4, 1])


def make_table(table, cells, counts):
    slot = lax.broadcasted_iota(jnp.int32, (CAP, NT), 0)
    cell = cells[...]
    row = (cell * 1366) >> 16
    table[0] = jnp.where(slot < counts[...], row, -100).astype(F32).astype(BF16)
    table[1] = (cell - row * TC).astype(F32).astype(BF16)


def to_group(fn, count):
    def step(k, carry):
        fn(k)
        return carry

    lax.fori_loop(1, count, step, 0)


def codes_start(table, tables, sem):
    a, b = coords()
    pltpu.make_async_copy(table, tables.at[b], sem.at[1]).start()

    def go(k):
        pltpu.make_async_remote_copy(
            src_ref=table, dst_ref=tables.at[b], send_sem=sem.at[0], recv_sem=sem.at[1],
            device_id=(a, lax.rem(b + k, NB)), device_id_type=MESH,
        ).start()

    to_group(go, NB)


def codes_forward(tables, mine, got, sem):
    a, b = coords()
    wait_bytes(tables, sem.at[1])
    lat = lax.broadcasted_iota(jnp.int32, (NA, NT), 0)
    tile = lax.broadcasted_iota(jnp.int32, (NA, NT), 1)
    pick = jnp.where(tile == lat * NB + b, 1.0, 0.0).astype(BF16)
    nt = (((1,), (1,)), ((), ()))
    rows = lax.dot_general(pick, tables[:, 0].reshape(NB * CAP, NT), nt, preferred_element_type=F32)
    cols = lax.dot_general(pick, tables[:, 1].reshape(NB * CAP, NT), nt, preferred_element_type=F32)
    codes = rows * TC + cols
    for i in range(NA):
        mine[i] = codes[i : i + 1]
    pltpu.make_async_copy(mine.at[a], got.at[a], sem.at[3]).start()

    def go(k):
        to = lax.rem(a + k, NA)
        pltpu.make_async_remote_copy(
            src_ref=mine.at[to], dst_ref=got.at[a], send_sem=sem.at[2], recv_sem=sem.at[3],
            device_id=(to, b), device_id_type=MESH,
        ).start()

    to_group(go, NA)


def place_codes(got, onehot, sem):
    wait_bytes(got, sem.at[3])
    rows = [got[i] for i in range(NA)] + [jnp.zeros((NT - NA, NT), F32)]
    codes = jnp.concatenate(rows, axis=0).T
    lane = lax.broadcasted_iota(jnp.int32, (NB * CAP, CELLS), 1).astype(F32)
    for i in range(NA):
        hit = codes[:, i : i + 1] == lane
        onehot[i * NB * CAP : (i + 1) * NB * CAP, :] = jnp.where(hit, 1.0, 0.0).astype(BF16)


def eye(dtype=None):
    return lax.broadcasted_iota(jnp.int32, (128, 128), 0) == lax.broadcasted_iota(jnp.int32, (128, 128), 1)


def pack_numbers(numbers, packed):
    mask = eye()
    for i in range(CELLS // 128):
        packed[i : i + 1] = jnp.where(mask, numbers[i * 128 : (i + 1) * 128], 0.0).sum(axis=0, keepdims=True)


def unpack_numbers(packed, first, count, out):
    mask = eye()
    ones = jnp.ones((256, 128), BF16)
    for i in range(count):
        row = packed[first + i : first + i + 1]
        high = jnp.floor(row * 0.125) * 8.0
        parts = [jnp.where(mask, jnp.broadcast_to(v, (128, 128)), 0.0).astype(BF16) for v in (high, row - high)]
        out[i * 128 : (i + 1) * 128] = jnp.dot(
            jnp.concatenate(parts, axis=1), ones, preferred_element_type=F32
        )


PACKED = {-1: (4, 2), 0: (0, 6), 1: (0, 2)}


def numbers_row(own, bufs, r):
    if r < HR:
        left, mid, right, at = bufs[4], bufs[0], bufs[5], (TR - HR + r) * TC - 512
    elif r < HR + TR:
        left, mid, right, at = bufs[2], own, bufs[3], (r - HR) * TC
    else:
        left, mid, right, at = bufs[6], bufs[1], bufs[7], (r - HR - TR) * TC
    return jnp.concatenate(
        [left[at + TC - SIDE : at + TC], mid[at : at + TC], right[at : at + SIDE]], axis=0
    )


def packed_copies(packed, bufs, send, recv):
    a, b = coords()
    copies = []
    for i, (da, db) in enumerate(DIRS):
        back = DIRS.index((-da, -db))
        copies.append(
            pltpu.make_async_remote_copy(
                src_ref=packed, dst_ref=bufs.at[back], send_sem=send.at[i], recv_sem=recv.at[back],
                device_id=(jnp.clip(a + da, 0, NA - 1), lax.rem(b + db + NB, NB)), device_id_type=MESH,
            )
        )
    return copies


def waits(copies):
    for i, (da, db) in enumerate(DIRS):
        when_exists(da, copies[i].wait_send)
        when_exists(da, copies[DIRS.index((-da, -db))].wait_recv)


def kernel(
    values_hbm, cells_hbm, counts_hbm, embed_hbm, density_hbm, weight_hbm, cot_hbm,
    out_ref, total, back,
    values, cells, counts, embed, density, weight, cot,
    table, tables, codes_mine, codes_got, recv, onehot, means, numbers, packed, packs,
    nN, nS, nW, nE, nNW, nNE, nSW, nSE,
    fN, fS, fW, fE, fNW, fNE, fSW, fSE,
    cN, cS, cW, cE, cNW, cNE, cSW, cSE,
    x0, x1, g1, g0, slope0, cot_ext, up1, grid2, top, grads, picked,
    *rest,
):
    w1_bufs, w2_bufs, e_bufs = rest[0:5], rest[5:10], rest[10:15]
    (load_sem, a2a_send, a2a_recv, back_send, back_recv, code_sem, halo_send, halo_recv, pack_send, pack_recv, cot_send, cot_recv,
     w1_pair, w1_sem, w2_pair, w2_sem, e_sem) = rest[15:]
    a, _ = coords()
    pos = place()
    fbufs = (fN, fS, fW, fE, fNW, fNE, fSW, fSE)
    nbufs = (nN, nS, nW, nE, nNW, nNE, nSW, nSE)
    cbufs = (cN, cS, cW, cE, cNW, cNE, cSW, cSE)
    w1 = Wave(0, pos, grads, total, w1_bufs, (w1_pair, w1_sem))
    w2 = Wave(1, pos, grads, total, w2_bufs, (w2_pair, w2_sem))
    es = EmbedSum(pos, grads, total, e_bufs, e_sem)
    barrier_signal()
    loads = [
        pltpu.make_async_copy(src, dst, load_sem.at[i])
        for i, (src, dst) in enumerate(
            (
                (cells_hbm, cells), (counts_hbm, counts), (values_hbm, values), (cot_hbm, cot),
                (embed_hbm, embed), (density_hbm, density), (weight_hbm, weight),
            )
        )
    ]
    for load in loads:
        load.start()
    halo_zero(fbufs)
    halo_zero(cbufs)
    halo_zero([packs.at[i] for i in range(8)])
    packed[...] = jnp.zeros_like(packed)
    for load in loads[:3]:
        load.wait()
    make_table(table, cells, counts)
    barrier_wait()
    codes_start(table, tables, code_sem)
    exchange_start(values, recv, a2a_send, a2a_recv)
    codes_forward(tables, codes_mine, codes_got, code_sem)
    for load in loads[3:]:
        load.wait()
    place_codes(codes_got, onehot, code_sem)
    for lat in range(NA):
        exchange_wait_recv(recv, a2a_recv, lat)
    both = jnp.concatenate([recv[...].reshape(SLOTS, F), jnp.ones((SLOTS, F), BF16)], axis=1)
    sums = lax.dot_general(
        onehot[...], both, (((0,), (0,)), ((), ())), preferred_element_type=F32
    )
    numbers[...] = sums[:, F:]
    means[...] = (sums[:, :F] / jnp.maximum(sums[:, F:], 1.0)).astype(BF16).reshape(TR, TC, F)
    pack_numbers(numbers, packed)
    halo = halo_copies(means, fbufs, HR, halo_send, halo_recv)
    packs_out = packed_copies(packed, packs, pack_send, pack_recv)
    halo_start(packs_out)
    halo_start(halo)
    cot_halo = halo_copies(cot, cbufs, HC, cot_send, cot_recv)
    halo_start(cot_halo)
    waits(packs_out)
    for i, (da, db) in enumerate(DIRS):
        first, count = PACKED[da]
        unpack_numbers(packs.at[i], first, count, nbufs[i])
    waits(halo)
    for r in range(TR + 2 * HR):
        mean_row = ext_row(means, fbufs, HR, r).astype(BF16)
        logs = jnp.log(1.0 + numbers_row(numbers, nbufs, r))
        embedded = jnp.dot(mean_row, embed[...], preferred_element_type=F32) + jnp.concatenate(
            [logs, logs], axis=1
        ) * density[...]
        put3(x0, slice(r, r + 1), embedded.astype(BF16).astype(F32))

    n = 11

    def fwd0(c, carry):
        pre = conv_fwd(x0, weight, 0, c * n, n)
        value, slope = gelu_parts(pre)
        old = x0[pl.ds(c * n + 1, n), :, CH : 2 * CH].reshape(n * W, CH).astype(F32)
        new = jnp.where(row_mask(a * TR - 3 + c * n, n), old + value, 0.0)
        new = new.astype(BF16).astype(F32)
        put3(x1, pl.ds(c * n, n), new)
        slope0[pl.ds(c * n, n)] = slope.reshape(n, W, CH)
        return carry

    lax.fori_loop(0, 2, fwd0, 0)
    waits(cot_halo)
    for r in range(TR + 2 * HC):
        cot_ext[r] = ext_row(cot, cbufs, HC, r)
    m = 10

    def fwd1(c, carry):
        pre = conv_fwd(x1, weight, 1, c * m, m)
        value, slope = gelu_parts(pre)
        old = x1[pl.ds(c * m + 1, m), :, CH : 2 * CH].reshape(m * W, CH).astype(F32)
        grid2[pl.ds(c * m, m)] = (old + value).astype(BF16).reshape(m, W, CH)
        grad = cot_ext[pl.ds(c * m, m)].reshape(m * W, CH) * slope
        put3(g1, pl.ds(c * m, m), grad.astype(BF16).astype(F32))
        return carry

    lax.fori_loop(0, 2, fwd1, 0)

    grad1 = g1[2 : 2 + TR, SIDE : SIDE + TC, CH : 2 * CH].reshape(CELLS, CH)
    kernel_grad(x1, 2, grad1, grads, 288, (1, 2))
    w1.pair_start()
    k = 9

    def bwd1(c, carry):
        up = conv_bwd(g1, weight, 1, c * k, k) + cot_ext[pl.ds(c * k + 1, k)].reshape(k * W, CH)
        up1[pl.ds(c * k, k)] = up.reshape(k, W, CH)
        grad = up * slope0[pl.ds(c * k + 2, k)].reshape(k * W, CH)
        grad = jnp.where(row_mask(a * TR - 1 + c * k, k), grad, 0.0)
        put3(g0, pl.ds(c * k, k), grad.astype(BF16).astype(F32))
        return carry

    lax.fori_loop(0, 2, bwd1, 0)
    w1.rs1_start()
    kernel_grad(x1, 2, grad1, grads, 288, (0,))
    kernel_grad(x0, 3, g0[1 : 1 + TR, SIDE : SIDE + TC, CH : 2 * CH].reshape(CELLS, CH), grads, 0, (0, 1, 2))
    w2.pair_start()
    j = 8

    def bwd0(c, carry):
        up = conv_bwd(g0, weight, 0, c * j, j) + up1[pl.ds(c * j + 1, j)].reshape(j * W, CH)
        top[pl.ds(c * j, j)] = up.reshape(j, W, CH)[:, SIDE : SIDE + TC].astype(BF16)
        return carry

    lax.fori_loop(0, 2, bwd0, 0)
    w2.rs1_start()
    top_grad = top[...].reshape(CELLS, CH)
    mean_rows = means[...].reshape(CELLS, F)
    store_units(
        grads,
        EMBED0,
        lax.dot_general(mean_rows, top_grad, (((0,), (0,)), ((), ())), preferred_element_type=F32),
    )
    es.pair_start()
    mean_grad = lax.dot_general(
        top_grad, embed[...], (((1,), (1,)), ((), ())), preferred_element_type=F32
    )
    scaled = (mean_grad / jnp.maximum(numbers[...], 1.0)).astype(BF16)
    picked[...] = jnp.dot(onehot[...], scaled, preferred_element_type=F32).astype(BF16).reshape(NT, CAP, F)
    out_ref[...] = grid2[2 : 2 + TR, SIDE : SIDE + TC, :]
    w1.rs2_start()
    es.rs_start()
    w2.rs2_start()
    exchange_start(picked, back, back_send, back_recv)
    w1.ag2_start()
    es.sum_start()
    w2.ag2_start()
    w1.ag1_start()
    es.ag_start()
    w2.ag1_start()
    w1.pair2_start()
    es.pair2_start()
    w2.pair2_start()
    for lat in range(NA):
        exchange_wait_recv(back, back_recv, lat)
    exchange_wait_send(values, a2a_send)
    exchange_wait_send(picked, back_send)
    wait_bytes(tables.at[pl.ds(0, NB - 1)], code_sem.at[0])
    wait_bytes(codes_got.at[pl.ds(0, NA - 1)], code_sem.at[2])
    w1.finish()
    w2.finish()
    es.finish()


def write_kernel(total, field, back, conv_out, embed_out, field_out, back_out, wide, sem):
    copies = [
        pltpu.make_async_copy(field, field_out, sem.at[0]),
        pltpu.make_async_copy(back, back_out, sem.at[1]),
    ]
    for copy in copies:
        copy.start()
    bounds = [64 * i for i in range(10)] + [UNITS]
    for i, (u0, u1) in enumerate(zip(bounds, bounds[1:])):
        rows = pl.ds(u0 * 8, (u1 - u0) * 8)
        for h in range(2):
            part = total[u0:u1, h].astype(F32).reshape((u1 - u0) * 8, 128)
            wide[rows, h * 128 : (h + 1) * 128] = part
        dst = embed_out if u0 == EMBED0 else conv_out.at[rows]
        copy = pltpu.make_async_copy(wide.at[rows], dst, sem.at[2 + i])
        copy.start()
        copies.append(copy)
    for copy in copies:
        copy.wait()


VM = pl.BlockSpec(memory_space=pltpu.VMEM)
ANY = pl.BlockSpec(memory_space=pl.ANY)
DMA = pltpu.SemaphoreType.DMA


def vmem(shape, dtype=BF16):
    return pltpu.VMEM(shape, dtype)


def halo_shapes(rows, width):
    wide, side, corner = (rows, TC, width), (TR, STRIP, width), (rows, STRIP, width)
    return [vmem(s) for s in (wide, wide, side, side, corner, corner, corner, corner)]


def wave_shapes(w):
    per = WAVES[w][1]
    units = 192 * per
    return [
        vmem((units, 8, 128)), vmem((units, 8, 128)), vmem((3, 3, 16 * per, 8, 128)),
        vmem((3, 16 * per, 8, 128)), vmem((3, 15, per, 8, 128)),
    ]


def body(obs_values, obs_cells, obs_counts, embed_weight, density_row, conv_weight, grid_cotangent):
    weight = conv_weight.reshape(2, 3, 3 * CH, CH)
    args = (obs_values[0], obs_cells[0].T, obs_counts, embed_weight, density_row.reshape(1, CH), weight, grid_cotangent)
    field, total, back = pl.pallas_call(
        kernel,
        out_shape=[
            jax.ShapeDtypeStruct((TR, TC, CH), BF16),
            jax.ShapeDtypeStruct((UNITS, 2, 8, 128), BF16),
            jax.ShapeDtypeStruct((NT, CAP, F), BF16),
        ],
        in_specs=[ANY] * 7,
        out_specs=[VM] * 3,
        scratch_shapes=[
            vmem((NT, CAP, F)), vmem((CAP, NT), jnp.int32), vmem((1, NT), jnp.int32), vmem((F, CH)),
            vmem((1, CH), F32), vmem((2, 3, 3 * CH, CH)), vmem((TR, TC, CH)),
            vmem((2, CAP, NT)), vmem((NB, 2, CAP, NT)), vmem((NA, 1, NT), F32), vmem((NA, 1, NT), F32),
            vmem((NT, CAP, F)), vmem((SLOTS, CELLS)), vmem((TR, TC, F)), vmem((CELLS, F), F32),
            vmem((8, 128), F32), vmem((8, 8, 128), F32),
            *[vmem((PACKED[da][1] * 128, 128), F32) for da, _ in DIRS],
            *halo_shapes(HR, F), *halo_shapes(HC, CH),
            vmem((24, W, 3 * CH)), vmem((22, W, 3 * CH)), vmem((20, W, 3 * CH)), vmem((18, W, 3 * CH)),
            vmem((22, W, CH), F32), vmem((20, W, CH), F32), vmem((18, W, CH), F32),
            vmem((20, W, CH)), vmem((TR, TC, CH)), vmem((UNITS, 2, 8, 128)), vmem((NT, CAP, F)),
            *wave_shapes(0), *wave_shapes(1),
            vmem((16, 8, 128)), vmem((16, 8, 128)), vmem((15, 1, 8, 128)), vmem((1, 8, 128)), vmem((3, 1, 8, 128)),
            DMA((7,)), DMA, DMA((NA,)), DMA, DMA((NA,)), DMA((4,)), DMA((8,)), DMA((8,)), DMA((8,)), DMA((8,)), DMA((8,)), DMA((8,)),
            DMA((2,)), DMA((3, 5, 2)), DMA((2,)), DMA((3, 5, 2)), DMA((5, 2)),
        ],
        compiler_params=pltpu.CompilerParams(
            collective_id=0, has_side_effects=True, vmem_limit_bytes=40 * 2**20
        ),
    )(*[pltpu.with_memory_space_constraint(arg, pltpu.HBM) for arg in args])
    grad_conv, grad_embed, field, back = pl.pallas_call(
        write_kernel,
        out_shape=[
            jax.ShapeDtypeStruct((EMBED0 * 8, CH), F32),
            jax.ShapeDtypeStruct((F, CH), F32),
            jax.ShapeDtypeStruct(field.shape, BF16),
            jax.ShapeDtypeStruct(back.shape, BF16),
        ],
        in_specs=[VM] * 3,
        out_specs=[ANY] * 4,
        scratch_shapes=[vmem((UNITS * 8, CH), F32), DMA((12,))],
        compiler_params=pltpu.CompilerParams(vmem_limit_bytes=20 * 2**20),
    )(total, field, back)
    return field, grad_conv.reshape(2, 3, 3, CH, CH), grad_embed, back[None]


def solution(mesh):
    return jax.shard_map(
        body,
        mesh=mesh,
        in_specs=(
            P(("lat", "lon"), None, None, None),
            P(("lat", "lon"), None, None),
            P(("lat", "lon"), None),
            P(),
            P(),
            P(),
            P("lat", "lon", None),
        ),
        out_specs=(P("lat", "lon", None), P(), P(), P(("lat", "lon"), None, None, None)),
        check_vma=False,
    )
```

```python
import functools

import jax
import jax.numpy as jnp
from jax import lax
from jax.experimental import pallas as pl
from jax.experimental.pallas import tpu as pltpu
from jax.sharding import PartitionSpec as P

MESH = pl.DeviceIdType.MESH
NA, NB = 8, 16
NT = NA * NB
TR, TC = 16, 48
CELLS = TR * TC
CH, F, CAP = 256, 128, 8
SLOTS = NT * CAP
HR = 4
HC = 2
SIDE = 8
W = TC + 2 * SIDE
POOL = 1536
UNITS = 592
F32, BF16 = jnp.float32, jnp.bfloat16
GC, GA = 0.7978845608028654, 0.044715


def coords():
    return lax.axis_index("lat"), lax.axis_index("lon")


def tile_dev(t):
    return (t // NB, lax.rem(t, NB))


FAR_Z = (2, 1, 3, 0)


def all_others(fn, planes=FAR_Z):
    a, b = coords()
    z, hi = a // 2, lax.rem(a, 2)
    for dz in planes:
        for dh in (1, 0):
            lat = lax.rem(z + dz, 4) * 2 + lax.rem(hi + dh, 2)

            def step(k, carry, lat=lat):
                fn(lat, lax.rem(b + k, NB))
                return carry

            lax.fori_loop(0 if dz or dh else 1, NB, step, 0)


def barrier_signal():
    sem = pltpu.get_barrier_semaphore()
    all_others(lambda lat, lon: pl.semaphore_signal(sem, inc=1, device_id=(lat, lon), device_id_type=MESH))


def barrier_wait():
    pl.semaphore_wait(pltpu.get_barrier_semaphore(), NT - 1)


def exchange_own(src, dst, recv):
    a, b = coords()
    me = a * NB + b
    pltpu.make_async_copy(src.at[me], dst.at[me], recv).start()


def exchange_start(src, dst, send, recv, planes):
    a, b = coords()
    me = a * NB + b

    def go(lat, lon):
        pltpu.make_async_remote_copy(
            src_ref=src.at[lat * NB + lon],
            dst_ref=dst.at[me],
            send_sem=send,
            recv_sem=recv,
            device_id=(lat, lon),
            device_id_type=MESH,
        ).start()

    all_others(go, planes)


def exchange_wait_send(src, send):
    part = src.at[pl.ds(0, NT - 1)]
    pltpu.make_async_copy(part, part, send).wait()


DIRS = [(-1, 0), (1, 0), (0, -1), (0, 1), (-1, -1), (-1, 1), (1, -1), (1, 1)]


def make_strips(src, strips):
    strips[0] = src[:, 0:SIDE, :]
    strips[1] = src[:, TC - SIDE : TC, :]


def make_pairs(src, pairs):
    for side, at in ((0, 0), (1, TC - 8)):
        cut = slice(0, HC) if side == 0 else slice(8 - HC, 8)
        for i in range(TR // 4):
            parts = [src[4 * i + j, at : at + 8].astype(F32)[cut] for j in range(4)]
            pairs[side, i] = jnp.concatenate(parts, axis=0).astype(BF16)


def pairs_start(src, pairs, bufs, send, recv):
    for da, db in DIRS:
        back = DIRS.index((-da, -db))
        if db == 0:
            part = src.at[pl.ds(0, HC) if da < 0 else pl.ds(TR - HC, HC)]
        else:
            blocks = {-1: pl.ds(0, 1), 0: pl.ds(0, TR // 4), 1: pl.ds(TR // 4 - 1, 1)}[da]
            part = pairs.at[(db + 1) // 2, blocks]
        pltpu.make_async_remote_copy(
            src_ref=part, dst_ref=bufs[back], send_sem=send, recv_sem=recv,
            device_id=neighbour(da, db), device_id_type=MESH,
        ).start()


PAIR_UNITS = (2 * HC * TC + 2 * TR * 2 + 4 * 8) * CH // 1024


def pairs_row(core, bufs, r):
    if r < HC:
        left, mid, right = bufs[4][0], bufs[0][r], bufs[5][0]
        at = 8 - 2 * HC + HC * r
    elif r < HC + TR:
        k = r - HC
        left, mid, right = bufs[2][k // 4], core[k], bufs[3][k // 4]
        at = HC * (k % 4)
    else:
        k = r - HC - TR
        left, mid, right = bufs[6][0], bufs[1][k], bufs[7][0]
        at = HC * k
    zero = jnp.zeros((SIDE - HC, CH), F32)
    return jnp.concatenate(
        [zero, left.astype(F32)[at : at + HC], mid.astype(F32), right.astype(F32)[at : at + HC], zero], axis=0
    )


def neighbour(da, db):
    a, b = coords()
    return (lax.rem(a + da + NA, NA), lax.rem(b + db + NB, NB))


def halo_start(src, strips, bufs, rows, send, recv):
    for da, db in DIRS:
        back = DIRS.index((-da, -db))
        row = {-1: pl.ds(0, rows), 0: pl.ds(0, TR), 1: pl.ds(TR - rows, rows)}[da]
        whole = src if db == 0 else strips.at[(db + 1) // 2]
        pltpu.make_async_remote_copy(
            src_ref=whole.at[row], dst_ref=bufs[back], send_sem=send, recv_sem=recv,
            device_id=neighbour(da, db), device_id_type=MESH,
        ).start()


def halo_units(rows, width):
    return (2 * rows * TC + 2 * TR * SIDE + 4 * rows * SIDE) * width // 1024


def halo_zero(bufs):
    a, _ = coords()
    for end, at in ((0, -1), (NA - 1, 1)):

        def clear(at=at):
            for i, (da, _) in enumerate(DIRS):
                if da == at:
                    bufs[i][...] = jnp.zeros(bufs[i].shape, bufs[i].dtype)

        pl.when(a == end)(clear)


def ext_row(core, bufs, rows, r):
    if r < rows:
        left, mid, right, k = bufs[4], bufs[0], bufs[5], r
    elif r < rows + TR:
        left, mid, right, k = bufs[2], core, bufs[3], r - rows
    else:
        left, mid, right, k = bufs[6], bufs[1], bufs[7], r - rows - TR
    return jnp.concatenate(
        [
            left[k].astype(F32),
            mid[k].astype(F32),
            right[k].astype(F32),
        ],
        axis=0,
    )


def put3(dst, rows, value):
    n = value.shape[0] // W
    for q, shift in ((0, 1), (1, 0), (2, value.shape[0] - 1)):
        moved = value if shift == 0 else pltpu.roll(value, shift, 0)
        dst[rows, :, q * CH : (q + 1) * CH] = moved.astype(BF16).reshape(n, W, CH)


def row_mask(first, n):
    rows = lax.broadcasted_iota(jnp.int32, (n * W, CH), 0) // W + first
    return (rows >= 0) & (rows < NA * TR)


def gelu_parts(x):
    x2 = x * x
    t = jnp.tanh(GC * x * (1.0 + GA * x2))
    half = 0.5 * (1.0 + t)
    value = x * half
    slope = half + 0.5 * x * (1.0 - t * t) * (GC * (1.0 + 3.0 * GA * x2))
    return value, slope


def conv_fwd(src, weight, layer, start, n):
    acc = None
    for p in range(3):
        window = src[pl.ds(start + p, n)].reshape(n * W, 3 * CH)
        part = jnp.dot(window, weight[layer, p], preferred_element_type=F32)
        acc = part if acc is None else acc + part
    return acc


def conv_bwd(src, weight, layer, start, n):
    acc = None
    for p in range(3):
        for q in range(3):
            lanes = slice((2 - q) * CH, (3 - q) * CH)
            window = src[pl.ds(start + 2 - p, n), :, lanes].reshape(n * W, CH)
            part = lax.dot_general(
                window,
                weight[layer, p, q * CH : (q + 1) * CH],
                (((1,), (1,)), ((), ())),
                preferred_element_type=F32,
            )
            acc = part if acc is None else acc + part
    return acc


def store_units(dst, first, value):
    n = value.shape[0] // 8
    for h in range(2):
        dst[first : first + n, h] = value[:, h * 128 : (h + 1) * 128].astype(BF16).reshape(n, 8, 128)


def kernel_grad(src, first, grad, dst, unit, taps_of):
    for p in taps_of:
        window = src[first + p : first + p + TR, SIDE : SIDE + TC, :].reshape(CELLS, 3 * CH)
        taps = lax.dot_general(
            window, grad, (((0,), (0,)), ((), ())), preferred_element_type=F32
        )
        store_units(dst, unit + p * 96, taps)


ORDERS = (("x", "y", "z"), ("y", "z", "x"), ("z", "x", "y"))
WAVES = ((384, 1), (0, 2))
EMBED0, EMBED_UNITS = 576, 16


def place():
    a, b = coords()
    return {"z": a // 2, "x": lax.rem(a, 2) * 2 + b // 8, "y": lax.rem(b // 2, 4), "c": lax.rem(b, 2)}


def device_at(pos):
    x = pos["x"]
    return (pos["z"] * 2 + x // 2, lax.rem(x, 2) * 8 + pos["y"] * 2 + pos["c"])


def along(pos, axis, step):
    moved = dict(pos)
    moved[axis] = lax.rem(pos[axis] + step, 4)
    return moved


def other_core(pos):
    moved = dict(pos)
    moved["c"] = 1 - pos["c"]
    return moved


def remote(src, dst, send, recv, pos):
    pltpu.make_async_remote_copy(
        src_ref=src, dst_ref=dst, send_sem=send, recv_sem=recv,
        device_id=device_at(pos), device_id_type=MESH,
    ).start()


def wait_bytes(ref, sem):
    pltpu.make_async_copy(ref, ref, sem).wait()


def add_parts(own, got, count):
    total = own.astype(F32)
    for i in range(count):
        total = total + got[i].astype(F32)
    return total.astype(BF16)


def on_plane(pos, axes, fn):
    def step(k, carry):
        peer = along(along(pos, axes[0], k // 4), axes[1], lax.rem(k, 4))
        fn(peer, k - 1)
        return carry

    lax.fori_loop(1, 16, step, 0)


class Wave:
    def __init__(self, w, pos, grads, total, bufs, sem, pool):
        self.first, self.per = WAVES[w]
        self.pos, self.grads, self.total, self.pool = pos, grads, total, pool
        self.pair, self.own, self.r1, self.t1, self.r2, self.t2 = bufs
        self.stream = 64 * self.per
        self.send, self.pair_got, self.back_got = sem.at[0], sem.at[1], sem.at[2]
        self.got1 = [sem.at[3 + s] for s in range(3)]
        self.got2 = [sem.at[6 + s] for s in range(3)]
        self.got3 = [sem.at[9 + s] for s in range(3)]
        self.got4 = {step: sem.at[11 + step] for step in (1, 2, 3)}

    def wait(self, units, sem):
        wait_bytes(self.pool.at[pl.ds(0, units * self.per)], sem)

    def pair_start(self):
        mine = self.grads.at[pl.ds(self.first, 3 * self.stream), 1 - self.pos["c"]]
        remote(mine, self.pair, self.send, self.pair_got, other_core(self.pos))

    def rs1_start(self):
        pos, part = self.pos, 16 * self.per
        wait_bytes(self.pair, self.pair_got)
        kept = self.grads[pl.ds(self.first, 3 * self.stream), pos["c"]]
        self.own[...] = (kept.astype(F32) + self.pair[...].astype(F32)).astype(BF16)
        for step in (2, 1, 3):
            for s, order in enumerate(ORDERS):
                peer = along(pos, order[0], step)
                src = self.own.at[pl.ds(s * self.stream + peer[order[0]] * part, part)]
                remote(src, self.r1.at[s, step - 1], self.send, self.got1[s], peer)

    def rs2_start(self):
        pos, part, per = self.pos, 16 * self.per, self.per
        for s, order in enumerate(ORDERS):
            wait_bytes(self.r1.at[s], self.got1[s])
            kept = self.own[pl.ds(s * self.stream + pos[order[0]] * part, part)]
            self.t1[s] = add_parts(kept, self.r1.at[s], 3)

            def go(peer, k, s=s, order=order):
                src = self.t1.at[s, pl.ds((peer[order[1]] * 4 + peer[order[2]]) * per, per)]
                remote(src, self.r2.at[s, k], self.send, self.got2[s], peer)

            on_plane(pos, order[1:], go)

    def block(self, s, order):
        pos, per = self.pos, self.per
        start = self.first + s * self.stream + pos[order[0]] * 16 * per
        return start, (pos[order[1]] * 4 + pos[order[2]]) * per

    def ag2_start(self):
        pos, per, c = self.pos, self.per, self.pos["c"]
        for s, order in enumerate(ORDERS):
            wait_bytes(self.r2.at[s], self.got2[s])
            start, inner = self.block(s, order)
            self.t2[s] = add_parts(self.t1[s, pl.ds(inner, per)], self.r2.at[s], 15)
            block = self.total.at[pl.ds(start + inner, per), c]
            pltpu.make_async_copy(self.t2.at[s], block, self.got3[s]).start()

            def go(peer, k, s=s, block=block):
                remote(self.t2.at[s], block, self.send, self.got3[s], peer)

            on_plane(pos, order[1:], go)

    def ag1_start(self):
        pos, per, c = self.pos, self.per, self.pos["c"]
        for s, order in enumerate(ORDERS):
            self.wait(16, self.got3[s])
            start, _ = self.block(s, order)
            block = self.total.at[pl.ds(start, 16 * per), c]
            for step in (2, 1, 3):
                remote(block, block, self.send, self.got4[step], along(pos, order[0], step))
            remote(block, block, self.send, self.back_got, other_core(pos))

    def pair2_start(self):
        pos, part, c = self.pos, 16 * self.per, self.pos["c"]
        for step in (1, 3, 2):
            self.wait(48, self.got4[step])
            for s, order in enumerate(ORDERS):
                came = lax.rem(pos[order[0]] + 4 - step, 4)
                block = self.total.at[pl.ds(self.first + s * self.stream + came * part, part), c]
                remote(block, block, self.send, self.back_got, other_core(pos))

    def finish(self):
        self.wait(192 + 3 * (48 + 15 + 15 + 48 + 16 + 48), self.send)
        self.wait(192, self.back_got)


class EmbedSum:
    def __init__(self, pos, grads, total, bufs, sem, pool):
        self.pos, self.grads, self.total, self.pool = pos, grads, total, pool
        self.pair, self.own, self.r1, self.t1, self.r2, self.t2 = bufs
        self.send, self.got = sem.at[0], [sem.at[1 + i] for i in range(5)]

    def pair_start(self):
        src = self.grads.at[pl.ds(EMBED0, EMBED_UNITS), 1 - self.pos["c"]]
        remote(src, self.pair, self.send, self.got[0], other_core(self.pos))

    def rs_start(self):
        pos = self.pos
        wait_bytes(self.pair, self.got[0])
        kept = self.grads[pl.ds(EMBED0, EMBED_UNITS), pos["c"]]
        self.own[...] = (kept.astype(F32) + self.pair[...].astype(F32)).astype(BF16)

        def go(peer, k):
            src = self.own.at[pl.ds(peer["y"] * 4 + peer["z"], 1)]
            remote(src, self.r1.at[k], self.send, self.got[1], peer)

        on_plane(pos, ("y", "z"), go)

    def sum_start(self):
        pos = self.pos
        wait_bytes(self.r1, self.got[1])
        self.t1[...] = add_parts(self.own[pl.ds(pos["y"] * 4 + pos["z"], 1)], self.r1, 15)
        for step in range(1, 4):
            remote(self.t1, self.r2.at[step - 1], self.send, self.got[2], along(pos, "x", step))

    def ag_start(self):
        pos, c = self.pos, self.pos["c"]
        wait_bytes(self.r2, self.got[2])
        at = EMBED0 + pos["y"] * 4 + pos["z"]
        parts = []
        for i in range(4):
            got = self.t1[...].astype(F32)
            for step in range(1, 4):
                got = jnp.where(lax.rem(pos["x"] - step + 4, 4) == i, self.r2[step - 1].astype(F32), got)
            parts.append(got)
        self.t2[...] = (((parts[0] + parts[1]) + parts[2]) + parts[3]).astype(BF16)
        block = self.total.at[pl.ds(at, 1), c]
        pltpu.make_async_copy(self.t2, block, self.got[3]).start()
        on_plane(pos, ("y", "z"), lambda peer, k: remote(self.t2, block, self.send, self.got[3], peer))

    def pair2_start(self):
        c = self.pos["c"]
        wait_bytes(self.pool.at[pl.ds(0, 16)], self.got[3])
        block = self.total.at[pl.ds(EMBED0, EMBED_UNITS), c]
        remote(block, block, self.send, self.got[4], other_core(self.pos))

    def finish(self):
        wait_bytes(self.pool.at[pl.ds(0, 16 + 15 + 3 + 15 + 16)], self.send)
        wait_bytes(self.pool.at[pl.ds(0, 16)], self.got[4])


def make_table(table, cells, counts):
    slot = lax.broadcasted_iota(jnp.int32, (CAP, NT), 0)
    cell = cells[...]
    row = (cell * 1366) >> 16
    table[0] = jnp.where(slot < counts[...], row, -100).astype(F32).astype(BF16)
    table[1] = (cell - row * TC).astype(F32).astype(BF16)


def to_group(fn, count):
    def step(k, carry):
        fn(k)
        return carry

    lax.fori_loop(1, count, step, 0)


def codes_start(table, tables, sem):
    a, b = coords()
    pltpu.make_async_copy(table, tables.at[b], sem.at[1]).start()

    def go(k):
        pltpu.make_async_remote_copy(
            src_ref=table, dst_ref=tables.at[b], send_sem=sem.at[0], recv_sem=sem.at[1],
            device_id=(a, lax.rem(b + k, NB)), device_id_type=MESH,
        ).start()

    to_group(go, NB)


def codes_forward(tables, mine, got, sem):
    a, b = coords()
    wait_bytes(tables, sem.at[1])
    lat = lax.broadcasted_iota(jnp.int32, (NA, NT), 0)
    tile = lax.broadcasted_iota(jnp.int32, (NA, NT), 1)
    pick = jnp.where(tile == lat * NB + b, 1.0, 0.0).astype(BF16)
    nt = (((1,), (1,)), ((), ()))
    rows = lax.dot_general(pick, tables[:, 0].reshape(NB * CAP, NT), nt, preferred_element_type=F32)
    cols = lax.dot_general(pick, tables[:, 1].reshape(NB * CAP, NT), nt, preferred_element_type=F32)
    codes = rows * TC + cols
    for i in range(NA):
        mine[i] = codes[i : i + 1]
    pltpu.make_async_copy(mine.at[a], got.at[a], sem.at[3]).start()

    def go(k):
        to = lax.rem(a + k, NA)
        pltpu.make_async_remote_copy(
            src_ref=mine.at[to], dst_ref=got.at[a], send_sem=sem.at[2], recv_sem=sem.at[3],
            device_id=(to, b), device_id_type=MESH,
        ).start()

    to_group(go, NA)


def place_codes(got, onehot, sem):
    wait_bytes(got, sem.at[3])
    rows = [got[i] for i in range(NA)] + [jnp.zeros((NT - NA, NT), F32)]
    codes = jnp.concatenate(rows, axis=0).T
    lane = lax.broadcasted_iota(jnp.int32, (NB * CAP, CELLS), 1).astype(F32)
    for i in range(NA):
        hit = codes[:, i : i + 1] == lane
        onehot[i * NB * CAP : (i + 1) * NB * CAP, :] = jnp.where(hit, 1.0, 0.0).astype(BF16)


def eye(dtype=None):
    return lax.broadcasted_iota(jnp.int32, (128, 128), 0) == lax.broadcasted_iota(jnp.int32, (128, 128), 1)


def pack_numbers(numbers, packed):
    mask = eye()
    for i in range(CELLS // 128):
        packed[i : i + 1] = jnp.where(mask, numbers[i * 128 : (i + 1) * 128], 0.0).sum(axis=0, keepdims=True)


def unpack_numbers(packed, first, count, out):
    mask = eye()
    ones = jnp.ones((256, 128), BF16)
    for i in range(count):
        row = packed[first + i : first + i + 1]
        high = jnp.floor(row * 0.125) * 8.0
        parts = [jnp.where(mask, jnp.broadcast_to(v, (128, 128)), 0.0).astype(BF16) for v in (high, row - high)]
        out[i * 128 : (i + 1) * 128] = jnp.dot(
            jnp.concatenate(parts, axis=1), ones, preferred_element_type=F32
        )


PACKED = {-1: (4, 2), 0: (0, 6), 1: (0, 2)}


def numbers_row(own, bufs, r):
    if r < HR:
        left, mid, right, at = bufs[4], bufs[0], bufs[5], (TR - HR + r) * TC - 512
    elif r < HR + TR:
        left, mid, right, at = bufs[2], own, bufs[3], (r - HR) * TC
    else:
        left, mid, right, at = bufs[6], bufs[1], bufs[7], (r - HR - TR) * TC
    return jnp.concatenate(
        [left[at + TC - SIDE : at + TC], mid[at : at + TC], right[at : at + SIDE]], axis=0
    )


def packed_start(packed, bufs, send, recv):
    for da, db in DIRS:
        pltpu.make_async_remote_copy(
            src_ref=packed, dst_ref=bufs.at[DIRS.index((-da, -db))], send_sem=send, recv_sem=recv,
            device_id=neighbour(da, db), device_id_type=MESH,
        ).start()


def kernel(
    values_hbm, cells_hbm, counts_hbm, embed_hbm, density_hbm, weight_hbm, cot_hbm,
    out_ref, total, back,
    values, cells, counts, embed, density, weight, cot,
    table, tables, codes_mine, codes_got, recv, onehot, means, numbers, packed, packs, mean_strips, cot_strips,
    nN, nS, nW, nE, nNW, nNE, nSW, nSE,
    fN, fS, fW, fE, fNW, fNE, fSW, fSE,
    cN, cS, cW, cE, cNW, cNE, cSW, cSE,
    x0, x1, g1, g0, slope0, cot_ext, up1, grid_out, top, grads, picked,
    *rest,
):
    w1_bufs, w2_bufs, e_bufs = rest[0:6], rest[6:12], rest[12:18]
    (pool, load_sem, a2a_send, a2a_recv, back_send, back_recv, code_sem, halo_sem, pack_sem, cot_sem,
     w1_sem, w2_sem, e_sem) = rest[18:]
    a, _ = coords()
    pos = place()
    fbufs = (fN, fS, fW, fE, fNW, fNE, fSW, fSE)
    nbufs = (nN, nS, nW, nE, nNW, nNE, nSW, nSE)
    cbufs = (cN, cS, cW, cE, cNW, cNE, cSW, cSE)
    w1 = Wave(0, pos, grads, total, w1_bufs, w1_sem, pool)
    w2 = Wave(1, pos, grads, total, w2_bufs, w2_sem, pool)
    es = EmbedSum(pos, grads, total, e_bufs, e_sem, pool)
    barrier_signal()
    loads = [
        pltpu.make_async_copy(src, dst, load_sem.at[i])
        for i, (src, dst) in enumerate(
            (
                (cells_hbm, cells), (counts_hbm, counts), (values_hbm, values), (cot_hbm, cot),
                (embed_hbm, embed), (density_hbm, density), (weight_hbm, weight),
            )
        )
    ]
    for load in loads:
        load.start()
    packed[...] = jnp.zeros_like(packed)
    for load in loads[:4]:
        load.wait()
    make_pairs(cot, cot_strips)
    make_table(table, cells, counts)
    barrier_wait()
    codes_start(table, tables, code_sem)
    exchange_own(values, recv, a2a_recv)
    exchange_start(values, recv, a2a_send, a2a_recv, FAR_Z)
    codes_forward(tables, codes_mine, codes_got, code_sem)
    for load in loads[4:]:
        load.wait()
    place_codes(codes_got, onehot, code_sem)
    wait_bytes(recv, a2a_recv)
    both = jnp.concatenate([recv[...].reshape(SLOTS, F), jnp.ones((SLOTS, F), BF16)], axis=1)
    sums = lax.dot_general(
        onehot[...], both, (((0,), (0,)), ((), ())), preferred_element_type=F32
    )
    numbers[...] = sums[:, F:]
    means[...] = (sums[:, :F] / jnp.maximum(sums[:, F:], 1.0)).astype(BF16).reshape(TR, TC, F)
    pack_numbers(numbers, packed)
    make_strips(means, mean_strips)
    packed_start(packed, packs, pack_sem.at[0], pack_sem.at[1])
    halo_start(means, mean_strips, fbufs, HR, halo_sem.at[0], halo_sem.at[1])
    pairs_start(cot, cot_strips, cbufs, cot_sem.at[0], cot_sem.at[1])
    wait_bytes(packs, pack_sem.at[1])
    halo_zero([packs.at[i] for i in range(8)])
    for i, (da, db) in enumerate(DIRS):
        first, count = PACKED[da]
        unpack_numbers(packs.at[i], first, count, nbufs[i])
    wait_bytes(pool.at[pl.ds(0, halo_units(HR, F))], halo_sem.at[1])
    halo_zero(fbufs)
    for r in range(TR + 2 * HR):
        mean_row = ext_row(means, fbufs, HR, r).astype(BF16)
        logs = jnp.log(1.0 + numbers_row(numbers, nbufs, r))
        embedded = jnp.dot(mean_row, embed[...], preferred_element_type=F32) + jnp.concatenate(
            [logs, logs], axis=1
        ) * density[...]
        put3(x0, slice(r, r + 1), embedded.astype(BF16).astype(F32))

    n = 11

    def fwd0(c, carry):
        pre = conv_fwd(x0, weight, 0, c * n, n)
        value, slope = gelu_parts(pre)
        old = x0[pl.ds(c * n + 1, n), :, CH : 2 * CH].reshape(n * W, CH).astype(F32)
        new = jnp.where(row_mask(a * TR - 3 + c * n, n), old + value, 0.0)
        new = new.astype(BF16).astype(F32)
        put3(x1, pl.ds(c * n, n), new)
        slope0[pl.ds(c * n, n)] = slope.reshape(n, W, CH)
        return carry

    lax.fori_loop(0, 2, fwd0, 0, unroll=True)
    wait_bytes(pool.at[pl.ds(0, PAIR_UNITS)], cot_sem.at[1])
    halo_zero(cbufs)
    for r in range(TR + 2 * HC):
        cot_ext[r] = pairs_row(cot, cbufs, r)
    m = 10

    def fwd1(c, carry):
        pre = conv_fwd(x1, weight, 1, c * m, m)
        value, slope = gelu_parts(pre)
        old = x1[pl.ds(c * m + 1, m), :, CH : 2 * CH].reshape(m * W, CH).astype(F32)
        final = (old + value).reshape(m, W, CH)
        grid_out[8 * c : 8 * c + 8] = final[2 - 2 * c : 10 - 2 * c, SIDE : SIDE + TC].astype(BF16)
        grad = cot_ext[pl.ds(c * m, m)].reshape(m * W, CH) * slope
        put3(g1, pl.ds(c * m, m), grad.astype(BF16).astype(F32))
        return carry

    for c in range(2):
        fwd1(c, 0)
    field_copy = pltpu.make_async_copy(grid_out, out_ref, load_sem.at[7])
    field_copy.start()

    grad1 = g1[2 : 2 + TR, SIDE : SIDE + TC, CH : 2 * CH].reshape(CELLS, CH)
    kernel_grad(x1, 2, grad1, grads, 288, (1, 2))
    w1.pair_start()
    k = 9

    def bwd1(c, carry):
        up = conv_bwd(g1, weight, 1, c * k, k) + cot_ext[pl.ds(c * k + 1, k)].reshape(k * W, CH)
        up1[pl.ds(c * k, k)] = up.reshape(k, W, CH)
        grad = up * slope0[pl.ds(c * k + 2, k)].reshape(k * W, CH)
        grad = jnp.where(row_mask(a * TR - 1 + c * k, k), grad, 0.0)
        put3(g0, pl.ds(c * k, k), grad.astype(BF16).astype(F32))
        return carry

    lax.fori_loop(0, 2, bwd1, 0, unroll=True)
    w1.rs1_start()
    kernel_grad(x1, 2, grad1, grads, 288, (0,))
    kernel_grad(x0, 3, g0[1 : 1 + TR, SIDE : SIDE + TC, CH : 2 * CH].reshape(CELLS, CH), grads, 0, (0, 1, 2))
    w2.pair_start()
    j = 8

    def bwd0(c, carry):
        up = conv_bwd(g0, weight, 0, c * j, j) + up1[pl.ds(c * j + 1, j)].reshape(j * W, CH)
        top[pl.ds(c * j, j)] = up.reshape(j, W, CH)[:, SIDE : SIDE + TC].astype(BF16)
        return carry

    lax.fori_loop(0, 2, bwd0, 0, unroll=True)
    w2.rs1_start()
    top_grad = top[...].reshape(CELLS, CH)
    mean_rows = means[...].reshape(CELLS, F)
    store_units(
        grads,
        EMBED0,
        lax.dot_general(mean_rows, top_grad, (((0,), (0,)), ((), ())), preferred_element_type=F32),
    )
    es.pair_start()
    mean_grad = lax.dot_general(
        top_grad, embed[...], (((1,), (1,)), ((), ())), preferred_element_type=F32
    )
    scaled = (mean_grad / jnp.maximum(numbers[...], 1.0)).astype(BF16)
    picked[...] = jnp.dot(onehot[...], scaled, preferred_element_type=F32).astype(BF16).reshape(NT, CAP, F)
    w1.rs2_start()
    es.rs_start()
    w2.rs2_start()
    exchange_own(picked, back, back_recv)
    exchange_start(picked, back, back_send, back_recv, FAR_Z)
    w1.ag2_start()
    es.sum_start()
    w2.ag2_start()
    w1.ag1_start()
    es.ag_start()
    w2.ag1_start()
    w1.pair2_start()
    es.pair2_start()
    w2.pair2_start()
    field_copy.wait()
    wait_bytes(packs, pack_sem.at[0])
    wait_bytes(pool.at[pl.ds(0, halo_units(HR, F))], halo_sem.at[0])
    wait_bytes(pool.at[pl.ds(0, PAIR_UNITS)], cot_sem.at[0])
    wait_bytes(back, back_recv)
    exchange_wait_send(values, a2a_send)
    exchange_wait_send(picked, back_send)
    wait_bytes(tables.at[pl.ds(0, NB - 1)], code_sem.at[0])
    wait_bytes(codes_got.at[pl.ds(0, NA - 1)], code_sem.at[2])
    w1.finish()
    w2.finish()
    es.finish()


def write_kernel(total, field, back, conv_out, embed_out, field_out, back_out, wide, sem):
    copies = [
        pltpu.make_async_copy(field, field_out, sem.at[0]),
        pltpu.make_async_copy(back, back_out, sem.at[1]),
    ]
    for copy in copies:
        copy.start()
    bounds = [64 * i for i in range(10)] + [UNITS]
    for i, (u0, u1) in enumerate(zip(bounds, bounds[1:])):
        rows = pl.ds(u0 * 8, (u1 - u0) * 8)
        for h in range(2):
            part = total[u0:u1, h].astype(F32).reshape((u1 - u0) * 8, 128)
            wide[rows, h * 128 : (h + 1) * 128] = part
        dst = embed_out if u0 == EMBED0 else conv_out.at[rows]
        copy = pltpu.make_async_copy(wide.at[rows], dst, sem.at[2 + i])
        copy.start()
        copies.append(copy)
    for copy in copies:
        copy.wait()


VM = pl.BlockSpec(memory_space=pltpu.VMEM)
ANY = pl.BlockSpec(memory_space=pl.ANY)
DMA = pltpu.SemaphoreType.DMA


def vmem(shape, dtype=BF16):
    return pltpu.VMEM(shape, dtype)


def halo_shapes(rows, width):
    wide, side, corner = (rows, TC, width), (TR, SIDE, width), (rows, SIDE, width)
    return [vmem(s) for s in (wide, wide, side, side, corner, corner, corner, corner)]


def pair_shapes():
    wide, side, corner = (HC, TC, CH), (TR // 4, 8, CH), (1, 8, CH)
    return [vmem(s) for s in (wide, wide, side, side, corner, corner, corner, corner)]


def wave_shapes(w):
    per = WAVES[w][1]
    units = 192 * per
    return [
        vmem((units, 8, 128)), vmem((units, 8, 128)), vmem((3, 3, 16 * per, 8, 128)),
        vmem((3, 16 * per, 8, 128)), vmem((3, 15, per, 8, 128)), vmem((3, per, 8, 128)),
    ]


def body(obs_values, obs_cells, obs_counts, embed_weight, density_row, conv_weight, grid_cotangent):
    weight = conv_weight.reshape(2, 3, 3 * CH, CH)
    args = (obs_values[0], obs_cells[0].T, obs_counts, embed_weight, density_row.reshape(1, CH), weight, grid_cotangent)
    field, total, back = pl.pallas_call(
        kernel,
        out_shape=[
            jax.ShapeDtypeStruct((TR, TC, CH), BF16),
            jax.ShapeDtypeStruct((UNITS, 2, 8, 128), BF16),
            jax.ShapeDtypeStruct((NT, CAP, F), BF16),
        ],
        in_specs=[ANY] * 7,
        out_specs=[ANY] * 3,
        scratch_shapes=[
            vmem((NT, CAP, F)), vmem((CAP, NT), jnp.int32), vmem((1, NT), jnp.int32), vmem((F, CH)),
            vmem((1, CH), F32), vmem((2, 3, 3 * CH, CH)), vmem((TR, TC, CH)),
            vmem((2, CAP, NT)), vmem((NB, 2, CAP, NT)), vmem((NA, 1, NT), F32), vmem((NA, 1, NT), F32),
            vmem((NT, CAP, F)), vmem((SLOTS, CELLS)), vmem((TR, TC, F)), vmem((CELLS, F), F32),
            vmem((8, 128), F32), vmem((8, 8, 128), F32), vmem((2, TR, SIDE, F)), vmem((2, TR // 4, 8, CH)),
            *[vmem((PACKED[da][1] * 128, 128), F32) for da, _ in DIRS],
            *halo_shapes(HR, F), *pair_shapes(),
            vmem((24, W, 3 * CH)), vmem((22, W, 3 * CH)), vmem((20, W, 3 * CH)), vmem((18, W, 3 * CH)),
            vmem((22, W, CH), F32), vmem((20, W, CH), F32), vmem((18, W, CH), F32),
            vmem((TR, TC, CH)), vmem((TR, TC, CH)), vmem((UNITS, 2, 8, 128)), vmem((NT, CAP, F)),
            *wave_shapes(0), *wave_shapes(1),
            vmem((16, 8, 128)), vmem((16, 8, 128)), vmem((15, 1, 8, 128)), vmem((1, 8, 128)), vmem((3, 1, 8, 128)),
            vmem((1, 8, 128)),
            vmem((POOL, 8, 128)), DMA((8,)), DMA, DMA, DMA, DMA, DMA((4,)), DMA((2,)), DMA((2,)), DMA((2,)),
            DMA((15,)), DMA((15,)), DMA((6,)),
        ],
        compiler_params=pltpu.CompilerParams(
            collective_id=0, has_side_effects=True, vmem_limit_bytes=40 * 2**20
        ),
    )(*[pltpu.with_memory_space_constraint(arg, pltpu.HBM) for arg in args])
    grad_conv, grad_embed, field, back = pl.pallas_call(
        write_kernel,
        out_shape=[
            jax.ShapeDtypeStruct((EMBED0 * 8, CH), F32),
            jax.ShapeDtypeStruct((F, CH), F32),
            jax.ShapeDtypeStruct(field.shape, BF16),
            jax.ShapeDtypeStruct(back.shape, BF16),
        ],
        in_specs=[VM] * 3,
        out_specs=[ANY] * 4,
        scratch_shapes=[vmem((UNITS * 8, CH), F32), DMA((12,))],
        compiler_params=pltpu.CompilerParams(vmem_limit_bytes=20 * 2**20),
    )(total, field, back)
    return field, grad_conv.reshape(2, 3, 3, CH, CH), grad_embed, back[None]


def solution(mesh):
    return jax.shard_map(
        body,
        mesh=mesh,
        in_specs=(
            P(("lat", "lon"), None, None, None),
            P(("lat", "lon"), None, None),
            P(("lat", "lon"), None),
            P(),
            P(),
            P(),
            P("lat", "lon", None),
        ),
        out_specs=(P("lat", "lon", None), P(), P(), P(("lat", "lon"), None, None, None)),
        check_vma=False,
    )
```

```python
import functools

import jax
import jax.numpy as jnp
from jax import lax
from jax.experimental import pallas as pl
from jax.experimental.pallas import tpu as pltpu
from jax.sharding import PartitionSpec as P

MESH = pl.DeviceIdType.MESH
NA, NB = 8, 16
NT = NA * NB
TR, TC = 16, 48
CELLS = TR * TC
CH, F, CAP = 256, 128, 8
SLOTS = NT * CAP
HR = 4
HC = 2
SIDE = 8
W = TC + 2 * SIDE
POOL = 1536
UNITS = 592
F32, BF16 = jnp.float32, jnp.bfloat16
GC, GA = 0.7978845608028654, 0.044715


def coords():
    return lax.axis_index("lat"), lax.axis_index("lon")


def tile_dev(t):
    return (t // NB, lax.rem(t, NB))


FAR_Z = (2, 1, 3, 0)


def all_others(fn, planes=FAR_Z):
    a, b = coords()
    z, hi = a // 2, lax.rem(a, 2)
    for dz in planes:
        for dh in (1, 0):
            lat = lax.rem(z + dz, 4) * 2 + lax.rem(hi + dh, 2)

            def step(k, carry, lat=lat):
                fn(lat, lax.rem(b + k, NB))
                return carry

            lax.fori_loop(0 if dz or dh else 1, NB, step, 0)


def barrier_signal():
    sem = pltpu.get_barrier_semaphore()
    all_others(lambda lat, lon: pl.semaphore_signal(sem, inc=1, device_id=(lat, lon), device_id_type=MESH))


def barrier_wait():
    pl.semaphore_wait(pltpu.get_barrier_semaphore(), NT - 1)


def exchange_own(src, dst, recv):
    a, b = coords()
    me = a * NB + b
    pltpu.make_async_copy(src.at[me], dst.at[me], recv).start()


def exchange_start(src, dst, send, recv, planes):
    a, b = coords()
    me = a * NB + b

    def go(lat, lon):
        pltpu.make_async_remote_copy(
            src_ref=src.at[lat * NB + lon],
            dst_ref=dst.at[me],
            send_sem=send,
            recv_sem=recv,
            device_id=(lat, lon),
            device_id_type=MESH,
        ).start()

    all_others(go, planes)


def exchange_wait_send(src, send):
    part = src.at[pl.ds(0, NT - 1)]
    pltpu.make_async_copy(part, part, send).wait()


DIRS = [(-1, 0), (1, 0), (0, -1), (0, 1), (-1, -1), (-1, 1), (1, -1), (1, 1)]


def make_strips(src, strips):
    strips[0] = src[:, 0:SIDE, :]
    strips[1] = src[:, TC - SIDE : TC, :]


def make_pairs(src, pairs):
    for side, at in ((0, 0), (1, TC - 8)):
        cut = slice(0, HC) if side == 0 else slice(8 - HC, 8)
        for i in range(TR // 4):
            parts = [src[4 * i + j, at : at + 8].astype(F32)[cut] for j in range(4)]
            pairs[side, i] = jnp.concatenate(parts, axis=0).astype(BF16)


def pairs_start(src, pairs, bufs, send, recv):
    for da, db in DIRS:
        back = DIRS.index((-da, -db))
        if db == 0:
            part = src.at[pl.ds(0, HC) if da < 0 else pl.ds(TR - HC, HC)]
        else:
            blocks = {-1: pl.ds(0, 1), 0: pl.ds(0, TR // 4), 1: pl.ds(TR // 4 - 1, 1)}[da]
            part = pairs.at[(db + 1) // 2, blocks]
        pltpu.make_async_remote_copy(
            src_ref=part, dst_ref=bufs[back], send_sem=send, recv_sem=recv,
            device_id=neighbour(da, db), device_id_type=MESH,
        ).start()


PAIR_UNITS = (2 * HC * TC + 2 * TR * 2 + 4 * 8) * CH // 1024


def pairs_row(core, bufs, r):
    if r < HC:
        left, mid, right = bufs[4][0], bufs[0][r], bufs[5][0]
        at = 8 - 2 * HC + HC * r
    elif r < HC + TR:
        k = r - HC
        left, mid, right = bufs[2][k // 4], core[k], bufs[3][k // 4]
        at = HC * (k % 4)
    else:
        k = r - HC - TR
        left, mid, right = bufs[6][0], bufs[1][k], bufs[7][0]
        at = HC * k
    zero = jnp.zeros((SIDE - HC, CH), F32)
    return jnp.concatenate(
        [zero, left.astype(F32)[at : at + HC], mid.astype(F32), right.astype(F32)[at : at + HC], zero], axis=0
    )


def neighbour(da, db):
    a, b = coords()
    return (lax.rem(a + da + NA, NA), lax.rem(b + db + NB, NB))


SIDES, ENDS, REST = DIRS[2:4], DIRS[0:2], DIRS[0:2] + DIRS[4:]


def halo_start(src, strips, bufs, rows, send, recv, dirs):
    for da, db in dirs:
        back = DIRS.index((-da, -db))
        row = {-1: pl.ds(0, rows), 0: pl.ds(0, TR), 1: pl.ds(TR - rows, rows)}[da]
        whole = src if db == 0 else strips.at[(db + 1) // 2]
        pltpu.make_async_remote_copy(
            src_ref=whole.at[row], dst_ref=bufs[back], send_sem=send, recv_sem=recv,
            device_id=neighbour(da, db), device_id_type=MESH,
        ).start()


def corners_start(bufs, packs, sems, pack_sems):
    for da, row in ((-1, 0), (1, TR - HR)):
        peer = neighbour(da, 0)
        for db, side in ((-1, 2), (1, 3)):
            corner = DIRS.index((-da, db))
            for src, dst, (send, recv) in (
                (bufs[side].at[pl.ds(row, HR)], bufs[corner], sems),
                (packs.at[side], packs.at[corner], pack_sems),
            ):
                pltpu.make_async_remote_copy(
                    src_ref=src, dst_ref=dst, send_sem=send, recv_sem=recv,
                    device_id=peer, device_id_type=MESH,
                ).start()


SIDE_UNITS = 2 * TR * SIDE * F // 1024
REST_UNITS = (2 * HR * TC + 4 * HR * SIDE) * F // 1024


def halo_zero(bufs):
    a, _ = coords()
    for end, at in ((0, -1), (NA - 1, 1)):

        def clear(at=at):
            for i, (da, _) in enumerate(DIRS):
                if da == at:
                    bufs[i][...] = jnp.zeros(bufs[i].shape, bufs[i].dtype)

        pl.when(a == end)(clear)


def ext_row(core, bufs, rows, r):
    if r < rows:
        left, mid, right, k = bufs[4], bufs[0], bufs[5], r
    elif r < rows + TR:
        left, mid, right, k = bufs[2], core, bufs[3], r - rows
    else:
        left, mid, right, k = bufs[6], bufs[1], bufs[7], r - rows - TR
    return jnp.concatenate(
        [
            left[k].astype(F32),
            mid[k].astype(F32),
            right[k].astype(F32),
        ],
        axis=0,
    )


def put3(dst, rows, value):
    n = value.shape[0] // W
    for q, shift in ((0, 1), (1, 0), (2, value.shape[0] - 1)):
        moved = value if shift == 0 else pltpu.roll(value, shift, 0)
        dst[rows, :, q * CH : (q + 1) * CH] = moved.astype(BF16).reshape(n, W, CH)


def zero_rows(dst, low, high):
    a, _ = coords()
    n = dst.shape[0]
    for end, rows in ((0, slice(0, low)), (NA - 1, slice(n - high, n))):

        def clear(rows=rows):
            dst[rows] = jnp.zeros((rows.stop - rows.start,) + dst.shape[1:], dst.dtype)

        pl.when(a == end)(clear)


def gelu_parts(x):
    x2 = x * x
    t = jnp.tanh(x * (GC + (GC * GA) * x2))
    half = 0.5 * t + 0.5
    value = x * half
    slope = half + value * (1.0 - half) * (2.0 * GC + (6.0 * GC * GA) * x2)
    return value, slope


def conv_fwd(src, weight, layer, start, n):
    acc = None
    for p in range(3):
        window = src[pl.ds(start + p, n)].reshape(n * W, 3 * CH)
        part = jnp.dot(window, weight[layer, p], preferred_element_type=F32)
        acc = part if acc is None else acc + part
    return acc


def conv_bwd(src, weight, layer, start, n):
    acc = None
    for p in range(3):
        for q in range(3):
            lanes = slice((2 - q) * CH, (3 - q) * CH)
            window = src[pl.ds(start + 2 - p, n), :, lanes].reshape(n * W, CH)
            part = lax.dot_general(
                window,
                weight[layer, p, q * CH : (q + 1) * CH],
                (((1,), (1,)), ((), ())),
                preferred_element_type=F32,
            )
            acc = part if acc is None else acc + part
    return acc


def store_units(dst, first, value):
    n = value.shape[0] // 8
    for h in range(2):
        dst[first : first + n, h] = value[:, h * 128 : (h + 1) * 128].astype(BF16).reshape(n, 8, 128)


def kernel_grad(src, first, grad, dst, unit, taps_of):
    for p in taps_of:
        window = src[first + p : first + p + TR, SIDE : SIDE + TC, :].reshape(CELLS, 3 * CH)
        taps = lax.dot_general(
            window, grad, (((0,), (0,)), ((), ())), preferred_element_type=F32
        )
        store_units(dst, unit + p * 96, taps)


ORDERS = (("x", "y", "z"), ("y", "z", "x"), ("z", "x", "y"))
WAVES = ((384, 1), (0, 2))
EMBED0, EMBED_UNITS = 576, 16


def place():
    a, b = coords()
    return {"z": a // 2, "x": lax.rem(a, 2) * 2 + b // 8, "y": lax.rem(b // 2, 4), "c": lax.rem(b, 2)}


def device_at(pos):
    x = pos["x"]
    return (pos["z"] * 2 + x // 2, lax.rem(x, 2) * 8 + pos["y"] * 2 + pos["c"])


def along(pos, axis, step):
    moved = dict(pos)
    moved[axis] = lax.rem(pos[axis] + step, 4)
    return moved


def other_core(pos):
    moved = dict(pos)
    moved["c"] = 1 - pos["c"]
    return moved


def remote(src, dst, send, recv, pos):
    pltpu.make_async_remote_copy(
        src_ref=src, dst_ref=dst, send_sem=send, recv_sem=recv,
        device_id=device_at(pos), device_id_type=MESH,
    ).start()


def wait_bytes(ref, sem):
    pltpu.make_async_copy(ref, ref, sem).wait()


def add_parts(own, got, count):
    total = own.astype(F32)
    for i in range(count):
        total = total + got[i].astype(F32)
    return total.astype(BF16)


PLANE_STEPS = (
    (2, 2), (2, 1), (2, 3), (1, 2), (3, 2), (1, 1), (1, 3), (3, 1), (3, 3), (2, 0), (0, 2), (1, 0), (3, 0), (0, 1), (0, 3),
)


def on_plane(pos, axes, fn):
    for k, (da, db) in enumerate(PLANE_STEPS):
        fn(along(along(pos, axes[0], da), axes[1], db), k)


class Wave:
    def __init__(self, w, pos, grads, total, bufs, sem, pool):
        self.first, self.per = WAVES[w]
        self.pos, self.grads, self.total, self.pool = pos, grads, total, pool
        self.pair, self.own, self.r1, self.t1, self.r2, self.t2 = bufs
        self.stream = 64 * self.per
        self.send, self.pair_got, self.back_got = sem.at[0], sem.at[1], sem.at[2]
        self.got1 = [sem.at[3 + s] for s in range(3)]
        self.got2 = [sem.at[6 + s] for s in range(3)]
        self.got3 = [sem.at[9 + s] for s in range(3)]
        self.got4 = {step: sem.at[11 + step] for step in (1, 2, 3)}

    def wait(self, units, sem):
        wait_bytes(self.pool.at[pl.ds(0, units * self.per)], sem)

    def pair_start(self):
        mine = self.grads.at[pl.ds(self.first, 3 * self.stream), 1 - self.pos["c"]]
        remote(mine, self.pair, self.send, self.pair_got, other_core(self.pos))

    def rs1_start(self):
        pos, part = self.pos, 16 * self.per
        wait_bytes(self.pair, self.pair_got)
        kept = self.grads[pl.ds(self.first, 3 * self.stream), pos["c"]]
        self.own[...] = (kept.astype(F32) + self.pair[...].astype(F32)).astype(BF16)
        for step in (2, 1, 3):
            for s, order in enumerate(ORDERS):
                peer = along(pos, order[0], step)
                src = self.own.at[pl.ds(s * self.stream + peer[order[0]] * part, part)]
                remote(src, self.r1.at[s, step - 1], self.send, self.got1[s], peer)

    def rs2_start(self):
        pos, part, per = self.pos, 16 * self.per, self.per
        for s, order in enumerate(ORDERS):
            wait_bytes(self.r1.at[s], self.got1[s])
            kept = self.own[pl.ds(s * self.stream + pos[order[0]] * part, part)]
            self.t1[s] = add_parts(kept, self.r1.at[s], 3)

            def go(peer, k, s=s, order=order):
                src = self.t1.at[s, pl.ds((peer[order[1]] * 4 + peer[order[2]]) * per, per)]
                remote(src, self.r2.at[s, k], self.send, self.got2[s], peer)

            on_plane(pos, order[1:], go)

    def block(self, s, order):
        pos, per = self.pos, self.per
        start = self.first + s * self.stream + pos[order[0]] * 16 * per
        return start, (pos[order[1]] * 4 + pos[order[2]]) * per

    def ag2_start(self):
        pos, per, c = self.pos, self.per, self.pos["c"]
        for s, order in enumerate(ORDERS):
            wait_bytes(self.r2.at[s], self.got2[s])
            start, inner = self.block(s, order)
            self.t2[s] = add_parts(self.t1[s, pl.ds(inner, per)], self.r2.at[s], 15)
            block = self.total.at[pl.ds(start + inner, per), c]
            pltpu.make_async_copy(self.t2.at[s], block, self.got3[s]).start()

            def go(peer, k, s=s, block=block):
                remote(self.t2.at[s], block, self.send, self.got3[s], peer)

            on_plane(pos, order[1:], go)

    def ag1_start(self):
        pos, per, c = self.pos, self.per, self.pos["c"]
        for s, order in enumerate(ORDERS):
            self.wait(16, self.got3[s])
            start, _ = self.block(s, order)
            block = self.total.at[pl.ds(start, 16 * per), c]
            for step in (2, 1, 3):
                remote(block, block, self.send, self.got4[step], along(pos, order[0], step))
            remote(block, block, self.send, self.back_got, other_core(pos))

    def pair2_start(self):
        pos, part, c = self.pos, 16 * self.per, self.pos["c"]
        for step in (1, 3, 2):
            self.wait(48, self.got4[step])
            for s, order in enumerate(ORDERS):
                came = lax.rem(pos[order[0]] + 4 - step, 4)
                block = self.total.at[pl.ds(self.first + s * self.stream + came * part, part), c]
                remote(block, block, self.send, self.back_got, other_core(pos))

    def finish(self):
        self.wait(192 + 3 * (48 + 15 + 15 + 48 + 16 + 48), self.send)
        self.wait(192, self.back_got)


class EmbedSum:
    def __init__(self, pos, grads, total, bufs, sem, pool):
        self.pos, self.grads, self.total, self.pool = pos, grads, total, pool
        self.pair, self.own, self.r1, self.t1, self.r2, self.t2 = bufs
        self.send, self.got = sem.at[0], [sem.at[1 + i] for i in range(5)]

    def pair_start(self):
        src = self.grads.at[pl.ds(EMBED0, EMBED_UNITS), 1 - self.pos["c"]]
        remote(src, self.pair, self.send, self.got[0], other_core(self.pos))

    def rs_start(self):
        pos = self.pos
        wait_bytes(self.pair, self.got[0])
        kept = self.grads[pl.ds(EMBED0, EMBED_UNITS), pos["c"]]
        self.own[...] = (kept.astype(F32) + self.pair[...].astype(F32)).astype(BF16)

        def go(peer, k):
            src = self.own.at[pl.ds(peer["y"] * 4 + peer["z"], 1)]
            remote(src, self.r1.at[k], self.send, self.got[1], peer)

        on_plane(pos, ("y", "z"), go)

    def sum_start(self):
        pos = self.pos
        wait_bytes(self.r1, self.got[1])
        self.t1[...] = add_parts(self.own[pl.ds(pos["y"] * 4 + pos["z"], 1)], self.r1, 15)
        for step in range(1, 4):
            remote(self.t1, self.r2.at[step - 1], self.send, self.got[2], along(pos, "x", step))

    def ag_start(self):
        pos, c = self.pos, self.pos["c"]
        wait_bytes(self.r2, self.got[2])
        at = EMBED0 + pos["y"] * 4 + pos["z"]
        parts = []
        for i in range(4):
            got = self.t1[...].astype(F32)
            for step in range(1, 4):
                got = jnp.where(lax.rem(pos["x"] - step + 4, 4) == i, self.r2[step - 1].astype(F32), got)
            parts.append(got)
        self.t2[...] = (((parts[0] + parts[1]) + parts[2]) + parts[3]).astype(BF16)
        block = self.total.at[pl.ds(at, 1), c]
        pltpu.make_async_copy(self.t2, block, self.got[3]).start()
        on_plane(pos, ("y", "z"), lambda peer, k: remote(self.t2, block, self.send, self.got[3], peer))

    def pair2_start(self):
        c = self.pos["c"]
        wait_bytes(self.pool.at[pl.ds(0, 16)], self.got[3])
        block = self.total.at[pl.ds(EMBED0, EMBED_UNITS), c]
        remote(block, block, self.send, self.got[4], other_core(self.pos))

    def finish(self):
        wait_bytes(self.pool.at[pl.ds(0, 16 + 15 + 3 + 15 + 16)], self.send)
        wait_bytes(self.pool.at[pl.ds(0, 16)], self.got[4])


def make_table(table, cells, counts):
    slot = lax.broadcasted_iota(jnp.int32, (CAP, NT), 0)
    cell = cells[...]
    row = (cell * 1366) >> 16
    table[0] = jnp.where(slot < counts[...], row, -100).astype(F32).astype(BF16)
    table[1] = (cell - row * TC).astype(F32).astype(BF16)


def to_group(fn, count):
    def step(k, carry):
        fn(k)
        return carry

    lax.fori_loop(1, count, step, 0)


def codes_start(table, tables, sem):
    a, b = coords()
    pltpu.make_async_copy(table, tables.at[b], sem.at[1]).start()

    def go(k):
        pltpu.make_async_remote_copy(
            src_ref=table, dst_ref=tables.at[b], send_sem=sem.at[0], recv_sem=sem.at[1],
            device_id=(a, lax.rem(b + k, NB)), device_id_type=MESH,
        ).start()

    to_group(go, NB)


def codes_forward(tables, mine, got, sem):
    a, b = coords()
    wait_bytes(tables, sem.at[1])
    lat = lax.broadcasted_iota(jnp.int32, (NA, NT), 0)
    tile = lax.broadcasted_iota(jnp.int32, (NA, NT), 1)
    pick = jnp.where(tile == lat * NB + b, 1.0, 0.0).astype(BF16)
    nt = (((1,), (1,)), ((), ()))
    rows = lax.dot_general(pick, tables[:, 0].reshape(NB * CAP, NT), nt, preferred_element_type=F32)
    cols = lax.dot_general(pick, tables[:, 1].reshape(NB * CAP, NT), nt, preferred_element_type=F32)
    codes = rows * TC + cols
    for i in range(NA):
        mine[i] = codes[i : i + 1]
    pltpu.make_async_copy(mine.at[a], got.at[a], sem.at[3]).start()

    def go(k):
        to = lax.rem(a + k, NA)
        pltpu.make_async_remote_copy(
            src_ref=mine.at[to], dst_ref=got.at[a], send_sem=sem.at[2], recv_sem=sem.at[3],
            device_id=(to, b), device_id_type=MESH,
        ).start()

    to_group(go, NA)


def place_codes(got, onehot, sem):
    wait_bytes(got, sem.at[3])
    rows = [got[i] for i in range(NA)] + [jnp.zeros((NT - NA, NT), F32)]
    codes = jnp.concatenate(rows, axis=0).T
    lane = lax.broadcasted_iota(jnp.int32, (NB * CAP, CELLS), 1).astype(F32)
    for i in range(NA):
        hit = codes[:, i : i + 1] == lane
        onehot[i * NB * CAP : (i + 1) * NB * CAP, :] = jnp.where(hit, 1.0, 0.0).astype(BF16)


def eye(dtype=None):
    return lax.broadcasted_iota(jnp.int32, (128, 128), 0) == lax.broadcasted_iota(jnp.int32, (128, 128), 1)


def pack_numbers(numbers, packed):
    mask = eye()
    for i in range(CELLS // 128):
        packed[i : i + 1] = jnp.where(mask, numbers[i * 128 : (i + 1) * 128], 0.0).sum(axis=0, keepdims=True)


def unpack_numbers(packed, first, count, out):
    mask = eye()
    ones = jnp.ones((256, 128), BF16)
    for i in range(count):
        row = packed[first + i : first + i + 1]
        high = jnp.floor(row * 0.125) * 8.0
        parts = [jnp.where(mask, jnp.broadcast_to(v, (128, 128)), 0.0).astype(BF16) for v in (high, row - high)]
        out[i * 128 : (i + 1) * 128] = jnp.dot(
            jnp.concatenate(parts, axis=1), ones, preferred_element_type=F32
        )


PACKED = {-1: (4, 2), 0: (0, 6), 1: (0, 2)}


def numbers_row(own, bufs, r):
    if r < HR:
        left, mid, right, at = bufs[4], bufs[0], bufs[5], (TR - HR + r) * TC - 512
    elif r < HR + TR:
        left, mid, right, at = bufs[2], own, bufs[3], (r - HR) * TC
    else:
        left, mid, right, at = bufs[6], bufs[1], bufs[7], (r - HR - TR) * TC
    return jnp.concatenate(
        [left[at + TC - SIDE : at + TC], mid[at : at + TC], right[at : at + SIDE]], axis=0
    )


def packed_start(packed, bufs, send, recv, dirs):
    for da, db in dirs:
        pltpu.make_async_remote_copy(
            src_ref=packed, dst_ref=bufs.at[DIRS.index((-da, -db))], send_sem=send, recv_sem=recv,
            device_id=neighbour(da, db), device_id_type=MESH,
        ).start()


def kernel(
    values_hbm, cells_hbm, counts_hbm, embed_hbm, density_hbm, weight_hbm, cot_hbm,
    out_ref, total, back,
    values, cells, counts, embed, density, weight, cot,
    table, tables, codes_mine, codes_got, recv, onehot, means, numbers, packed, packs, mean_strips, cot_strips,
    nN, nS, nW, nE, nNW, nNE, nSW, nSE,
    fN, fS, fW, fE, fNW, fNE, fSW, fSE,
    cN, cS, cW, cE, cNW, cNE, cSW, cSE,
    x0, x1, g1, g0, slope0, cot_ext, up1, grid_out, top, grads, picked,
    *rest,
):
    w1_bufs, w2_bufs, e_bufs = rest[0:6], rest[6:12], rest[12:18]
    (pool, load_sem, a2a_send, a2a_recv, back_send, back_recv, code_sem, halo_sem, pack_sem, cot_sem,
     w1_sem, w2_sem, e_sem) = rest[18:]
    a, _ = coords()
    pos = place()
    fbufs = (fN, fS, fW, fE, fNW, fNE, fSW, fSE)
    nbufs = (nN, nS, nW, nE, nNW, nNE, nSW, nSE)
    cbufs = (cN, cS, cW, cE, cNW, cNE, cSW, cSE)
    w1 = Wave(0, pos, grads, total, w1_bufs, w1_sem, pool)
    w2 = Wave(1, pos, grads, total, w2_bufs, w2_sem, pool)
    es = EmbedSum(pos, grads, total, e_bufs, e_sem, pool)
    barrier_signal()
    loads = [
        pltpu.make_async_copy(src, dst, load_sem.at[i])
        for i, (src, dst) in enumerate(
            (
                (cells_hbm, cells), (counts_hbm, counts), (values_hbm, values), (cot_hbm, cot),
                (embed_hbm, embed), (density_hbm, density), (weight_hbm, weight),
            )
        )
    ]
    for load in loads:
        load.start()
    packed[...] = jnp.zeros_like(packed)
    for load in loads[:4]:
        load.wait()
    make_pairs(cot, cot_strips)
    make_table(table, cells, counts)
    barrier_wait()
    codes_start(table, tables, code_sem)
    exchange_own(values, recv, a2a_recv)
    exchange_start(values, recv, a2a_send, a2a_recv, FAR_Z)
    codes_forward(tables, codes_mine, codes_got, code_sem)
    for load in loads[4:]:
        load.wait()
    place_codes(codes_got, onehot, code_sem)
    wait_bytes(recv, a2a_recv)
    both = jnp.concatenate([recv[...].reshape(SLOTS, F), jnp.ones((SLOTS, F), BF16)], axis=1)
    sums = lax.dot_general(
        onehot[...], both, (((0,), (0,)), ((), ())), preferred_element_type=F32
    )
    numbers[...] = sums[:, F:]
    means[...] = (sums[:, :F] / jnp.maximum(sums[:, F:], 1.0)).astype(BF16).reshape(TR, TC, F)
    pack_numbers(numbers, packed)
    make_strips(means, mean_strips)
    for i, dirs in enumerate((SIDES, ENDS)):
        packed_start(packed, packs, pack_sem.at[0], pack_sem.at[1 + i], dirs)
        halo_start(means, mean_strips, fbufs, HR, halo_sem.at[0], halo_sem.at[1 + i], dirs)

    def unpack(dirs):
        for da, db in dirs:
            first, count = PACKED[da]
            i = DIRS.index((da, db))
            unpack_numbers(packs.at[i], first, count, nbufs[i])

    def field_row(r):
        mean_row = ext_row(means, fbufs, HR, r).astype(BF16)
        logs = jnp.log(1.0 + numbers_row(numbers, nbufs, r))
        embedded = jnp.dot(mean_row, embed[...], preferred_element_type=F32) + jnp.concatenate(
            [logs, logs], axis=1
        ) * density[...]
        put3(x0, slice(r, r + 1), embedded)

    def fwd0(i, n):
        value, slope = gelu_parts(conv_fwd(x0, weight, 0, i, n))
        old = x0[i + 1 : i + 1 + n, :, CH : 2 * CH].reshape(n * W, CH).astype(F32)
        put3(x1, slice(i, i + n), old + value)
        slope0[i : i + n] = slope.reshape(n, W, CH)

    wait_bytes(packs.at[pl.ds(0, 2)], pack_sem.at[1])
    wait_bytes(pool.at[pl.ds(0, SIDE_UNITS)], halo_sem.at[1])
    corners_start(fbufs, packs, (halo_sem.at[0], halo_sem.at[2]), (pack_sem.at[0], pack_sem.at[2]))
    unpack(SIDES)
    for r in range(HR, HR + TR):
        field_row(r)
    pairs_start(cot, cot_strips, cbufs, cot_sem.at[0], cot_sem.at[1])
    fwd0(4, 7)
    fwd0(11, 7)
    wait_bytes(packs.at[pl.ds(0, 6)], pack_sem.at[2])
    wait_bytes(pool.at[pl.ds(0, REST_UNITS)], halo_sem.at[2])
    halo_zero([packs.at[i] for i in range(8)])
    halo_zero(fbufs)
    unpack(REST)
    for r in tuple(range(HR)) + tuple(range(HR + TR, TR + 2 * HR)):
        field_row(r)
    fwd0(0, 4)
    fwd0(18, 4)
    zero_rows(x1, 3, 3)
    wait_bytes(pool.at[pl.ds(0, PAIR_UNITS)], cot_sem.at[1])
    halo_zero(cbufs)
    for r in range(TR + 2 * HC):
        cot_ext[r] = pairs_row(cot, cbufs, r)
    m = 10

    def fwd1(c, carry):
        pre = conv_fwd(x1, weight, 1, c * m, m)
        value, slope = gelu_parts(pre)
        old = x1[pl.ds(c * m + 1, m), :, CH : 2 * CH].reshape(m * W, CH).astype(F32)
        final = (old + value).reshape(m, W, CH)
        grid_out[8 * c : 8 * c + 8] = final[2 - 2 * c : 10 - 2 * c, SIDE : SIDE + TC].astype(BF16)
        grad = cot_ext[pl.ds(c * m, m)].reshape(m * W, CH) * slope
        put3(g1, pl.ds(c * m, m), grad)
        return carry

    for c in range(2):
        fwd1(c, 0)
    field_copy = pltpu.make_async_copy(grid_out, out_ref, load_sem.at[7])
    field_copy.start()

    grad1 = g1[2 : 2 + TR, SIDE : SIDE + TC, CH : 2 * CH].reshape(CELLS, CH)
    kernel_grad(x1, 2, grad1, grads, 288, (1, 2))
    w1.pair_start()
    k = 9

    def bwd1(c, carry):
        up = conv_bwd(g1, weight, 1, c * k, k) + cot_ext[pl.ds(c * k + 1, k)].reshape(k * W, CH)
        up1[pl.ds(c * k, k)] = up.reshape(k, W, CH)
        grad = up * slope0[pl.ds(c * k + 2, k)].reshape(k * W, CH)
        put3(g0, pl.ds(c * k, k), grad)
        return carry

    lax.fori_loop(0, 2, bwd1, 0, unroll=True)
    zero_rows(g0, 1, 1)
    w1.rs1_start()
    kernel_grad(x1, 2, grad1, grads, 288, (0,))
    kernel_grad(x0, 3, g0[1 : 1 + TR, SIDE : SIDE + TC, CH : 2 * CH].reshape(CELLS, CH), grads, 0, (0, 1, 2))
    w2.pair_start()
    j = 8

    def bwd0(c, carry):
        up = conv_bwd(g0, weight, 0, c * j, j) + up1[pl.ds(c * j + 1, j)].reshape(j * W, CH)
        top[pl.ds(c * j, j)] = up.reshape(j, W, CH)[:, SIDE : SIDE + TC].astype(BF16)
        return carry

    lax.fori_loop(0, 2, bwd0, 0, unroll=True)
    w2.rs1_start()
    top_grad = top[...].reshape(CELLS, CH)
    mean_rows = means[...].reshape(CELLS, F)
    store_units(
        grads,
        EMBED0,
        lax.dot_general(mean_rows, top_grad, (((0,), (0,)), ((), ())), preferred_element_type=F32),
    )
    es.pair_start()
    mean_grad = lax.dot_general(
        top_grad, embed[...], (((1,), (1,)), ((), ())), preferred_element_type=F32
    )
    scaled = (mean_grad / jnp.maximum(numbers[...], 1.0)).astype(BF16)
    picked[...] = jnp.dot(onehot[...], scaled, preferred_element_type=F32).astype(BF16).reshape(NT, CAP, F)
    w1.rs2_start()
    es.rs_start()
    w2.rs2_start()
    exchange_own(picked, back, back_recv)
    exchange_start(picked, back, back_send, back_recv, FAR_Z)
    w1.ag2_start()
    es.sum_start()
    w2.ag2_start()
    w1.ag1_start()
    es.ag_start()
    w2.ag1_start()
    w1.pair2_start()
    es.pair2_start()
    w2.pair2_start()
    field_copy.wait()
    wait_bytes(packs, pack_sem.at[0])
    wait_bytes(pool.at[pl.ds(0, SIDE_UNITS + REST_UNITS)], halo_sem.at[0])
    wait_bytes(pool.at[pl.ds(0, PAIR_UNITS)], cot_sem.at[0])
    wait_bytes(back, back_recv)
    exchange_wait_send(values, a2a_send)
    exchange_wait_send(picked, back_send)
    wait_bytes(tables.at[pl.ds(0, NB - 1)], code_sem.at[0])
    wait_bytes(codes_got.at[pl.ds(0, NA - 1)], code_sem.at[2])
    w1.finish()
    w2.finish()
    es.finish()


def write_kernel(total, field, back, conv_out, embed_out, field_out, back_out, wide, sem):
    copies = [
        pltpu.make_async_copy(field, field_out, sem.at[0]),
        pltpu.make_async_copy(back, back_out, sem.at[1]),
    ]
    for copy in copies:
        copy.start()
    bounds = [64 * i for i in range(10)] + [UNITS]
    for i, (u0, u1) in enumerate(zip(bounds, bounds[1:])):
        rows = pl.ds(u0 * 8, (u1 - u0) * 8)
        for h in range(2):
            part = total[u0:u1, h].astype(F32).reshape((u1 - u0) * 8, 128)
            wide[rows, h * 128 : (h + 1) * 128] = part
        dst = embed_out if u0 == EMBED0 else conv_out.at[rows]
        copy = pltpu.make_async_copy(wide.at[rows], dst, sem.at[2 + i])
        copy.start()
        copies.append(copy)
    for copy in copies:
        copy.wait()


VM = pl.BlockSpec(memory_space=pltpu.VMEM)
ANY = pl.BlockSpec(memory_space=pl.ANY)
DMA = pltpu.SemaphoreType.DMA


def vmem(shape, dtype=BF16):
    return pltpu.VMEM(shape, dtype)


def halo_shapes(rows, width):
    wide, side, corner = (rows, TC, width), (TR, SIDE, width), (rows, SIDE, width)
    return [vmem(s) for s in (wide, wide, side, side, corner, corner, corner, corner)]


def pair_shapes():
    wide, side, corner = (HC, TC, CH), (TR // 4, 8, CH), (1, 8, CH)
    return [vmem(s) for s in (wide, wide, side, side, corner, corner, corner, corner)]


def wave_shapes(w):
    per = WAVES[w][1]
    units = 192 * per
    return [
        vmem((units, 8, 128)), vmem((units, 8, 128)), vmem((3, 3, 16 * per, 8, 128)),
        vmem((3, 16 * per, 8, 128)), vmem((3, 15, per, 8, 128)), vmem((3, per, 8, 128)),
    ]


def body(obs_values, obs_cells, obs_counts, embed_weight, density_row, conv_weight, grid_cotangent):
    weight = conv_weight.reshape(2, 3, 3 * CH, CH)
    args = (obs_values[0], obs_cells[0].T, obs_counts, embed_weight, density_row.reshape(1, CH), weight, grid_cotangent)
    field, total, back = pl.pallas_call(
        kernel,
        out_shape=[
            jax.ShapeDtypeStruct((TR, TC, CH), BF16),
            jax.ShapeDtypeStruct((UNITS, 2, 8, 128), BF16),
            jax.ShapeDtypeStruct((NT, CAP, F), BF16),
        ],
        in_specs=[ANY] * 7,
        out_specs=[ANY] * 3,
        scratch_shapes=[
            vmem((NT, CAP, F)), vmem((CAP, NT), jnp.int32), vmem((1, NT), jnp.int32), vmem((F, CH)),
            vmem((1, CH), F32), vmem((2, 3, 3 * CH, CH)), vmem((TR, TC, CH)),
            vmem((2, CAP, NT)), vmem((NB, 2, CAP, NT)), vmem((NA, 1, NT), F32), vmem((NA, 1, NT), F32),
            vmem((NT, CAP, F)), vmem((SLOTS, CELLS)), vmem((TR, TC, F)), vmem((CELLS, F), F32),
            vmem((8, 128), F32), vmem((8, 8, 128), F32), vmem((2, TR, SIDE, F)), vmem((2, TR // 4, 8, CH)),
            *[vmem((PACKED[da][1] * 128, 128), F32) for da, _ in DIRS],
            *halo_shapes(HR, F), *pair_shapes(),
            vmem((24, W, 3 * CH)), vmem((22, W, 3 * CH)), vmem((20, W, 3 * CH)), vmem((18, W, 3 * CH)),
            vmem((22, W, CH), F32), vmem((20, W, CH), F32), vmem((18, W, CH), F32),
            vmem((TR, TC, CH)), vmem((TR, TC, CH)), vmem((UNITS, 2, 8, 128)), vmem((NT, CAP, F)),
            *wave_shapes(0), *wave_shapes(1),
            vmem((16, 8, 128)), vmem((16, 8, 128)), vmem((15, 1, 8, 128)), vmem((1, 8, 128)), vmem((3, 1, 8, 128)),
            vmem((1, 8, 128)),
            vmem((POOL, 8, 128)), DMA((8,)), DMA, DMA, DMA, DMA, DMA((4,)), DMA((3,)), DMA((3,)), DMA((2,)),
            DMA((15,)), DMA((15,)), DMA((6,)),
        ],
        compiler_params=pltpu.CompilerParams(
            collective_id=0, has_side_effects=True, vmem_limit_bytes=40 * 2**20
        ),
    )(*[pltpu.with_memory_space_constraint(arg, pltpu.HBM) for arg in args])
    grad_conv, grad_embed, field, back = pl.pallas_call(
        write_kernel,
        out_shape=[
            jax.ShapeDtypeStruct((EMBED0 * 8, CH), F32),
            jax.ShapeDtypeStruct((F, CH), F32),
            jax.ShapeDtypeStruct(field.shape, BF16),
            jax.ShapeDtypeStruct(back.shape, BF16),
        ],
        in_specs=[VM] * 3,
        out_specs=[ANY] * 4,
        scratch_shapes=[vmem((UNITS * 8, CH), F32), DMA((12,))],
        compiler_params=pltpu.CompilerParams(vmem_limit_bytes=20 * 2**20),
    )(total, field, back)
    return field, grad_conv.reshape(2, 3, 3, CH, CH), grad_embed, back[None]


def solution(mesh):
    return jax.shard_map(
        body,
        mesh=mesh,
        in_specs=(
            P(("lat", "lon"), None, None, None),
            P(("lat", "lon"), None, None),
            P(("lat", "lon"), None),
            P(),
            P(),
            P(),
            P("lat", "lon", None),
        ),
        out_specs=(P("lat", "lon", None), P(), P(), P(("lat", "lon"), None, None, None)),
        check_vma=False,
    )
```

```python
import functools

import jax
import jax.numpy as jnp
from jax import lax
from jax.experimental import pallas as pl
from jax.experimental.pallas import tpu as pltpu
from jax.sharding import PartitionSpec as P

MESH = pl.DeviceIdType.MESH
NA, NB = 8, 16
NT = NA * NB
TR, TC = 16, 48
CELLS = TR * TC
CH, F, CAP = 256, 128, 8
SLOTS = NT * CAP
HR = 4
HC = 2
SIDE = 8
W = TC + 2 * SIDE
POOL = 1536
UNITS = 592
F32, BF16 = jnp.float32, jnp.bfloat16
GC, GA = 0.7978845608028654, 0.044715


def coords():
    return lax.axis_index("lat"), lax.axis_index("lon")


def tile_dev(t):
    return (t // NB, lax.rem(t, NB))


FAR_Z = (2, 1, 3, 0)


def all_others(fn, planes=FAR_Z):
    a, b = coords()
    z, hi = a // 2, lax.rem(a, 2)
    for dz in planes:
        for dh in (1, 0):
            lat = lax.rem(z + dz, 4) * 2 + lax.rem(hi + dh, 2)

            def step(k, carry, lat=lat):
                fn(lat, lax.rem(b + k, NB))
                return carry

            lax.fori_loop(0 if dz or dh else 1, NB, step, 0)


def barrier_signal():
    sem = pltpu.get_barrier_semaphore()
    all_others(lambda lat, lon: pl.semaphore_signal(sem, inc=1, device_id=(lat, lon), device_id_type=MESH))


def barrier_wait():
    pl.semaphore_wait(pltpu.get_barrier_semaphore(), NT - 1)


def exchange_own(src, dst, recv):
    a, b = coords()
    me = a * NB + b
    pltpu.make_async_copy(src.at[me], dst.at[me], recv).start()


def exchange_start(src, dst, send, recv, planes):
    a, b = coords()
    me = a * NB + b

    def go(lat, lon):
        pltpu.make_async_remote_copy(
            src_ref=src.at[lat * NB + lon],
            dst_ref=dst.at[me],
            send_sem=send,
            recv_sem=recv,
            device_id=(lat, lon),
            device_id_type=MESH,
        ).start()

    all_others(go, planes)


def exchange_wait_send(src, send):
    part = src.at[pl.ds(0, NT - 1)]
    pltpu.make_async_copy(part, part, send).wait()


DIRS = [(-1, 0), (1, 0), (0, -1), (0, 1), (-1, -1), (-1, 1), (1, -1), (1, 1)]


def make_strips(src, strips):
    strips[0] = src[:, 0:SIDE, :]
    strips[1] = src[:, TC - SIDE : TC, :]


def make_pairs(src, pairs):
    for side, at in ((0, 0), (1, TC - 8)):
        cut = slice(0, HC) if side == 0 else slice(8 - HC, 8)
        for i in range(TR // 4):
            parts = [src[4 * i + j, at : at + 8].astype(F32)[cut] for j in range(4)]
            pairs[side, i] = jnp.concatenate(parts, axis=0).astype(BF16)


def pairs_start(src, pairs, bufs, send, recv):
    for da, db in DIRS:
        back = DIRS.index((-da, -db))
        if db == 0:
            part = src.at[pl.ds(0, HC) if da < 0 else pl.ds(TR - HC, HC)]
        else:
            blocks = {-1: pl.ds(0, 1), 0: pl.ds(0, TR // 4), 1: pl.ds(TR // 4 - 1, 1)}[da]
            part = pairs.at[(db + 1) // 2, blocks]
        pltpu.make_async_remote_copy(
            src_ref=part, dst_ref=bufs[back], send_sem=send, recv_sem=recv,
            device_id=neighbour(da, db), device_id_type=MESH,
        ).start()


PAIR_UNITS = (2 * HC * TC + 2 * TR * 2 + 4 * 8) * CH // 1024


def pairs_row(core, bufs, r):
    if r < HC:
        left, mid, right = bufs[4][0], bufs[0][r], bufs[5][0]
        at = 8 - 2 * HC + HC * r
    elif r < HC + TR:
        k = r - HC
        left, mid, right = bufs[2][k // 4], core[k], bufs[3][k // 4]
        at = HC * (k % 4)
    else:
        k = r - HC - TR
        left, mid, right = bufs[6][0], bufs[1][k], bufs[7][0]
        at = HC * k
    zero = jnp.zeros((SIDE - HC, CH), F32)
    return jnp.concatenate(
        [zero, left.astype(F32)[at : at + HC], mid.astype(F32), right.astype(F32)[at : at + HC], zero], axis=0
    )


def neighbour(da, db):
    a, b = coords()
    return (lax.rem(a + da + NA, NA), lax.rem(b + db + NB, NB))


SIDES, ENDS, REST = DIRS[2:4], DIRS[0:2], DIRS[0:2] + DIRS[4:]


def halo_start(src, strips, bufs, rows, send, recv, dirs):
    for da, db in dirs:
        back = DIRS.index((-da, -db))
        row = {-1: pl.ds(0, rows), 0: pl.ds(0, TR), 1: pl.ds(TR - rows, rows)}[da]
        whole = src if db == 0 else strips.at[(db + 1) // 2]
        pltpu.make_async_remote_copy(
            src_ref=whole.at[row], dst_ref=bufs[back], send_sem=send, recv_sem=recv,
            device_id=neighbour(da, db), device_id_type=MESH,
        ).start()


def corners_start(bufs, packs, sems, pack_sems):
    for da, row in ((-1, 0), (1, TR - HR)):
        peer = neighbour(da, 0)
        for db, side in ((-1, 2), (1, 3)):
            corner = DIRS.index((-da, db))
            for src, dst, (send, recv) in (
                (bufs[side].at[pl.ds(row, HR)], bufs[corner], sems),
                (packs.at[side], packs.at[corner], pack_sems),
            ):
                pltpu.make_async_remote_copy(
                    src_ref=src, dst_ref=dst, send_sem=send, recv_sem=recv,
                    device_id=peer, device_id_type=MESH,
                ).start()


SIDE_UNITS = 2 * TR * SIDE * F // 1024
REST_UNITS = (2 * HR * TC + 4 * HR * SIDE) * F // 1024


def halo_zero(bufs):
    a, _ = coords()
    for end, at in ((0, -1), (NA - 1, 1)):

        def clear(at=at):
            for i, (da, _) in enumerate(DIRS):
                if da == at:
                    bufs[i][...] = jnp.zeros(bufs[i].shape, bufs[i].dtype)

        pl.when(a == end)(clear)


def ext_row(core, bufs, rows, r):
    if r < rows:
        left, mid, right, k = bufs[4], bufs[0], bufs[5], r
    elif r < rows + TR:
        left, mid, right, k = bufs[2], core, bufs[3], r - rows
    else:
        left, mid, right, k = bufs[6], bufs[1], bufs[7], r - rows - TR
    return jnp.concatenate(
        [
            left[k].astype(F32),
            mid[k].astype(F32),
            right[k].astype(F32),
        ],
        axis=0,
    )


def put3(dst, rows, value):
    n = value.shape[0] // W
    for q, shift in ((0, 1), (1, 0), (2, value.shape[0] - 1)):
        moved = value if shift == 0 else pltpu.roll(value, shift, 0)
        dst[rows, :, q * CH : (q + 1) * CH] = moved.astype(BF16).reshape(n, W, CH)


def zero_rows(dst, low, high):
    a, _ = coords()
    n = dst.shape[0]
    for end, rows in ((0, slice(0, low)), (NA - 1, slice(n - high, n))):

        def clear(rows=rows):
            dst[rows] = jnp.zeros((rows.stop - rows.start,) + dst.shape[1:], dst.dtype)

        pl.when(a == end)(clear)


def gelu_parts(x):
    x2 = x * x
    t = jnp.tanh(x * (GC + (GC * GA) * x2))
    half = 0.5 * t + 0.5
    value = x * half
    slope = half + value * (1.0 - half) * (2.0 * GC + (6.0 * GC * GA) * x2)
    return value, slope


def conv_fwd(src, weight, layer, start, n):
    acc = None
    for p in range(3):
        window = src[pl.ds(start + p, n)].reshape(n * W, 3 * CH)
        part = jnp.dot(window, weight[layer, p], preferred_element_type=F32)
        acc = part if acc is None else acc + part
    return acc


def conv_bwd(src, weight, layer, start, n):
    acc = None
    for p in range(3):
        for q in range(3):
            lanes = slice((2 - q) * CH, (3 - q) * CH)
            window = src[pl.ds(start + 2 - p, n), :, lanes].reshape(n * W, CH)
            part = lax.dot_general(
                window,
                weight[layer, p, q * CH : (q + 1) * CH],
                (((1,), (1,)), ((), ())),
                preferred_element_type=F32,
            )
            acc = part if acc is None else acc + part
    return acc


def store_units(dst, first, value):
    n = value.shape[0] // 8
    for h in range(2):
        dst[first : first + n, h] = value[:, h * 128 : (h + 1) * 128].astype(BF16).reshape(n, 8, 128)


def kernel_grad(src, first, grad, dst, unit, taps_of):
    for p in taps_of:
        window = src[first + p : first + p + TR, SIDE : SIDE + TC, :].reshape(CELLS, 3 * CH)
        taps = lax.dot_general(
            window, grad, (((0,), (0,)), ((), ())), preferred_element_type=F32
        )
        store_units(dst, unit + p * 96, taps)


ORDERS = (("x", "y", "z"), ("y", "z", "x"), ("z", "x", "y"))
WAVES = ((384, 1), (0, 2))
EMBED0, EMBED_UNITS = 576, 16


def place():
    a, b = coords()
    return {"z": a // 2, "x": lax.rem(a, 2) * 2 + b // 8, "y": lax.rem(b // 2, 4), "c": lax.rem(b, 2)}


def device_at(pos):
    x = pos["x"]
    return (pos["z"] * 2 + x // 2, lax.rem(x, 2) * 8 + pos["y"] * 2 + pos["c"])


def along(pos, axis, step):
    moved = dict(pos)
    moved[axis] = lax.rem(pos[axis] + step, 4)
    return moved


def other_core(pos):
    moved = dict(pos)
    moved["c"] = 1 - pos["c"]
    return moved


def remote(src, dst, send, recv, pos):
    pltpu.make_async_remote_copy(
        src_ref=src, dst_ref=dst, send_sem=send, recv_sem=recv,
        device_id=device_at(pos), device_id_type=MESH,
    ).start()


def wait_bytes(ref, sem):
    pltpu.make_async_copy(ref, ref, sem).wait()


def add_parts(own, got, count):
    total = own.astype(F32)
    for i in range(count):
        total = total + got[i].astype(F32)
    return total.astype(BF16)


PLANE_STEPS = (
    (2, 2), (2, 1), (2, 3), (1, 2), (3, 2), (1, 1), (1, 3), (3, 1), (3, 3), (2, 0), (0, 2), (1, 0), (3, 0), (0, 1), (0, 3),
)


def on_plane(pos, axes, fn):
    for k, (da, db) in enumerate(PLANE_STEPS):
        fn(along(along(pos, axes[0], da), axes[1], db), k)


class Wave:
    def __init__(self, w, pos, grads, total, bufs, sem, pool):
        self.first, self.per = WAVES[w]
        self.pos, self.grads, self.total, self.pool = pos, grads, total, pool
        self.pair, self.own, self.r1, self.t1, self.r2, self.t2 = bufs
        self.stream = 64 * self.per
        self.send, self.pair_got, self.back_got = sem.at[0], sem.at[1], sem.at[2]
        self.got1 = [sem.at[3 + s] for s in range(3)]
        self.got2 = [sem.at[6 + s] for s in range(3)]
        self.got3 = [sem.at[9 + s] for s in range(3)]
        self.got4 = {step: sem.at[11 + step] for step in (1, 2, 3)}

    def wait(self, units, sem):
        wait_bytes(self.pool.at[pl.ds(0, units * self.per)], sem)

    def pair_start(self):
        mine = self.grads.at[pl.ds(self.first, 3 * self.stream), 1 - self.pos["c"]]
        remote(mine, self.pair, self.send, self.pair_got, other_core(self.pos))

    def rs1_start(self):
        pos, part = self.pos, 16 * self.per
        wait_bytes(self.pair, self.pair_got)
        kept = self.grads[pl.ds(self.first, 3 * self.stream), pos["c"]]
        self.own[...] = (kept.astype(F32) + self.pair[...].astype(F32)).astype(BF16)
        for step in (2, 1, 3):
            for s, order in enumerate(ORDERS):
                peer = along(pos, order[0], step)
                src = self.own.at[pl.ds(s * self.stream + peer[order[0]] * part, part)]
                remote(src, self.r1.at[s, step - 1], self.send, self.got1[s], peer)

    def rs2_start(self):
        pos, part, per = self.pos, 16 * self.per, self.per
        for s, order in enumerate(ORDERS):
            wait_bytes(self.r1.at[s], self.got1[s])
            kept = self.own[pl.ds(s * self.stream + pos[order[0]] * part, part)]
            self.t1[s] = add_parts(kept, self.r1.at[s], 3)

            def go(peer, k, s=s, order=order):
                src = self.t1.at[s, pl.ds((peer[order[1]] * 4 + peer[order[2]]) * per, per)]
                remote(src, self.r2.at[s, k], self.send, self.got2[s], peer)

            on_plane(pos, order[1:], go)

    def block(self, s, order):
        pos, per = self.pos, self.per
        start = self.first + s * self.stream + pos[order[0]] * 16 * per
        return start, (pos[order[1]] * 4 + pos[order[2]]) * per

    def ag2_start(self):
        pos, per, c = self.pos, self.per, self.pos["c"]
        for s, order in enumerate(ORDERS):
            wait_bytes(self.r2.at[s], self.got2[s])
            start, inner = self.block(s, order)
            self.t2[s] = add_parts(self.t1[s, pl.ds(inner, per)], self.r2.at[s], 15)
            block = self.total.at[pl.ds(start + inner, per), c]
            pltpu.make_async_copy(self.t2.at[s], block, self.got3[s]).start()

            def go(peer, k, s=s, block=block):
                remote(self.t2.at[s], block, self.send, self.got3[s], peer)

            on_plane(pos, order[1:], go)

    def ag1_start(self):
        pos, per, c = self.pos, self.per, self.pos["c"]
        for s, order in enumerate(ORDERS):
            self.wait(16, self.got3[s])
            start, _ = self.block(s, order)
            block = self.total.at[pl.ds(start, 16 * per), c]
            for step in (2, 1, 3):
                remote(block, block, self.send, self.got4[step], along(pos, order[0], step))
            remote(block, block, self.send, self.back_got, other_core(pos))

    def pair2_start(self):
        pos, part, c = self.pos, 16 * self.per, self.pos["c"]
        for step in (1, 3, 2):
            self.wait(48, self.got4[step])
            for s, order in enumerate(ORDERS):
                came = lax.rem(pos[order[0]] + 4 - step, 4)
                block = self.total.at[pl.ds(self.first + s * self.stream + came * part, part), c]
                remote(block, block, self.send, self.back_got, other_core(pos))

    def finish(self):
        self.wait(192 + 3 * (48 + 15 + 15 + 48 + 16 + 48), self.send)
        self.wait(192, self.back_got)


class EmbedSum:
    def __init__(self, pos, grads, total, bufs, sem, pool):
        self.pos, self.grads, self.total, self.pool = pos, grads, total, pool
        self.pair, self.own, self.r1, self.t1, self.r2, self.t2 = bufs
        self.send, self.got = sem.at[0], [sem.at[1 + i] for i in range(5)]

    def pair_start(self):
        src = self.grads.at[pl.ds(EMBED0, EMBED_UNITS), 1 - self.pos["c"]]
        remote(src, self.pair, self.send, self.got[0], other_core(self.pos))

    def rs_start(self):
        pos = self.pos
        wait_bytes(self.pair, self.got[0])
        kept = self.grads[pl.ds(EMBED0, EMBED_UNITS), pos["c"]]
        self.own[...] = (kept.astype(F32) + self.pair[...].astype(F32)).astype(BF16)

        def go(peer, k):
            src = self.own.at[pl.ds(peer["y"] * 4 + peer["z"], 1)]
            remote(src, self.r1.at[k], self.send, self.got[1], peer)

        on_plane(pos, ("y", "z"), go)

    def sum_start(self):
        pos = self.pos
        wait_bytes(self.r1, self.got[1])
        self.t1[...] = add_parts(self.own[pl.ds(pos["y"] * 4 + pos["z"], 1)], self.r1, 15)
        for step in range(1, 4):
            remote(self.t1, self.r2.at[step - 1], self.send, self.got[2], along(pos, "x", step))

    def ag_start(self):
        pos, c = self.pos, self.pos["c"]
        wait_bytes(self.r2, self.got[2])
        at = EMBED0 + pos["y"] * 4 + pos["z"]
        parts = []
        for i in range(4):
            got = self.t1[...].astype(F32)
            for step in range(1, 4):
                got = jnp.where(lax.rem(pos["x"] - step + 4, 4) == i, self.r2[step - 1].astype(F32), got)
            parts.append(got)
        self.t2[...] = (((parts[0] + parts[1]) + parts[2]) + parts[3]).astype(BF16)
        block = self.total.at[pl.ds(at, 1), c]
        pltpu.make_async_copy(self.t2, block, self.got[3]).start()
        on_plane(pos, ("y", "z"), lambda peer, k: remote(self.t2, block, self.send, self.got[3], peer))

    def pair2_start(self):
        c = self.pos["c"]
        wait_bytes(self.pool.at[pl.ds(0, 16)], self.got[3])
        block = self.total.at[pl.ds(EMBED0, EMBED_UNITS), c]
        remote(block, block, self.send, self.got[4], other_core(self.pos))

    def finish(self):
        wait_bytes(self.pool.at[pl.ds(0, 16 + 15 + 3 + 15 + 16)], self.send)
        wait_bytes(self.pool.at[pl.ds(0, 16)], self.got[4])


def make_table(table, cells, counts):
    slot = lax.broadcasted_iota(jnp.int32, (CAP, NT), 0)
    cell = cells[...]
    row = (cell * 1366) >> 16
    table[0] = jnp.where(slot < counts[...], row, -100).astype(F32).astype(BF16)
    table[1] = (cell - row * TC).astype(F32).astype(BF16)


def to_group(fn, count):
    def step(k, carry):
        fn(k)
        return carry

    lax.fori_loop(1, count, step, 0)


def codes_start(table, tables, sem):
    a, b = coords()
    pltpu.make_async_copy(table, tables.at[b], sem.at[1]).start()

    def go(k):
        pltpu.make_async_remote_copy(
            src_ref=table, dst_ref=tables.at[b], send_sem=sem.at[0], recv_sem=sem.at[1],
            device_id=(a, lax.rem(b + k, NB)), device_id_type=MESH,
        ).start()

    to_group(go, NB)


def codes_forward(tables, mine, got, sem):
    a, b = coords()
    wait_bytes(tables, sem.at[1])
    lat = lax.broadcasted_iota(jnp.int32, (NA, NT), 0)
    tile = lax.broadcasted_iota(jnp.int32, (NA, NT), 1)
    pick = jnp.where(tile == lat * NB + b, 1.0, 0.0).astype(BF16)
    nt = (((1,), (1,)), ((), ()))
    rows = lax.dot_general(pick, tables[:, 0].reshape(NB * CAP, NT), nt, preferred_element_type=F32)
    cols = lax.dot_general(pick, tables[:, 1].reshape(NB * CAP, NT), nt, preferred_element_type=F32)
    codes = rows * TC + cols
    for i in range(NA):
        mine[i] = codes[i : i + 1]
    pltpu.make_async_copy(mine.at[a], got.at[a], sem.at[3]).start()

    def go(k):
        to = lax.rem(a + k, NA)
        pltpu.make_async_remote_copy(
            src_ref=mine.at[to], dst_ref=got.at[a], send_sem=sem.at[2], recv_sem=sem.at[3],
            device_id=(to, b), device_id_type=MESH,
        ).start()

    to_group(go, NA)


def place_codes(got, onehot, sem):
    wait_bytes(got, sem.at[3])
    rows = [got[i] for i in range(NA)] + [jnp.zeros((NT - NA, NT), F32)]
    codes = jnp.concatenate(rows, axis=0).T
    lane = lax.broadcasted_iota(jnp.int32, (NB * CAP, CELLS), 1).astype(F32)
    for i in range(NA):
        hit = codes[:, i : i + 1] == lane
        onehot[i * NB * CAP : (i + 1) * NB * CAP, :] = jnp.where(hit, 1.0, 0.0).astype(BF16)


def eye(dtype=None):
    return lax.broadcasted_iota(jnp.int32, (128, 128), 0) == lax.broadcasted_iota(jnp.int32, (128, 128), 1)


def pack_numbers(numbers, packed):
    mask = eye()
    for i in range(CELLS // 128):
        packed[i : i + 1] = jnp.where(mask, numbers[i * 128 : (i + 1) * 128], 0.0).sum(axis=0, keepdims=True)


def unpack_numbers(packed, first, count, out):
    mask = eye()
    ones = jnp.ones((256, 128), BF16)
    for i in range(count):
        row = packed[first + i : first + i + 1]
        high = jnp.floor(row * 0.125) * 8.0
        parts = [jnp.where(mask, jnp.broadcast_to(v, (128, 128)), 0.0).astype(BF16) for v in (high, row - high)]
        out[i * 128 : (i + 1) * 128] = jnp.dot(
            jnp.concatenate(parts, axis=1), ones, preferred_element_type=F32
        )


PACKED = {-1: (4, 2), 0: (0, 6), 1: (0, 2)}


def numbers_row(own, bufs, r):
    if r < HR:
        left, mid, right, at = bufs[4], bufs[0], bufs[5], (TR - HR + r) * TC - 512
    elif r < HR + TR:
        left, mid, right, at = bufs[2], own, bufs[3], (r - HR) * TC
    else:
        left, mid, right, at = bufs[6], bufs[1], bufs[7], (r - HR - TR) * TC
    return jnp.concatenate(
        [left[at + TC - SIDE : at + TC], mid[at : at + TC], right[at : at + SIDE]], axis=0
    )


def packed_start(packed, bufs, send, recv, dirs):
    for da, db in dirs:
        pltpu.make_async_remote_copy(
            src_ref=packed, dst_ref=bufs.at[DIRS.index((-da, -db))], send_sem=send, recv_sem=recv,
            device_id=neighbour(da, db), device_id_type=MESH,
        ).start()


def kernel(
    values_hbm, cells_hbm, counts_hbm, embed_hbm, density_hbm, weight_hbm, cot_hbm,
    out_ref, total, back,
    values, cells, counts, embed, density, weight, cot,
    table, tables, codes_mine, codes_got, recv, onehot, means, numbers, packed, packs, mean_strips, cot_strips,
    nN, nS, nW, nE, nNW, nNE, nSW, nSE,
    fN, fS, fW, fE, fNW, fNE, fSW, fSE,
    cN, cS, cW, cE, cNW, cNE, cSW, cSE,
    x0, x1, g1, g0, slope0, cot_ext, up1, grid_out, top, grads, picked,
    *rest,
):
    w1_bufs, w2_bufs, e_bufs = rest[0:6], rest[6:12], rest[12:18]
    (pool, load_sem, a2a_send, a2a_recv, back_send, back_recv, code_sem, halo_sem, pack_sem, cot_sem,
     w1_sem, w2_sem, e_sem) = rest[18:]
    a, _ = coords()
    pos = place()
    fbufs = (fN, fS, fW, fE, fNW, fNE, fSW, fSE)
    nbufs = (nN, nS, nW, nE, nNW, nNE, nSW, nSE)
    cbufs = (cN, cS, cW, cE, cNW, cNE, cSW, cSE)
    w1 = Wave(0, pos, grads, total, w1_bufs, w1_sem, pool)
    w2 = Wave(1, pos, grads, total, w2_bufs, w2_sem, pool)
    es = EmbedSum(pos, grads, total, e_bufs, e_sem, pool)
    barrier_signal()
    loads = [
        pltpu.make_async_copy(src, dst, load_sem.at[i])
        for i, (src, dst) in enumerate(
            (
                (cells_hbm, cells), (counts_hbm, counts), (values_hbm, values), (cot_hbm, cot),
                (embed_hbm, embed), (density_hbm, density), (weight_hbm, weight),
            )
        )
    ]
    for load in loads:
        load.start()
    packed[...] = jnp.zeros_like(packed)
    for load in loads[:4]:
        load.wait()
    make_pairs(cot, cot_strips)
    make_table(table, cells, counts)
    barrier_wait()
    codes_start(table, tables, code_sem)
    exchange_own(values, recv, a2a_recv)
    exchange_start(values, recv, a2a_send, a2a_recv, FAR_Z)
    codes_forward(tables, codes_mine, codes_got, code_sem)
    for load in loads[4:]:
        load.wait()
    place_codes(codes_got, onehot, code_sem)
    wait_bytes(recv, a2a_recv)
    both = jnp.concatenate([recv[...].reshape(SLOTS, F), jnp.ones((SLOTS, F), BF16)], axis=1)
    sums = lax.dot_general(
        onehot[...], both, (((0,), (0,)), ((), ())), preferred_element_type=F32
    )
    numbers[...] = sums[:, F:]
    means[...] = (sums[:, :F] / jnp.maximum(sums[:, F:], 1.0)).astype(BF16).reshape(TR, TC, F)
    pack_numbers(numbers, packed)
    make_strips(means, mean_strips)
    for i, dirs in enumerate((SIDES, ENDS)):
        packed_start(packed, packs, pack_sem.at[0], pack_sem.at[1 + i], dirs)
        halo_start(means, mean_strips, fbufs, HR, halo_sem.at[0], halo_sem.at[1 + i], dirs)

    def unpack(dirs):
        for da, db in dirs:
            first, count = PACKED[da]
            i = DIRS.index((da, db))
            unpack_numbers(packs.at[i], first, count, nbufs[i])

    def field_row(r):
        mean_row = ext_row(means, fbufs, HR, r).astype(BF16)
        logs = jnp.log(1.0 + numbers_row(numbers, nbufs, r))
        embedded = jnp.dot(mean_row, embed[...], preferred_element_type=F32) + jnp.concatenate(
            [logs, logs], axis=1
        ) * density[...]
        put3(x0, slice(r, r + 1), embedded)

    def fwd0(i, n):
        value, slope = gelu_parts(conv_fwd(x0, weight, 0, i, n))
        old = x0[i + 1 : i + 1 + n, :, CH : 2 * CH].reshape(n * W, CH).astype(F32)
        put3(x1, slice(i, i + n), old + value)
        slope0[i : i + n] = slope.reshape(n, W, CH)

    wait_bytes(packs.at[pl.ds(0, 2)], pack_sem.at[1])
    wait_bytes(pool.at[pl.ds(0, SIDE_UNITS)], halo_sem.at[1])
    corners_start(fbufs, packs, (halo_sem.at[0], halo_sem.at[2]), (pack_sem.at[0], pack_sem.at[2]))
    pairs_start(cot, cot_strips, cbufs, cot_sem.at[0], cot_sem.at[1])
    unpack(SIDES)
    for r in range(HR, HR + TR):
        field_row(r)
    fwd0(4, 7)
    fwd0(11, 7)
    wait_bytes(packs.at[pl.ds(0, 6)], pack_sem.at[2])
    wait_bytes(pool.at[pl.ds(0, REST_UNITS)], halo_sem.at[2])
    halo_zero([packs.at[i] for i in range(8)])
    halo_zero(fbufs)
    unpack(REST)
    for r in tuple(range(HR)) + tuple(range(HR + TR, TR + 2 * HR)):
        field_row(r)
    fwd0(0, 4)
    fwd0(18, 4)
    zero_rows(x1, 3, 3)
    wait_bytes(pool.at[pl.ds(0, PAIR_UNITS)], cot_sem.at[1])
    halo_zero(cbufs)
    for r in range(TR + 2 * HC):
        cot_ext[r] = pairs_row(cot, cbufs, r)
    m = 10

    def fwd1(c, carry):
        pre = conv_fwd(x1, weight, 1, c * m, m)
        value, slope = gelu_parts(pre)
        old = x1[pl.ds(c * m + 1, m), :, CH : 2 * CH].reshape(m * W, CH).astype(F32)
        final = (old + value).reshape(m, W, CH)
        grid_out[8 * c : 8 * c + 8] = final[2 - 2 * c : 10 - 2 * c, SIDE : SIDE + TC].astype(BF16)
        grad = cot_ext[pl.ds(c * m, m)].reshape(m * W, CH) * slope
        put3(g1, pl.ds(c * m, m), grad)
        return carry

    for c in range(2):
        fwd1(c, 0)
    field_copy = pltpu.make_async_copy(grid_out, out_ref, load_sem.at[7])
    field_copy.start()

    grad1 = g1[2 : 2 + TR, SIDE : SIDE + TC, CH : 2 * CH].reshape(CELLS, CH)
    kernel_grad(x1, 2, grad1, grads, 288, (1, 2))
    w1.pair_start()
    k = 9

    def bwd1(c, carry):
        up = conv_bwd(g1, weight, 1, c * k, k) + cot_ext[pl.ds(c * k + 1, k)].reshape(k * W, CH)
        up1[pl.ds(c * k, k)] = up.reshape(k, W, CH)
        grad = up * slope0[pl.ds(c * k + 2, k)].reshape(k * W, CH)
        put3(g0, pl.ds(c * k, k), grad)
        return carry

    lax.fori_loop(0, 2, bwd1, 0, unroll=True)
    zero_rows(g0, 1, 1)
    w1.rs1_start()
    kernel_grad(x1, 2, grad1, grads, 288, (0,))
    kernel_grad(x0, 3, g0[1 : 1 + TR, SIDE : SIDE + TC, CH : 2 * CH].reshape(CELLS, CH), grads, 0, (0, 1, 2))
    w2.pair_start()
    j = 8

    def bwd0(c, carry):
        up = conv_bwd(g0, weight, 0, c * j, j) + up1[pl.ds(c * j + 1, j)].reshape(j * W, CH)
        top[pl.ds(c * j, j)] = up.reshape(j, W, CH)[:, SIDE : SIDE + TC].astype(BF16)
        return carry

    lax.fori_loop(0, 2, bwd0, 0, unroll=True)
    w2.rs1_start()
    top_grad = top[...].reshape(CELLS, CH)
    mean_rows = means[...].reshape(CELLS, F)
    store_units(
        grads,
        EMBED0,
        lax.dot_general(mean_rows, top_grad, (((0,), (0,)), ((), ())), preferred_element_type=F32),
    )
    es.pair_start()
    mean_grad = lax.dot_general(
        top_grad, embed[...], (((1,), (1,)), ((), ())), preferred_element_type=F32
    )
    scaled = (mean_grad / jnp.maximum(numbers[...], 1.0)).astype(BF16)
    picked[...] = jnp.dot(onehot[...], scaled, preferred_element_type=F32).astype(BF16).reshape(NT, CAP, F)
    w1.rs2_start()
    es.rs_start()
    w2.rs2_start()
    exchange_own(picked, back, back_recv)
    exchange_start(picked, back, back_send, back_recv, FAR_Z)
    w1.ag2_start()
    es.sum_start()
    w2.ag2_start()
    w1.ag1_start()
    es.ag_start()
    w2.ag1_start()
    w1.pair2_start()
    es.pair2_start()
    w2.pair2_start()
    field_copy.wait()
    wait_bytes(packs, pack_sem.at[0])
    wait_bytes(pool.at[pl.ds(0, SIDE_UNITS + REST_UNITS)], halo_sem.at[0])
    wait_bytes(pool.at[pl.ds(0, PAIR_UNITS)], cot_sem.at[0])
    wait_bytes(back, back_recv)
    exchange_wait_send(values, a2a_send)
    exchange_wait_send(picked, back_send)
    wait_bytes(tables.at[pl.ds(0, NB - 1)], code_sem.at[0])
    wait_bytes(codes_got.at[pl.ds(0, NA - 1)], code_sem.at[2])
    w1.finish()
    w2.finish()
    es.finish()


def write_kernel(total, field, back, conv_out, embed_out, field_out, back_out, wide, sem):
    copies = [
        pltpu.make_async_copy(field, field_out, sem.at[0]),
        pltpu.make_async_copy(back, back_out, sem.at[1]),
    ]
    for copy in copies:
        copy.start()
    bounds = [64 * i for i in range(10)] + [UNITS]
    for i, (u0, u1) in enumerate(zip(bounds, bounds[1:])):
        rows = pl.ds(u0 * 8, (u1 - u0) * 8)
        for h in range(2):
            part = total[u0:u1, h].astype(F32).reshape((u1 - u0) * 8, 128)
            wide[rows, h * 128 : (h + 1) * 128] = part
        dst = embed_out if u0 == EMBED0 else conv_out.at[rows]
        copy = pltpu.make_async_copy(wide.at[rows], dst, sem.at[2 + i])
        copy.start()
        copies.append(copy)
    for copy in copies:
        copy.wait()


VM = pl.BlockSpec(memory_space=pltpu.VMEM)
ANY = pl.BlockSpec(memory_space=pl.ANY)
DMA = pltpu.SemaphoreType.DMA


def vmem(shape, dtype=BF16):
    return pltpu.VMEM(shape, dtype)


def halo_shapes(rows, width):
    wide, side, corner = (rows, TC, width), (TR, SIDE, width), (rows, SIDE, width)
    return [vmem(s) for s in (wide, wide, side, side, corner, corner, corner, corner)]


def pair_shapes():
    wide, side, corner = (HC, TC, CH), (TR // 4, 8, CH), (1, 8, CH)
    return [vmem(s) for s in (wide, wide, side, side, corner, corner, corner, corner)]


def wave_shapes(w):
    per = WAVES[w][1]
    units = 192 * per
    return [
        vmem((units, 8, 128)), vmem((units, 8, 128)), vmem((3, 3, 16 * per, 8, 128)),
        vmem((3, 16 * per, 8, 128)), vmem((3, 15, per, 8, 128)), vmem((3, per, 8, 128)),
    ]


def body(obs_values, obs_cells, obs_counts, embed_weight, density_row, conv_weight, grid_cotangent):
    weight = conv_weight.reshape(2, 3, 3 * CH, CH)
    args = (obs_values[0], obs_cells[0].T, obs_counts, embed_weight, density_row.reshape(1, CH), weight, grid_cotangent)
    field, total, back = pl.pallas_call(
        kernel,
        out_shape=[
            jax.ShapeDtypeStruct((TR, TC, CH), BF16),
            jax.ShapeDtypeStruct((UNITS, 2, 8, 128), BF16),
            jax.ShapeDtypeStruct((NT, CAP, F), BF16),
        ],
        in_specs=[ANY] * 7,
        out_specs=[ANY] * 3,
        scratch_shapes=[
            vmem((NT, CAP, F)), vmem((CAP, NT), jnp.int32), vmem((1, NT), jnp.int32), vmem((F, CH)),
            vmem((1, CH), F32), vmem((2, 3, 3 * CH, CH)), vmem((TR, TC, CH)),
            vmem((2, CAP, NT)), vmem((NB, 2, CAP, NT)), vmem((NA, 1, NT), F32), vmem((NA, 1, NT), F32),
            vmem((NT, CAP, F)), vmem((SLOTS, CELLS)), vmem((TR, TC, F)), vmem((CELLS, F), F32),
            vmem((8, 128), F32), vmem((8, 8, 128), F32), vmem((2, TR, SIDE, F)), vmem((2, TR // 4, 8, CH)),
            *[vmem((PACKED[da][1] * 128, 128), F32) for da, _ in DIRS],
            *halo_shapes(HR, F), *pair_shapes(),
            vmem((24, W, 3 * CH)), vmem((22, W, 3 * CH)), vmem((20, W, 3 * CH)), vmem((18, W, 3 * CH)),
            vmem((22, W, CH), F32), vmem((20, W, CH), F32), vmem((18, W, CH), F32),
            vmem((TR, TC, CH)), vmem((TR, TC, CH)), vmem((UNITS, 2, 8, 128)), vmem((NT, CAP, F)),
            *wave_shapes(0), *wave_shapes(1),
            vmem((16, 8, 128)), vmem((16, 8, 128)), vmem((15, 1, 8, 128)), vmem((1, 8, 128)), vmem((3, 1, 8, 128)),
            vmem((1, 8, 128)),
            vmem((POOL, 8, 128)), DMA((8,)), DMA, DMA, DMA, DMA, DMA((4,)), DMA((3,)), DMA((3,)), DMA((2,)),
            DMA((15,)), DMA((15,)), DMA((6,)),
        ],
        compiler_params=pltpu.CompilerParams(
            collective_id=0, has_side_effects=True, vmem_limit_bytes=40 * 2**20
        ),
    )(*[pltpu.with_memory_space_constraint(arg, pltpu.HBM) for arg in args])
    grad_conv, grad_embed, field, back = pl.pallas_call(
        write_kernel,
        out_shape=[
            jax.ShapeDtypeStruct((EMBED0 * 8, CH), F32),
            jax.ShapeDtypeStruct((F, CH), F32),
            jax.ShapeDtypeStruct(field.shape, BF16),
            jax.ShapeDtypeStruct(back.shape, BF16),
        ],
        in_specs=[VM] * 3,
        out_specs=[ANY] * 4,
        scratch_shapes=[vmem((UNITS * 8, CH), F32), DMA((12,))],
        compiler_params=pltpu.CompilerParams(vmem_limit_bytes=20 * 2**20),
    )(total, field, back)
    return field, grad_conv.reshape(2, 3, 3, CH, CH), grad_embed, back[None]


def solution(mesh):
    return jax.shard_map(
        body,
        mesh=mesh,
        in_specs=(
            P(("lat", "lon"), None, None, None),
            P(("lat", "lon"), None, None),
            P(("lat", "lon"), None),
            P(),
            P(),
            P(),
            P("lat", "lon", None),
        ),
        out_specs=(P("lat", "lon", None), P(), P(), P(("lat", "lon"), None, None, None)),
        check_vma=False,
    )
```
